32 devices in a mesh: seg: 8 (over y, x, core), head: 4 (over z).
Axes of the slice: x: 2, y: 2, z: 4, core: 2. Of those that a mesh axis runs over, the one named last changes fastest.
Arguments:
- queries: bfloat16 [4096, 4096], P('seg', 'head'), may hold values from -6 to 6
- key_tokens: bfloat16 [4096, 4096], P('seg', 'head'), may hold values from -0.52734375 to 0.52734375
- values: bfloat16 [4096, 4096], P('seg', 'head'), may hold values from -6 to 6
- upstream: bfloat16 [4096, 4096], P('seg', 'head'), may hold values from -6 to 6
- norm_gain: float32 [4096], P('head'), may hold values from 0.1 to 1.9
- decay_rate: float32 [32], P('head'), may hold values from 1.2207031e-05 to 0.00390625
- block_length: int32 [8], replicated, may hold values from 1 to 512, 3072 in all
- parent: int32 [8], replicated, may hold values from -1 to 6, as said below
Outputs:
- attention_out: bfloat16 [4096, 4096], P('seg', 'head')
- query_grad: bfloat16 [4096, 4096], P('seg', 'head')
- key_grad: bfloat16 [4096, 4096], P('seg', 'head')
- value_grad: bfloat16 [4096, 4096], P('seg', 'head')
The draws below stay inside these ranges and needn't reach their ends.
Inputs may be any that keep to these rules, and one draw needn't show every extreme that they name: parent[0] is -1; every other block's parent is -1 or an earlier block, and block 7 always continues block 6.
All inputs are finite; a program needn't handle non-finite values.
Results may differ from the reference program's by a relative error of at most 0.012.
Values sent between devices are 32-bit elements; how exact they have to be, the bound alone decides.
No kernel may reach another device: no remote copies, remote signals or barrier semaphores. Data moves between devices by JAX's collectives and lax.ppermute only.
A program may use at most 64 MiB of HBM per device.

```python
import math
import jax
import jax.numpy as jnp
import numpy as np
from jax import lax

HEADS = 32
DH = 128
TOK_DEV = 512
BLOCKS = 8
TOKENS = 4096


def draw_parent(key, part):
    indices = jnp.arange(BLOCKS, dtype=jnp.int32)
    kinds = jax.random.randint(jax.random.fold_in(key, 11), (BLOCKS,), 0, 8)
    distant = jax.random.randint(jax.random.fold_in(key, 12), (BLOCKS,), 0, jnp.maximum(indices, 1))
    parent = jnp.where(kinds == 0, -1, jnp.where(kinds < 5, indices - 1, distant))
    parent = jnp.where(indices == 0, -1, parent)
    parent = jnp.where(indices == BLOCKS - 1, BLOCKS - 2, parent)
    return parent.astype(jnp.int32)


def levels(rng, extent, split, smallest, high):
    def one(axis_at, blocks):
        draws = jax.random.uniform(jax.random.fold_in(jax.random.fold_in(rng, 6), axis_at), (blocks,), jnp.float32, smallest / len(split), high / len(split))
        return jnp.repeat(jnp.exp(draws), extent[axis_at] // blocks).reshape((-1,) + (1,) * (len(extent) - axis_at - 1))

    gain = one(*split[0])
    for cut in split[1:]:
        gain = gain * one(*cut)
    return gain


def split_up(number_of, total, bound, lean):
    weights = [(1 << 20) // math.isqrt(rank ** lean) + 1 for rank in range(2, number_of + 1)]
    spare, holding = total - bound - (number_of - 1), [1] * (number_of - 1)
    while spare > 0:
        movable = [i for i in range(number_of - 1) if holding[i] < bound]
        whole, left = sum([weights[i] for i in movable]), spare
        for i in movable:
            addition = min(bound - holding[i], max(1, left * weights[i] // whole), spare)
            holding[i] = holding[i] + addition
            spare = spare - addition
    return np.array([bound] + holding)


def ragged(rng, number_of, total, reach, slope):
    if number_of == 2:
        one = jax.random.randint(rng, (), max(1, total - reach), min(reach, total - 1) + 1)
        return jnp.stack([one, total - one])
    tallies = jnp.asarray(split_up(number_of, total, reach, slope), jnp.int32)
    couples = (number_of - 1) // 2
    giver, sink = tallies[1:1 + 2 * couples:2], tallies[2:2 + 2 * couples:2]
    margin = jnp.minimum(giver - 1, reach - sink)
    moved = jax.random.randint(jax.random.fold_in(rng, 1), (couples,), 0, 1 << 20) % (margin + 1)
    tallies = tallies.at[1:1 + 2 * couples:2].set(giver - moved).at[2:2 + 2 * couples:2].set(sink + moved)
    return tallies[jax.random.permutation(jax.random.fold_in(rng, 2), number_of)]


def scatter_about(rng, dims, spread, reach, cuts=(), kind=jnp.bfloat16):
    values = jax.random.normal(rng, dims, jnp.float32) * spread
    if len(cuts) > 0:
        values = levels(rng, dims, cuts, -0.22, 0.18) * values
    return jnp.clip(values, min=-reach, max=reach).astype(kind)


def setup_inputs(seed: int = 0) -> dict:
    key_list = jax.random.split(jax.random.key(seed), 9)
    return {
        "queries": scatter_about(key_list[0], (TOKENS, HEADS * DH), 1.0, 6.0, ((0, 8), (1, 4))),
        "key_tokens": scatter_about(key_list[1], (TOKENS, HEADS * DH), (DH ** -0.5), 0.52734375, ((0, 8), (1, 4))),
        "values": scatter_about(key_list[2], (TOKENS, HEADS * DH), 1.0, 6.0, ((0, 8), (1, 4))),
        "upstream": scatter_about(key_list[3], (TOKENS, HEADS * DH), 1.0, 6.0, ((0, 8), (1, 4))),
        "norm_gain": jnp.clip(1.0 + 0.18 * jax.random.normal(key_list[4], (HEADS * DH,), jnp.float32), 0.1, 1.9),
        "decay_rate": jnp.clip(jnp.exp(math.log(0.00390625) - 5.768321 * jax.random.uniform(key_list[5], (HEADS,), jnp.float32) ** levels(key_list[5], (HEADS,), ((0, 4),), -0.2, 0.2)), 1.220703143189894e-05, 0.00390625),
        "block_length": ragged(key_list[6], BLOCKS, BLOCKS * TOK_DEV * 3 // 4, TOK_DEV, 1).astype(jnp.int32),
        "parent": draw_parent(jax.random.fold_in(key_list[8], 71), 0),
    }


norm_eps = 1e-05
highest = lax.Precision.HIGHEST

def ancestry(block_length, parent, decay_rate):
    count = parent.shape[0]
    columns = jnp.arange(count, dtype=jnp.int32)
    linked = (parent[:, None] == columns[None, :]).astype(jnp.float32)
    for step in range(max(1, (count - 1).bit_length())):
        linked = jnp.minimum(linked + jnp.dot(linked, linked, precision=highest), 1.0)
    lengths = block_length.astype(jnp.float32)
    depth = jnp.dot(linked, lengths, precision=highest)
    distance = jnp.maximum(depth[:, None] - depth[None, :] - lengths[None, :], 0.0)
    decayed = jnp.exp(-distance[:, :, None] * decay_rate[None, None, :])
    return jnp.where(linked[:, :, None] > 0.5, decayed, 0.0)

def block_local(query_full, key_full, value_full, length, decay_rate):
    row_count, width_here = query_full.shape
    heads_here = decay_rate.shape[0]
    head_size = width_here // heads_here
    block_rows = min(512, row_count)
    block_count = row_count // block_rows
    shape_blocks = (block_count, block_rows, heads_here, head_size)
    query_blocks = query_full.reshape(shape_blocks)
    key_blocks = key_full.reshape(shape_blocks)
    value_blocks = value_full.reshape(shape_blocks)
    offsets = jnp.arange(block_rows, dtype=jnp.float32)
    spacing = offsets[:, None] - offsets[None, :]
    inner_decay = jnp.where(spacing[None] >= 0, jnp.exp(-decay_rate[:, None, None] * jnp.maximum(spacing, 0.0)[None]), 0.0)
    query_decay = jnp.exp(-(offsets[:, None] + 1.0) * decay_rate[None, :])
    key_decay = jnp.exp(-(block_rows - 1.0 - offsets)[:, None] * decay_rate[None, :])
    block_decay = jnp.exp(-float(block_rows) * decay_rate)

    def advance(carry_state, pieces):
        query_part, key_part, value_part = pieces
        raw_scores = jnp.einsum('uhd,whd->huw', query_part, key_part, preferred_element_type=jnp.float32)
        weighted = (raw_scores * inner_decay).astype(jnp.bfloat16)
        within_block = jnp.einsum('huw,whe->uhe', weighted, value_part, preferred_element_type=jnp.float32)
        from_state = jnp.einsum('uhd,hde->uhe', query_part * query_decay[:, :, None], carry_state, precision=highest)
        carry_state = block_decay[:, None, None] * carry_state + jnp.einsum('whd,whe->hde', key_part * key_decay[:, :, None], value_part.astype(jnp.float32), precision=highest)
        return (carry_state, within_block + from_state)
    initial = jnp.zeros((heads_here, head_size, head_size), jnp.float32)
    unused, block_outputs = lax.scan(advance, initial, (query_blocks, key_blocks, value_blocks))
    local_out = block_outputs.reshape(row_count, width_here)
    positions = jnp.arange(row_count, dtype=jnp.float32)
    remaining = jnp.maximum(length.astype(jnp.float32) - 1.0 - positions, 0.0)
    key_end = jnp.exp(-remaining[:, None] * decay_rate[None, :])
    key_heads = key_full.reshape(row_count, heads_here, head_size)
    value_heads = value_full.reshape(row_count, heads_here, head_size)
    local_state = jnp.einsum('thd,the->hde', key_heads * key_end[:, :, None], value_heads.astype(jnp.float32), precision=highest)
    return (local_out, local_state)

def correction(query_full, carried, decay_rate):
    row_count, width_here = query_full.shape
    heads_here = decay_rate.shape[0]
    head_size = width_here // heads_here
    positions = jnp.arange(row_count, dtype=jnp.float32)
    query_scale = jnp.exp(-(positions[:, None] + 1.0) * decay_rate[None, :])
    query_heads = query_full.reshape(row_count, heads_here, head_size)
    result = jnp.einsum('thd,hde->the', query_heads * query_scale[:, :, None], carried, precision=highest)
    return result.reshape(row_count, width_here)

def reference(queries, key_tokens, values, upstream, norm_gain, decay_rate, block_length, parent):
    width = HEADS * DH
    weights = ancestry(block_length, parent, decay_rate)
    valid_mask = (jnp.arange(TOK_DEV)[None, :] < block_length[:, None])[:, :, None]

    def forward(query_in, key_in, value_in):
        query_full = jnp.where(valid_mask, query_in.reshape(BLOCKS, TOK_DEV, width), 0)
        key_full = jnp.where(valid_mask, key_in.reshape(BLOCKS, TOK_DEV, width), 0)
        value_full = jnp.where(valid_mask, value_in.reshape(BLOCKS, TOK_DEV, width), 0)

        def one_block(items):
            return block_local(items[0], items[1], items[2], items[3], decay_rate)
        local_out, local_state = lax.map(jax.checkpoint(one_block), (query_full, key_full, value_full, block_length))

        def carried_for(weight_row):
            return jnp.einsum('jh,jhde->hde', weight_row, local_state, precision=highest)
        carried = lax.map(carried_for, weights)

        def corrected(items):
            return correction(items[0], items[1], decay_rate)
        attended = (local_out + lax.map(corrected, (query_full, carried))).reshape(TOKENS, width)
        inverse = lax.rsqrt(lax.optimization_barrier(jnp.mean(attended * attended, axis=1)) + norm_eps)
        return (attended * inverse[:, None] * norm_gain[None, :]).astype(jnp.bfloat16)
    attention_out, pull = jax.vjp(forward, queries, key_tokens, values)
    query_grad, key_grad, value_grad = pull(upstream)
    return (attention_out, query_grad.astype(jnp.bfloat16), key_grad.astype(jnp.bfloat16), value_grad.astype(jnp.bfloat16))
```

```python
import functools

import jax
import jax.numpy as jnp
from jax import lax
from jax.experimental import pallas as pl
from jax.experimental.pallas import tpu as pltpu
from jax.sharding import PartitionSpec as P

norm_eps = 1e-05
f32 = jnp.float32
bf16 = jnp.bfloat16
VMEM_LIMIT = 40 * 1024 * 1024

SMEM_SPEC = pl.BlockSpec(memory_space=pltpu.SMEM)
VMEM_SPEC = pl.BlockSpec(memory_space=pltpu.VMEM)


def nn(a, b):
    return lax.dot_general(a, b, (((1,), (0,)), ((), ())), preferred_element_type=f32)


def nt(a, b):
    return lax.dot_general(a, b, (((1,), (1,)), ((), ())), preferred_element_type=f32)


def tn(a, b):
    return lax.dot_general(a, b, (((0,), (0,)), ((), ())), preferred_element_type=f32)


def row_index(rows, columns):
    return lax.broadcasted_iota(jnp.int32, (rows, columns), 0)


def key_scale(rows, size, length, rate):
    slot = row_index(rows, size)
    remaining = jnp.maximum(length - 1 - slot, 0).astype(f32)
    return jnp.where(slot < length, jnp.exp(-rate * remaining), 0.0)


def query_scale(rows, size, rate):
    return jnp.exp(-rate * (row_index(rows, size) + 1).astype(f32))


def masked_rows(array, length):
    return jnp.where(row_index(*array.shape) < length, array, jnp.zeros_like(array))


def column(row):
    count = row.shape[1]
    return jnp.broadcast_to(row, (count, count)).T


def write_pieces(whole, outs, chip):
    piece = outs[0].shape[0]
    for offset, out in enumerate(outs):
        at = pl.multiple_of((chip ^ offset) * piece, piece)
        out[...] = whole[pl.ds(at, piece), :]


def read_pieces(pieces, whole, chip):
    piece = pieces[0].shape[0]
    for offset, part in enumerate(pieces):
        at = pl.multiple_of((chip ^ offset) * piece, piece)
        whole[pl.ds(at, piece), :] = part[...]


def state_kernel(chips, length_ref, rate_ref, key_ref, value_ref, *rest):
    outs, whole = rest[:chips], rest[chips]
    own = lax.axis_index("seg")
    step = pl.program_id(0)
    rows, wide = key_ref.shape
    size = whole.shape[1]
    length = length_ref[own]
    here = wide // size
    scaled = []
    for at in range(here):
        scale = key_scale(rows, size, length, rate_ref[step * here + at])
        part = value_ref[:, at * size:(at + 1) * size].astype(f32) * scale
        scaled.append(part.astype(bf16))
    both = tn(key_ref[...], jnp.concatenate(scaled, axis=1))
    for at in range(here):
        span = slice(at * size, (at + 1) * size)
        begin = pl.multiple_of(step * wide + at * size, size)
        whole[pl.ds(begin, size), :] = both[span, span]

    @pl.when(step == pl.num_programs(0) - 1)
    def finish():
        write_pieces(whole, outs, own // 2)


def decay_tile(tile, rate, distance, transposed):
    u = lax.broadcasted_iota(jnp.int32, (tile, tile), 1 if transposed else 0)
    w = lax.broadcasted_iota(jnp.int32, (tile, tile), 0 if transposed else 1)
    spacing = u - w + distance
    decay = jnp.exp(-rate * jnp.maximum(spacing, 0).astype(f32))
    return jnp.where(spacing >= 0, decay, 0.0) if distance < tile else decay


def local_kernel(size, tile, length_ref, rate_ref, query_ref, key_ref, value_ref, out_ref):
    own = lax.axis_index("seg")
    step = pl.program_id(0)
    rows, wide = query_ref.shape
    here = wide // size
    length = length_ref[own]
    count = rows // tile
    for at in range(here):
        span = slice(at * size, (at + 1) * size)
        rate = rate_ref[step * here + at]
        query = masked_rows(query_ref[:, span], length)
        decays = [decay_tile(tile, rate, tile * gap, False) for gap in range(count)]
        for i in range(count):
            total = None
            for j in range(i + 1):
                w_span = slice(j * tile, (j + 1) * tile)
                scores = nt(query[i * tile:(i + 1) * tile], key_ref[w_span, span])
                weighted = (scores * decays[i - j]).astype(bf16)
                part = nn(weighted, value_ref[w_span, span])
                total = part if total is None else total + part
            out_ref[i * tile:(i + 1) * tile, span] = total


def tree_distances(length_ref, parent_ref, table, count):
    def clear(at, carry):
        table[at] = jnp.int32(-1)
        return carry

    lax.fori_loop(0, count * count, clear, 0)

    def one(block, carry):
        def up(at):
            node, distance = at
            table[block * count + node] = distance
            return parent_ref[node], distance + length_ref[node]

        lax.while_loop(lambda at: at[0] >= 0, up, (parent_ref[block], jnp.int32(0)))
        return carry

    lax.fori_loop(0, count, one, 0)


def mix_kernel(chips, size, backward, length_ref, parent_ref, rate_ref, *rest):
    mine, other, outs, table = rest[:chips], rest[chips:2 * chips], rest[2 * chips:3 * chips], rest[3 * chips]
    own = lax.axis_index("seg")
    chip, core = own // 2, own % 2
    count = 2 * chips
    tree_distances(length_ref, parent_ref, table, count)
    piece = mine[0].shape[0]
    part = min(piece, size)
    for at in range(piece // part):
        head = (chip * piece + at * part) // size
        rate = rate_ref[head]
        span = slice(at * part, (at + 1) * part)
        totals = [jnp.zeros((part, size), f32) for _ in range(chips)]
        for offset in range(chips):
            for sibling, sources in ((0, mine), (1, other)):
                source = (chip ^ offset) * 2 + (core ^ sibling)
                data = sources[offset][span, :]
                for target in range(chips):
                    wanted = (chip ^ target) * 2 + core
                    place = source * count + wanted if backward else wanted * count + source
                    distance = table[place]
                    level = jnp.full((8, size), -rate * distance.astype(f32), f32)
                    weight = jnp.exp(level) * (distance >= 0).astype(f32)
                    weight = jnp.concatenate([weight] * (part // 8), axis=0)
                    totals[target] = totals[target] + weight * data
        for target in range(chips):
            outs[target][span, :] = totals[target]


def attend_kernel(chips, length_ref, rate_ref, query_ref, upstream_ref, local_ref, gain_ref, *rest):
    pieces, attended_ref, sums_ref, whole = rest[:chips], rest[chips], rest[chips + 1], rest[chips + 2]
    own = lax.axis_index("seg")
    rows, wide = query_ref.shape
    size = whole.shape[1]
    length = length_ref[own]
    read_pieces(pieces, whole, own // 2)
    squares = jnp.zeros((rows, size), f32)
    inners = jnp.zeros((rows, size), f32)
    for head in range(wide // size):
        span = slice(head * size, (head + 1) * size)
        query = masked_rows(query_ref[:, span], length)
        carried = whole[span, :].astype(bf16)
        scale = query_scale(rows, size, rate_ref[head])
        attended = local_ref[:, span] + scale * nn(query, carried)
        attended_ref[:, span] = attended
        scaled = upstream_ref[:, span].astype(f32) * gain_ref[:, span]
        squares = squares + attended * attended
        inners = inners + scaled * attended
    groups = rows // size
    for at in range(groups):
        span = slice(at * size, (at + 1) * size)
        sums_ref[at:at + 1, :] = jnp.sum(squares[span].T, axis=0, keepdims=True)
        sums_ref[groups + at:groups + at + 1, :] = jnp.sum(inners[span].T, axis=0, keepdims=True)


def norm_columns(sum_refs, width, inverse_ref, factor_ref):
    total = sum_refs[0][...]
    for ref in sum_refs[1:]:
        total = total + ref[...]
    groups = total.shape[0] // 2
    size = total.shape[1]
    inverse = lax.rsqrt(total[:groups] / width + norm_eps)
    factor = inverse * inverse * inverse * total[groups:] / width
    for at in range(groups):
        span = slice(at * size, (at + 1) * size)
        inverse_ref[span, :] = column(inverse[at:at + 1])
        factor_ref[span, :] = column(factor[at:at + 1])


def state_grad_kernel(chips, sums, width, length_ref, rate_ref, query_ref, upstream_ref, attended_ref, gain_ref, *rest):
    sum_refs, outs = rest[:sums], rest[sums:sums + chips]
    inverse_ref, factor_ref, whole = rest[sums + chips:]
    own = lax.axis_index("seg")
    rows, wide = query_ref.shape
    size = whole.shape[1]
    length = length_ref[own]
    norm_columns(sum_refs, width, inverse_ref, factor_ref)
    inverse = inverse_ref[...]
    factor = factor_ref[...]
    heads = wide // size
    group = min(2, heads)
    for first in range(0, heads, group):
        parts = []
        for head in range(first, first + group):
            span = slice(head * size, (head + 1) * size)
            scaled = upstream_ref[:, span].astype(f32) * gain_ref[:, span]
            grad = inverse * scaled - factor * attended_ref[:, span]
            parts.append((grad * query_scale(rows, size, rate_ref[head])).astype(bf16))
        span = slice(first * size, (first + group) * size)
        query = masked_rows(query_ref[:, span], length)
        both = tn(query, jnp.concatenate(parts, axis=1))
        for at in range(group):
            inner = slice(at * size, (at + 1) * size)
            whole[(first + at) * size:(first + at + 1) * size, :] = both[inner, inner]
    write_pieces(whole, outs, own // 2)


def backward_kernel(chips, sums, width, tile, first, filled, length_ref, rate_ref, query_ref, key_ref, value_ref, upstream_ref, attended_ref, gain_ref, *rest):
    sum_refs, pieces = rest[:sums], rest[sums:sums + chips]
    outs = rest[sums + chips + filled:]
    out_ref, query_grad_ref, key_grad_ref, value_grad_ref, inverse_ref, factor_ref, whole = outs
    own = lax.axis_index("seg")
    step = pl.program_id(0)
    rows, wide = query_ref.shape
    size = whole.shape[1]
    here = wide // size
    length = length_ref[own]
    count = rows // tile

    @pl.when(step == 0)
    def begin():
        norm_columns(sum_refs, width, inverse_ref, factor_ref)
        read_pieces(pieces, whole, own // 2)

    for at in range(here):
        span = slice(at * size, (at + 1) * size)
        head = (first + step) * here + at
        rate = rate_ref[head]
        query = masked_rows(query_ref[:, span], length)
        key = key_ref[:, span]
        value = value_ref[:, span]
        gain = gain_ref[:, span]
        inverse = inverse_ref[...]
        attended = attended_ref[:, span]
        out_ref[:, span] = (attended * inverse * gain).astype(bf16)
        scaled = upstream_ref[:, span].astype(f32) * gain
        grad = (inverse * scaled - factor_ref[...] * attended).astype(bf16)
        carried = whole[pl.ds(pl.multiple_of(head * size, size), size), :].astype(bf16)
        query_grad = nt(grad, carried) * query_scale(rows, size, rate)
        decays = [decay_tile(tile, rate, tile * gap, True) for gap in range(count)]
        local_query = [None] * count
        for j in range(count):
            w_span = slice(j * tile, (j + 1) * tile)
            key_total = value_total = None
            for i in range(j, count):
                u_span = slice(i * tile, (i + 1) * tile)
                decay = decays[i - j]
                weighted = (nt(key[w_span], query[u_span]) * decay).astype(bf16)
                weighted_grad = nt(value[w_span], grad[u_span]).astype(bf16).astype(f32)
                score_grad = (weighted_grad * decay).astype(bf16)
                value_part = nn(weighted, grad[u_span])
                key_part = nn(score_grad, query[u_span])
                query_part = tn(score_grad, key[w_span])
                value_total = value_part if value_total is None else value_total + value_part
                key_total = key_part if key_total is None else key_total + key_part
                local_query[i] = query_part if local_query[i] is None else local_query[i] + query_part
            key_grad_ref[w_span, span] = key_total.astype(bf16)
            value_grad_ref[w_span, span] = value_total.astype(bf16)
        query_grad = query_grad + jnp.concatenate(local_query, axis=0)
        query_grad_ref[:, span] = masked_rows(query_grad, length).astype(bf16)


def finish_kernel(chips, length_ref, rate_ref, key_ref, value_ref, key_local_ref, value_local_ref, *rest):
    pieces, key_grad_ref, value_grad_ref, whole = rest[:chips], rest[chips], rest[chips + 1], rest[chips + 2]
    own = lax.axis_index("seg")
    rows, wide = key_ref.shape
    size = whole.shape[1]
    length = length_ref[own]
    read_pieces(pieces, whole, own // 2)
    for head in range(wide // size):
        span = slice(head * size, (head + 1) * size)
        scale = key_scale(rows, size, length, rate_ref[head])
        state_grad = whole[span, :].astype(bf16)
        key_part = scale * nt(value_ref[:, span], state_grad)
        value_part = scale * nn(key_ref[:, span], state_grad)
        key_grad_ref[:, span] = (key_local_ref[:, span].astype(f32) + key_part).astype(bf16)
        value_grad_ref[:, span] = (value_local_ref[:, span].astype(f32) + value_part).astype(bf16)


def params():
    return pltpu.CompilerParams(vmem_limit_bytes=VMEM_LIMIT)


def shape(dims, dtype):
    return jax.ShapeDtypeStruct(dims, dtype)


def exchange(pieces, count):
    moved = [pieces[0]]
    for offset in range(1, len(pieces)):
        pairs = [(at, at ^ (2 * offset)) for at in range(count)]
        moved.append(lax.ppermute(pieces[offset], "seg", pairs))
    return moved


def swap_cores(pieces, count):
    pairs = [(at, at ^ 1) for at in range(count)]
    return [lax.ppermute(piece, "seg", pairs) for piece in pieces]


def head_sums(sums, count):
    if count <= 4:
        return [sums] + [lax.ppermute(sums, "head", [(at, at ^ step) for at in range(count)]) for step in range(1, count)]
    step = 1
    while step < count:
        sums = sums + lax.ppermute(sums, "head", [(at, at ^ step) for at in range(count)])
        step *= 2
    return [sums]


def local(seg_count, head_count, queries, key_tokens, values, upstream, norm_gain, decay_rate, block_length, parent):
    rows, wide = queries.shape
    heads = decay_rate.shape[0]
    size = wide // heads
    width = wide * head_count
    chips = seg_count // 2
    piece = wide // chips
    group = min(2, heads) * size
    steps = wide // group
    tile = min(256, rows)
    gain = norm_gain[None, :]
    piece_shapes = [shape((piece, size), f32)] * chips
    piece_specs = [VMEM_SPEC] * chips
    whole = pltpu.VMEM((wide, size), f32)

    def column_spec(first=0):
        return pl.BlockSpec((rows, group), lambda step: (0, first + step))

    states = pl.pallas_call(
        functools.partial(state_kernel, chips),
        grid=(steps,),
        out_shape=piece_shapes,
        in_specs=[SMEM_SPEC] * 2 + [column_spec()] * 2,
        out_specs=[pl.BlockSpec((piece, size), lambda step: (0, 0))] * chips,
        scratch_shapes=[whole],
        compiler_params=params(),
        name="block_state",
    )(block_length, decay_rate, key_tokens, values)

    local_out = pl.pallas_call(
        functools.partial(local_kernel, size, tile),
        grid=(steps,),
        out_shape=shape((rows, wide), f32),
        in_specs=[SMEM_SPEC] * 2 + [column_spec()] * 3,
        out_specs=column_spec(),
        compiler_params=params(),
        cost_estimate=pl.CostEstimate(flops=3 * rows * rows * wide, bytes_accessed=10 * rows * wide, transcendentals=rows * rows * heads),
        name="local_attention",
    )(block_length, decay_rate, queries, key_tokens, values)

    def mix(pieces, backward):
        mine = exchange(pieces, seg_count)
        other = swap_cores(mine, seg_count)
        mixed = pl.pallas_call(
            functools.partial(mix_kernel, chips, size, backward),
            out_shape=piece_shapes,
            in_specs=[SMEM_SPEC] * 3 + piece_specs * 2,
            out_specs=piece_specs,
            scratch_shapes=[pltpu.SMEM((seg_count * seg_count,), jnp.int32)],
            compiler_params=params(),
            name="mix_backward" if backward else "mix_forward",
        )(block_length, parent, decay_rate, *mine, *other)
        return exchange(mixed, seg_count)

    carried = mix(states, False)

    attended, sums = pl.pallas_call(
        functools.partial(attend_kernel, chips),
        out_shape=[shape((rows, wide), f32), shape((2 * rows // size, size), f32)],
        in_specs=[SMEM_SPEC] * 2 + [VMEM_SPEC] * (4 + chips),
        out_specs=[VMEM_SPEC] * 2,
        scratch_shapes=[whole],
        compiler_params=params(),
        name="attend",
    )(block_length, decay_rate, queries, upstream, local_out, gain, *carried)

    sum_parts = head_sums(sums, head_count)
    columns = pltpu.VMEM((rows, size), f32)

    state_grads = pl.pallas_call(
        functools.partial(state_grad_kernel, chips, len(sum_parts), width),
        out_shape=piece_shapes,
        in_specs=[SMEM_SPEC] * 2 + [VMEM_SPEC] * (4 + len(sum_parts)),
        out_specs=piece_specs,
        scratch_shapes=[columns, columns, whole],
        compiler_params=params(),
        name="state_grad",
    )(block_length, decay_rate, queries, upstream, attended, gain, *sum_parts)

    def backward(first, amount, filled):
        names = len(sum_parts) + chips
        gain_spec = pl.BlockSpec((1, group), lambda step: (0, first + step))
        at = 2 + 6 + names
        return pl.pallas_call(
            functools.partial(backward_kernel, chips, len(sum_parts), width, tile, first, len(filled)),
            grid=(amount,),
            out_shape=[shape((rows, wide), bf16)] * 4,
            in_specs=[SMEM_SPEC] * 2
            + [column_spec(first)] * 5
            + [gain_spec]
            + [VMEM_SPEC] * names
            + [pl.BlockSpec(memory_space=pl.ANY)] * len(filled),
            out_specs=[column_spec(first)] * 4,
            scratch_shapes=[columns, columns, whole],
            input_output_aliases={at + i: i for i in range(len(filled))},
            compiler_params=params(),
            cost_estimate=pl.CostEstimate(
                flops=8 * rows * rows * group * amount, bytes_accessed=16 * rows * group * amount, transcendentals=rows * rows * amount
            ),
            name="local_backward",
        )(block_length, decay_rate, queries, key_tokens, values, upstream, attended, gain, *sum_parts, *carried, *filled)

    half = steps // 2
    grads = backward(0, steps - half, [])
    if half:
        grads = backward(steps - half, half, grads)
    attention_out, query_grad, key_local, value_local = grads

    state_sums = mix(state_grads, True)

    key_grad, value_grad = pl.pallas_call(
        functools.partial(finish_kernel, chips),
        out_shape=[shape((rows, wide), bf16)] * 2,
        in_specs=[SMEM_SPEC] * 2 + [VMEM_SPEC] * (4 + chips),
        out_specs=[VMEM_SPEC] * 2,
        scratch_shapes=[whole],
        compiler_params=params(),
        name="finish",
    )(block_length, decay_rate, key_tokens, values, key_local, value_local, *state_sums)
    return attention_out, query_grad, key_grad, value_grad


def solution(mesh):
    sizes = dict(mesh.shape)
    tokens = P("seg", "head")
    return jax.shard_map(
        functools.partial(local, sizes["seg"], sizes["head"]),
        mesh=mesh,
        in_specs=(tokens, tokens, tokens, tokens, P("head"), P("head"), P(), P()),
        out_specs=(tokens, tokens, tokens, tokens),
        check_vma=False,
    )
```

```python
import functools

import jax
import jax.numpy as jnp
from jax import lax
from jax.experimental import pallas as pl
from jax.experimental.pallas import tpu as pltpu
from jax.sharding import PartitionSpec as P

norm_eps = 1e-05
f32 = jnp.float32
bf16 = jnp.bfloat16
VMEM_LIMIT = 40 * 1024 * 1024
FIRST_LIMIT = 504 * 1024 * 1024 // 10

SMEM_SPEC = pl.BlockSpec(memory_space=pltpu.SMEM)
VMEM_SPEC = pl.BlockSpec(memory_space=pltpu.VMEM)
ANY_SPEC = pl.BlockSpec(memory_space=pl.ANY)


def nn(a, b):
    return lax.dot_general(a, b, (((1,), (0,)), ((), ())), preferred_element_type=f32)


def nt(a, b):
    return lax.dot_general(a, b, (((1,), (1,)), ((), ())), preferred_element_type=f32)


def tn(a, b):
    return lax.dot_general(a, b, (((0,), (0,)), ((), ())), preferred_element_type=f32)


def row_index(rows, columns):
    return lax.broadcasted_iota(jnp.int32, (rows, columns), 0)


def key_scale(rows, size, length, rate):
    slot = row_index(rows, size).astype(f32)
    remaining = (length - 1) - slot
    return jnp.where(remaining >= 0, jnp.exp(-rate * remaining), 0.0)


def query_scale(rows, size, rate):
    return jnp.exp(-rate * (row_index(rows, size) + 1).astype(f32))


def masked_rows(array, length):
    return jnp.where(row_index(*array.shape) < length, array, jnp.zeros_like(array))


def column(row):
    count = row.shape[1]
    return jnp.broadcast_to(row, (count, count)).T


def write_pieces(whole, outs, chip):
    piece = outs[0].shape[0]
    for offset, out in enumerate(outs):
        at = pl.multiple_of((chip ^ offset) * piece, piece)
        out[...] = whole[pl.ds(at, piece), :]


def read_pieces(pieces, whole, chip):
    piece = pieces[0].shape[0]
    for offset, part in enumerate(pieces):
        at = pl.multiple_of((chip ^ offset) * piece, piece)
        whole[pl.ds(at, piece), :] = part[...]


def near_kernel(query_any, key_any, value_any, query_ref, key_ref, value_ref, sems):
    copies = [
        pltpu.make_async_copy(source, target, sems.at[at])
        for at, (source, target) in enumerate(((key_any, key_ref), (value_any, value_ref), (query_any, query_ref)))
    ]
    for copy in copies:
        copy.start()
    for copy in copies:
        copy.wait()


def state_kernel(chips, length_ref, rate_ref, key_ref, value_ref, *rest):
    outs, whole = rest[:chips], rest[chips]
    own = lax.axis_index("seg")
    rows, wide = key_ref.shape
    size = whole.shape[1]
    lengths = length_ref[...].astype(f32)
    mine = lax.broadcasted_iota(jnp.int32, lengths.shape, 1) == own
    length = jnp.sum(jnp.where(mine, lengths, 0.0), axis=1, keepdims=True)
    pair = min(2 * size, wide)
    for first in range(0, wide, pair):
        scaled = []
        for begin in range(first, first + pair, size):
            head = begin // size
            scale = key_scale(rows, size, length, rate_ref[:, head:head + 1])
            scaled.append((value_ref[:, begin:begin + size].astype(f32) * scale).astype(bf16))
        both = tn(key_ref[:, first:first + pair], jnp.concatenate(scaled, axis=1))
        for begin in range(0, pair, size):
            span = slice(begin, begin + size)
            whole[first + begin:first + begin + size, :] = both[span, span]
    write_pieces(whole, outs, own // 2)


def decay_tiles(tile, rate, count, transposed):
    u = lax.broadcasted_iota(jnp.int32, (tile, tile), 1 if transposed else 0)
    w = lax.broadcasted_iota(jnp.int32, (tile, tile), 0 if transposed else 1)
    base = jnp.exp((w - u).astype(f32) * rate)
    tiles = [jnp.where(u >= w, base, 0.0)]
    for gap in range(1, count):
        tiles.append(base * jnp.exp(jnp.full((1, tile), -(gap * tile), f32) * rate))
    return tiles


def tree_distances(length_ref, parent_ref, table, count):
    for at in range(count):
        table[at] = jnp.int32(-1)

    def one(block, carry):
        above = parent_ref[block]
        passed = length_ref[jnp.maximum(above, 0)]
        for at in range(count):
            distance = table[(above + 1) * count + at]
            distance = jnp.where(distance >= 0, distance + passed, distance)
            table[(block + 1) * count + at] = jnp.where(above == at, 0, distance)
        return carry

    lax.fori_loop(0, count, one, 0)


def weight_table(length_ref, parent_ref, rate_ref, distances, table_ref, chips, size, piece):
    own = lax.axis_index("seg")
    chip, core = own // 2, own % 2
    count = 2 * chips
    tree_distances(length_ref, parent_ref, distances, count)
    row = row_index(8, size)
    rates = jnp.full((8, size), rate_ref[(chip * piece) // size], f32)
    for at in range(1, piece // size):
        rates = jnp.where(row == at, rate_ref[(chip * piece) // size + at], rates)
    for backward in range(2):
        for target in range(chips):
            wanted = (chip ^ target) * 2 + core
            for offset in range(chips):
                for sibling in range(2):
                    source = (chip ^ offset) * 2 + (core ^ sibling)
                    place = (source + 1) * count + wanted if backward else (wanted + 1) * count + source
                    distance = distances[place].astype(f32)
                    linked = (distance >= 0.0).astype(f32)
                    slot = ((backward * chips + target) * chips + offset) * 2 + sibling
                    table_ref[slot] = jnp.exp(rates * -distance) * linked


def local_head(size, tile, head, near, rate, query, key_ref, value_ref, out_ref):
    span = slice(head * size, (head + 1) * size)
    count = query.shape[0] // tile
    decays = decay_tiles(tile, rate, count, False)
    for i in range(count):
        total = None
        for j in range(i + 1):
            w_span = slice(j * tile, (j + 1) * tile)
            scores = nt(query[i * tile:(i + 1) * tile], key_ref[w_span, span])
            weighted = (scores * decays[i - j]).astype(bf16)
            part = nn(weighted, value_ref[w_span, span])
            total = part if total is None else total + part
        out_ref[i * tile:(i + 1) * tile, near * size:(near + 1) * size] = total


def local_kernel(size, tile, chips, piece, picked, length_ref, parent_ref, rate_ref, query_ref, key_ref, value_ref, *rest):
    out_ref, masked_ref, table_ref, facts_ref, distances = rest
    own = lax.axis_index("seg")
    rows, wide = query_ref.shape
    heads = wide // size
    length = length_ref[own]
    weight_table(length_ref, parent_ref, rate_ref, distances, table_ref, chips, size, piece)
    for head in range(heads):
        facts_ref[head:head + 1, :] = jnp.full((1, size), rate_ref[head], f32)
    facts_ref[heads:, :] = jnp.full((1, size), length.astype(f32), f32)
    masked_ref[...] = masked_rows(query_ref[...], length)
    for head in picked:
        query = masked_ref[:, head * size:(head + 1) * size]
        local_head(size, tile, head, head - picked[0], rate_ref[head], query, key_ref, value_ref, out_ref)


def tile_pairs(count):
    return [(i, j) for j in range(count) for i in range(j, count)]


def weighted_kernel(size, tile, picked, facts_ref, query_ref, key_ref, value_ref, out_ref, local_ref):
    rows, wide = query_ref.shape
    count = rows // tile
    for head in range(wide // size):
        span = slice(head * size, (head + 1) * size)
        rate = facts_ref[head:head + 1, :1]
        decays = decay_tiles(tile, rate, count, True)
        for place, (i, j) in enumerate(tile_pairs(count)):
            scores = nt(key_ref[j * tile:(j + 1) * tile, span], query_ref[i * tile:(i + 1) * tile, span])
            out_ref[head, place] = (scores * decays[i - j]).astype(bf16)
        if head in picked:
            local_head(size, tile, head, head - picked[0], rate, query_ref[:, span], key_ref, value_ref, local_ref)


def pick(refs, size, head):
    for ref in refs:
        here = ref.shape[1] // size
        if head < here:
            return ref[:, head * size:(head + 1) * size]
        head -= here


def mix_kernel(chips, size, backward, table_ref, *rest):
    mine, other, outs = rest[:chips], rest[chips:2 * chips], rest[len(rest) - chips:]
    piece = mine[0].shape[0]
    part = min(piece, size)
    for at in range(piece // part):
        span = slice(at * part, (at + 1) * part)
        totals = [None] * chips
        for offset in range(chips):
            for sibling, sources in ((0, mine), (1, other)):
                data = sources[offset][span, :]
                for target in range(chips):
                    slot = ((backward * chips + target) * chips + offset) * 2 + sibling
                    term = table_ref[slot, at:at + 1, :] * data
                    totals[target] = term if totals[target] is None else totals[target] + term
        for target in range(chips):
            outs[target][span, :] = totals[target]


def attend_kernel(chips, parts, facts_ref, query_ref, upstream_ref, gain_ref, *rest):
    local_refs, rest = rest[:parts], rest[parts:]
    pieces, attended_ref, sums_ref, whole = rest[:chips], rest[-3], rest[-2], rest[-1]
    own = lax.axis_index("seg")
    rows, wide = query_ref.shape
    size = whole.shape[1]
    read_pieces(pieces, whole, own // 2)
    squares = jnp.zeros((rows, size), f32)
    inners = jnp.zeros((rows, size), f32)
    for head in range(wide // size):
        span = slice(head * size, (head + 1) * size)
        carried = whole[span, :].astype(bf16)
        scale = query_scale(rows, size, facts_ref[head:head + 1, :])
        attended = pick(local_refs, size, head) + scale * nn(query_ref[:, span], carried)
        attended_ref[:, span] = attended
        scaled = upstream_ref[:, span].astype(f32) * gain_ref[:, span]
        squares = squares + attended * attended
        inners = inners + scaled * attended
    groups = rows // size
    for at in range(groups):
        span = slice(at * size, (at + 1) * size)
        sums_ref[at:at + 1, :] = jnp.sum(squares[span].T, axis=0, keepdims=True)
        sums_ref[groups + at:groups + at + 1, :] = jnp.sum(inners[span].T, axis=0, keepdims=True)


def norm_columns(sum_refs, width, inverse_ref, factor_ref):
    total = sum_refs[0][...]
    for ref in sum_refs[1:]:
        total = total + ref[...]
    groups = total.shape[0] // 2
    size = total.shape[1]
    inverse = lax.rsqrt(total[:groups] / width + norm_eps)
    factor = inverse * inverse * inverse * total[groups:] / width
    for at in range(groups):
        span = slice(at * size, (at + 1) * size)
        inverse_ref[span, :] = column(inverse[at:at + 1])
        factor_ref[span, :] = column(factor[at:at + 1])


def state_grad_kernel(chips, sums, width, facts_ref, query_ref, upstream_ref, attended_ref, gain_ref, *rest):
    sum_refs, outs = rest[:sums], rest[sums:sums + chips]
    inverse_ref, factor_ref, whole = rest[sums + chips:]
    own = lax.axis_index("seg")
    rows, wide = query_ref.shape
    size = whole.shape[1]
    norm_columns(sum_refs, width, inverse_ref, factor_ref)
    inverse = inverse_ref[...]
    factor = factor_ref[...]
    heads = wide // size
    group = min(2, heads)
    for first in range(0, heads, group):
        parts = []
        for head in range(first, first + group):
            span = slice(head * size, (head + 1) * size)
            scaled = upstream_ref[:, span].astype(f32) * gain_ref[:, span]
            grad = inverse * scaled - factor * attended_ref[:, span]
            parts.append((grad * query_scale(rows, size, facts_ref[head:head + 1, :])).astype(bf16))
        span = slice(first * size, (first + group) * size)
        both = tn(query_ref[:, span], jnp.concatenate(parts, axis=1))
        for at in range(group):
            inner = slice(at * size, (at + 1) * size)
            whole[(first + at) * size:(first + at + 1) * size, :] = both[inner, inner]
    write_pieces(whole, outs, own // 2)


def backward_kernel(chips, sums, width, tile, heads, done, facts_ref, query_ref, key_ref, value_ref, upstream_ref, attended_ref, weighted_ref, gain_ref, *rest):
    sum_refs, pieces, rest = rest[:sums], rest[sums:sums + chips], rest[sums + chips:]
    earlier, rest = rest[:2 * done], rest[2 * done:]
    if done:
        out_any, query_grad_any, key_grad_ref, value_grad_ref, inverse_ref, factor_ref, whole, out_ref, query_grad_ref, sems = rest
    else:
        out_ref, query_grad_ref, key_grad_ref, value_grad_ref, token_ref, inverse_ref, factor_ref, whole = rest
        token_ref[...] = jnp.zeros_like(token_ref)
    own = lax.axis_index("seg")
    rows, wide = query_ref.shape
    size = whole.shape[1]
    count = rows // tile
    copies = []

    def send(source, target, columns):
        copies.append(pltpu.make_async_copy(source, target.at[:, columns], sems.at[len(copies)]))
        copies[-1].start()

    if done:
        for source, target in zip(earlier, (out_any, query_grad_any)):
            send(source, target, pl.ds(0, source.shape[1]))
    norm_columns(sum_refs, width, inverse_ref, factor_ref)
    read_pieces(pieces, whole, own // 2)
    length = facts_ref[wide // size:, :]
    used = row_index(rows, size).astype(f32) < length
    for head in heads:
        span = slice(head * size, (head + 1) * size)
        near = slice((head - heads[0]) * size, (head - heads[0] + 1) * size)
        rate = facts_ref[head:head + 1, :]
        query = query_ref[:, span]
        key = key_ref[:, span]
        value = value_ref[:, span]
        gain = gain_ref[:, span]
        inverse = inverse_ref[...]
        attended = attended_ref[:, span]
        out_ref[:, near] = (attended * inverse * gain).astype(bf16)
        scaled = upstream_ref[:, span].astype(f32) * gain
        grad = (inverse * scaled - factor_ref[...] * attended).astype(bf16)
        carried = whole[span, :].astype(bf16)
        query_grad = nt(grad, carried) * query_scale(rows, size, rate)
        decays = decay_tiles(tile, rate[:, :1], count, True)
        query_totals, key_totals, value_totals = [None] * count, [None] * count, [None] * count
        for place, (i, j) in enumerate(tile_pairs(count)):
            u_span, w_span = slice(i * tile, (i + 1) * tile), slice(j * tile, (j + 1) * tile)
            score_grad = (nt(value[w_span], grad[u_span]) * decays[i - j]).astype(bf16)
            for totals, index, part in (
                (value_totals, j, nn(weighted_ref[head, place], grad[u_span])),
                (key_totals, j, nn(score_grad, query[u_span])),
                (query_totals, i, tn(score_grad, key[w_span])),
            ):
                totals[index] = part if totals[index] is None else totals[index] + part
        key_grad_ref[:, near] = jnp.concatenate(key_totals, axis=0).astype(bf16)
        value_grad_ref[:, near] = jnp.concatenate(value_totals, axis=0).astype(bf16)
        query_grad = query_grad + jnp.concatenate(query_totals, axis=0)
        query_grad_ref[:, near] = jnp.where(used, query_grad, 0.0).astype(bf16)
        if done:
            for source, target in ((out_ref, out_any), (query_grad_ref, query_grad_any)):
                send(source.at[:, near], target, pl.ds(head * size, size))
    for copy in copies:
        copy.wait()


def finish_kernel(chips, parts, step, facts_ref, key_ref, value_ref, *rest):
    local_refs, rest = rest[:2 * parts], rest[2 * parts:]
    pieces, key_hbm, value_hbm = rest[:chips], rest[chips], rest[chips + 1]
    whole, key_grad_ref, value_grad_ref, sems = rest[chips + 2:]
    own = lax.axis_index("seg")
    rows, wide = key_ref.shape
    size = whole.shape[1]
    heads = wide // size
    length = facts_ref[heads:, :]
    read_pieces(pieces, whole, own // 2)
    copies = []
    for at in range(wide // step):
        for begin in range(at * step, (at + 1) * step, size):
            span = slice(begin, begin + size)
            head = begin // size
            scale = key_scale(rows, size, length, facts_ref[head:head + 1, :])
            state_grad = whole[span, :].astype(bf16)
            key_part = scale * nt(value_ref[:, span], state_grad)
            value_part = scale * nn(key_ref[:, span], state_grad)
            key_grad_ref[:, span] = (pick(local_refs[::2], size, head).astype(f32) + key_part).astype(bf16)
            value_grad_ref[:, span] = (pick(local_refs[1::2], size, head).astype(f32) + value_part).astype(bf16)
        span = pl.ds(at * step, step)
        for kind, (source, target) in enumerate(((key_grad_ref, key_hbm), (value_grad_ref, value_hbm))):
            copy = pltpu.make_async_copy(source.at[:, span], target.at[:, span], sems.at[2 * at + kind])
            copy.start()
            copies.append(copy)
    for copy in copies:
        copy.wait()


def params(limit=VMEM_LIMIT):
    return pltpu.CompilerParams(vmem_limit_bytes=limit)


def shape(dims, dtype):
    return jax.ShapeDtypeStruct(dims, dtype)


def pass_on(piece_ref, before_ref, out_ref):
    pass


def after(piece, before):
    return pl.pallas_call(
        pass_on,
        out_shape=shape(piece.shape, piece.dtype),
        in_specs=[ANY_SPEC] * 2,
        out_specs=ANY_SPEC,
        input_output_aliases={0: 0},
        compiler_params=params(),
        name="after",
    )(piece, before)


def exchange(pieces, count):
    moved = [pieces[0]]
    for offset in range(1, len(pieces)):
        pairs = [(at, at ^ (2 * offset)) for at in range(count)]
        moved.append(lax.ppermute(pieces[offset], "seg", pairs))
    return moved


def swap_cores(pieces, count):
    pairs = [(at, at ^ 1) for at in range(count)]
    return [lax.ppermute(piece, "seg", pairs) for piece in pieces]


def add_kernel(left_ref, right_ref, out_ref):
    out_ref[...] = left_ref[...] + right_ref[...]


def head_sums(sums, count):
    step = 1
    parts = [sums]
    while step < count:
        if len(parts) == 2:
            parts = [
                pl.pallas_call(
                    add_kernel,
                    out_shape=shape(sums.shape, sums.dtype),
                    in_specs=[VMEM_SPEC] * 2,
                    out_specs=VMEM_SPEC,
                    compiler_params=params(),
                    name="add_sums",
                )(*parts)
            ]
        parts.append(lax.ppermute(parts[0], "head", [(at, at ^ step) for at in range(count)]))
        step *= 2
    return parts


def local(seg_count, head_count, queries, key_tokens, values, upstream, norm_gain, decay_rate, block_length, parent):
    rows, wide = queries.shape
    heads = decay_rate.shape[0]
    size = wide // heads
    width = wide * head_count
    chips = seg_count // 2
    piece = wide // chips
    group = min(2, heads) * size
    tile = min(256, rows)
    gain = norm_gain[None, :]
    piece_shapes = [shape((piece, size), f32)] * chips
    piece_specs = [VMEM_SPEC] * chips
    whole = pltpu.VMEM((wide, size), f32)
    tokens = pltpu.VMEM((rows, wide), bf16)

    query_near, key_near, value_near = pl.pallas_call(
        near_kernel,
        out_shape=[shape((rows, wide), bf16)] * 3,
        in_specs=[ANY_SPEC] * 3,
        out_specs=[VMEM_SPEC] * 3,
        scratch_shapes=[pltpu.SemaphoreType.DMA((3,))],
        compiler_params=params(FIRST_LIMIT),
        name="bring_near",
    )(queries, key_tokens, values)

    states = pl.pallas_call(
        functools.partial(state_kernel, chips),
        out_shape=piece_shapes,
        in_specs=[VMEM_SPEC] * 4,
        out_specs=piece_specs,
        scratch_shapes=[whole],
        compiler_params=params(),
        name="block_state",
    )(block_length[None, :], decay_rate[None, :], key_near, value_near)

    slots = 2 * chips * chips * 2
    half = heads // 2
    first_heads, last_heads = range(half), range(half, heads)
    first_local, masked, table, facts = pl.pallas_call(
        functools.partial(local_kernel, size, tile, chips, piece, first_heads),
        out_shape=[
            shape((rows, half * size), f32),
            shape((rows, wide), bf16),
            shape((slots, 8, size), f32),
            shape((heads + 1, size), f32),
        ],
        in_specs=[SMEM_SPEC] * 3 + [VMEM_SPEC] * 3,
        out_specs=[VMEM_SPEC] * 4,
        scratch_shapes=[pltpu.SMEM((seg_count * (seg_count + 1),), jnp.int32)],
        compiler_params=params(),
        cost_estimate=pl.CostEstimate(flops=2 * rows * rows * wide, bytes_accessed=10 * rows * wide, transcendentals=rows * rows * half),
        name="local_attention",
    )(block_length, parent, decay_rate, query_near, key_near, value_near)

    pairs = len(tile_pairs(rows // tile))
    weighted, last_local = pl.pallas_call(
        functools.partial(weighted_kernel, size, tile, last_heads),
        out_shape=[shape((heads, pairs, tile, tile), bf16), shape((rows, (heads - half) * size), f32)],
        in_specs=[VMEM_SPEC] * 4,
        out_specs=[VMEM_SPEC] * 2,
        compiler_params=params(),
        cost_estimate=pl.CostEstimate(flops=4 * rows * rows * wide, bytes_accessed=10 * rows * wide, transcendentals=rows * rows * heads),
        name="weighted_scores",
    )(facts, masked, key_near, value_near)

    def mix(pieces, backward, before):
        mine = exchange(pieces, seg_count)
        mine = mine[:1] + [after(piece, before) for piece in mine[1:]]
        other = swap_cores(mine, seg_count)
        mixed = pl.pallas_call(
            functools.partial(mix_kernel, chips, size, backward),
            out_shape=piece_shapes,
            in_specs=[VMEM_SPEC] + piece_specs * 2,
            out_specs=piece_specs,
            compiler_params=params(),
            name="mix_backward" if backward else "mix_forward",
        )(table, *mine, *other)
        return exchange(mixed, seg_count)

    carried = mix(states, 0, table)

    attended, sums = pl.pallas_call(
        functools.partial(attend_kernel, chips, 2),
        out_shape=[shape((rows, wide), f32), shape((2 * rows // size, size), f32)],
        in_specs=[VMEM_SPEC] * (6 + chips),
        out_specs=[VMEM_SPEC] * 2,
        scratch_shapes=[whole],
        compiler_params=params(),
        name="attend",
    )(facts, masked, upstream, gain, first_local, last_local, *carried)

    sum_parts = head_sums(sums, head_count)
    columns = pltpu.VMEM((rows, size), f32)

    state_grads = pl.pallas_call(
        functools.partial(state_grad_kernel, chips, len(sum_parts), width),
        out_shape=piece_shapes,
        in_specs=[VMEM_SPEC] * (5 + len(sum_parts)),
        out_specs=piece_specs,
        scratch_shapes=[columns, columns, whole],
        compiler_params=params(),
        name="state_grad",
    )(facts, masked, upstream, attended, gain, *sum_parts)

    def backward(picked, earlier):
        done = len(earlier) // 2
        near = (rows, len(picked) * size)
        if done:
            out_shape = [shape((rows, wide), bf16)] * 2 + [shape(near, bf16)] * 2
            out_specs = [ANY_SPEC] * 2 + [VMEM_SPEC] * 2
            scratch = [pltpu.VMEM(near, bf16)] * 2 + [pltpu.SemaphoreType.DMA((2 * (done + len(picked)),))]
        else:
            out_shape = [shape(near, bf16)] * 4 + [shape((8, size), f32)]
            out_specs = [VMEM_SPEC] * 5
            scratch = []
        return pl.pallas_call(
            functools.partial(backward_kernel, chips, len(sum_parts), width, tile, picked, done),
            out_shape=out_shape,
            in_specs=[VMEM_SPEC] * (8 + len(sum_parts) + chips + len(earlier)),
            out_specs=out_specs,
            scratch_shapes=[columns, columns, whole] + scratch,
            compiler_params=params(),
            cost_estimate=pl.CostEstimate(
                flops=8 * rows * rows * near[1], bytes_accessed=16 * rows * near[1], transcendentals=rows * rows * len(picked)
            ),
            name="local_backward",
        )(facts, masked, key_near, value_near, upstream, attended, weighted, gain, *sum_parts, *carried, *earlier)

    out_part, query_part, *local_grads, token = backward(first_heads, [])
    state_sums = mix(state_grads, 1, token)
    attention_out, query_grad, *more = backward(last_heads, [out_part, query_part])
    local_grads = local_grads + more

    key_grad, value_grad = pl.pallas_call(
        functools.partial(finish_kernel, chips, len(local_grads) // 2, size),
        out_shape=[shape((rows, wide), bf16)] * 2,
        in_specs=[VMEM_SPEC] * (3 + len(local_grads) + chips),
        out_specs=[ANY_SPEC] * 2,
        scratch_shapes=[whole, tokens, tokens, pltpu.SemaphoreType.DMA((2 * heads,))],
        compiler_params=params(),
        name="finish",
    )(facts, key_near, value_near, *local_grads, *state_sums)
    return attention_out, query_grad, key_grad, value_grad


def solution(mesh):
    sizes = dict(mesh.shape)
    tokens = P("seg", "head")
    return jax.shard_map(
        functools.partial(local, sizes["seg"], sizes["head"]),
        mesh=mesh,
        in_specs=(tokens, tokens, tokens, tokens, P("head"), P("head"), P(), P()),
        out_specs=(tokens, tokens, tokens, tokens),
        check_vma=False,
    )
```

```python
import functools

import jax
import jax.numpy as jnp
from jax import lax
from jax.experimental import pallas as pl
from jax.experimental.pallas import tpu as pltpu
from jax.sharding import PartitionSpec as P

norm_eps = 1e-05
f32 = jnp.float32
bf16 = jnp.bfloat16
VMEM_LIMIT = 40 * 1024 * 1024
FIRST_LIMIT = 504 * 1024 * 1024 // 10

SMEM_SPEC = pl.BlockSpec(memory_space=pltpu.SMEM)
VMEM_SPEC = pl.BlockSpec(memory_space=pltpu.VMEM)
ANY_SPEC = pl.BlockSpec(memory_space=pl.ANY)


def nn(a, b):
    return lax.dot_general(a, b, (((1,), (0,)), ((), ())), preferred_element_type=f32)


def nt(a, b):
    return lax.dot_general(a, b, (((1,), (1,)), ((), ())), preferred_element_type=f32)


def tn(a, b):
    return lax.dot_general(a, b, (((0,), (0,)), ((), ())), preferred_element_type=f32)


def side_by_side(parts):
    return jnp.concatenate(parts, axis=1)


def block_diagonal(blocks):
    zero = jnp.zeros_like(blocks[0])
    return jnp.concatenate([side_by_side([block if i == j else zero for j in range(len(blocks))]) for i, block in enumerate(blocks)], axis=0)


def row_index(rows, columns):
    return lax.broadcasted_iota(jnp.int32, (rows, columns), 0)


def key_scale(rows, size, length, rate):
    slot = row_index(rows, size).astype(f32)
    remaining = (length - 1) - slot
    return jnp.where(remaining >= 0, jnp.exp(-rate * remaining), 0.0)


def query_scale(rows, size, rate):
    return jnp.exp(-rate * (row_index(rows, size) + 1).astype(f32))


def masked_rows(array, length):
    return jnp.where(row_index(*array.shape) < length, array, jnp.zeros_like(array))


def column(row):
    count = row.shape[1]
    return jnp.broadcast_to(row, (count, count)).T


def add_to(totals, index, part):
    totals[index] = part if totals[index] is None else totals[index] + part


def core_offset(slot, core):
    crossed = (slot & ~3) | ((slot & 1) << 1) | ((slot & 2) >> 1)
    return slot + core * (crossed - slot)


class Layout:
    def __init__(self, rows, wide, size, chips):
        self.rows, self.wide, self.size, self.chips = rows, wide, size, chips
        self.heads = wide // size
        self.piece = wide // chips
        self.each = self.piece // size
        self.tile = min(256, rows)
        self.count = rows // self.tile

    def chip(self, slot, sibling=0):
        own = lax.axis_index("seg")
        crossing = False
        return (own // 2) ^ (core_offset(slot, (own % 2) ^ sibling) if crossing else slot)

    def head(self, place):
        if not self.each:
            return place
        return self.chip(place // self.each) * self.each + place % self.each

    def span(self, place):
        if not self.each:
            return pl.ds(place * self.size, self.size)
        return pl.ds(pl.multiple_of(self.head(place) * self.size, self.size), self.size)

    def near(self, places, place):
        at = list(places).index(place)
        return slice(at * self.size, (at + 1) * self.size)

    def places(self, offsets):
        if not self.each:
            return list(range(self.heads)) if 0 in offsets else []
        return [offset * self.each + at for offset in offsets for at in range(self.each)]

    def pairs(self, places):
        return [places[at:at + 2] for at in range(0, len(places), 2)]

    def state(self, pieces, place):
        if self.each:
            at = place % self.each
            return pieces[place // self.each][at * self.size:(at + 1) * self.size, :]
        first = place * self.size // self.piece
        parts = []
        for owner in range(first, first + self.size // self.piece):
            part = pieces[0][...]
            for offset in range(1, self.chips):
                part = jnp.where(self.chip(offset) == owner, pieces[offset][...], part)
            parts.append(part)
        return jnp.concatenate(parts, axis=0)


def near_kernel(key_any, value_any, query_any, key_ref, value_ref, query_ref, sems):
    moves = ((key_any, key_ref), (value_any, value_ref), (query_any, query_ref))
    copies = [pltpu.make_async_copy(source, target, sems.at[at]) for at, (source, target) in enumerate(moves)]
    for copy in copies:
        copy.start()
    for copy in copies:
        copy.wait()


def write_states(layout, offsets, left, right, outs, whole):
    size = layout.size
    if layout.each:
        places = layout.places(offsets)
        targets = [(outs[place // size_of], place % size_of) for place, size_of in ((at, layout.each) for at in range(len(places)))]
    else:
        places = list(range(layout.heads))
        targets = [(whole, place) for place in places]
    group = min(2, len(places))
    for first in range(0, len(places), group):
        chosen = places[first:first + group]
        both = tn(
            jnp.concatenate([left(place) for place in chosen], axis=1),
            jnp.concatenate([right(place) for place in chosen], axis=1),
        )
        for at in range(len(chosen)):
            inner = slice(at * size, (at + 1) * size)
            target, row = targets[first + at]
            target[row * size:(row + 1) * size, :] = both[inner, inner]
    if not layout.each:
        for offset, out in zip(offsets, outs):
            begin = pl.multiple_of(layout.chip(offset) * layout.piece, layout.piece)
            out[...] = whole[pl.ds(begin, layout.piece), :]


def state_kernel(layout, offsets, length_ref, rate_ref, key_ref, value_ref, *rest):
    outs, whole = rest[:len(offsets)], rest[len(offsets)]
    rows, size = layout.rows, layout.size
    lengths = length_ref[...].astype(f32)
    mine = lax.broadcasted_iota(jnp.int32, lengths.shape, 1) == lax.axis_index("seg")
    length = jnp.sum(jnp.where(mine, lengths, 0.0), axis=1, keepdims=True)
    rates = rate_ref[...]
    lane = lax.broadcasted_iota(jnp.int32, rates.shape, 1)

    def left(place):
        return key_ref[:, layout.span(place)]

    def right(place):
        rate = jnp.sum(jnp.where(lane == layout.head(place), rates, 0.0), axis=1, keepdims=True)
        return (value_ref[:, layout.span(place)].astype(f32) * key_scale(rows, size, length, rate)).astype(bf16)

    write_states(layout, offsets, left, right, outs, whole)


def decay_tiles(tile, rate, count, transposed):
    u = lax.broadcasted_iota(jnp.int32, (tile, tile), 1 if transposed else 0)
    w = lax.broadcasted_iota(jnp.int32, (tile, tile), 0 if transposed else 1)
    base = jnp.exp((w - u).astype(f32) * rate)
    tiles = [jnp.where(u >= w, base, 0.0)]
    for gap in range(1, count):
        tiles.append(base * jnp.exp(jnp.full((1, tile), -(gap * tile), f32) * rate))
    return tiles


def tree_distances(length_ref, parent_ref, table, count):
    for at in range(count):
        table[at] = jnp.int32(-1)

    def one(block, carry):
        above = parent_ref[block]
        passed = length_ref[jnp.maximum(above, 0)]
        for at in range(count):
            distance = table[(above + 1) * count + at]
            distance = jnp.where(distance >= 0, distance + passed, distance)
            table[(block + 1) * count + at] = jnp.where(above == at, 0, distance)
        return carry

    lax.fori_loop(0, count, one, 0)


def weight_table(layout, length_ref, parent_ref, rate_ref, distances, table_ref):
    own = lax.axis_index("seg")
    chip, core = own // 2, own % 2
    chips, size, piece = layout.chips, layout.size, layout.piece
    count = 2 * chips
    tree_distances(length_ref, parent_ref, distances, count)
    row = row_index(8, size)
    rates = jnp.full((8, size), rate_ref[(chip * piece) // size], f32)
    for at in range(1, piece // size):
        rates = jnp.where(row == at, rate_ref[(chip * piece) // size + at], rates)
    for backward in range(2):
        for target in range(chips):
            wanted = layout.chip(target) * 2 + core
            for offset in range(chips):
                for sibling in range(2):
                    source = layout.chip(offset, sibling) * 2 + (core ^ sibling)
                    place = (source + 1) * count + wanted if backward else (wanted + 1) * count + source
                    distance = distances[place].astype(f32)
                    linked = (distance >= 0.0).astype(f32)
                    slot = ((backward * chips + target) * chips + offset) * 2 + sibling
                    table_ref[slot] = jnp.exp(rates * -distance) * linked


def local_head(layout, rate, query, key, value):
    tile, count = layout.tile, layout.count
    decays = decay_tiles(tile, rate, count, False)
    totals = [None] * count
    for i in range(count):
        for j in range(i + 1):
            w_span = slice(j * tile, (j + 1) * tile)
            scores = nt(query[i * tile:(i + 1) * tile], key[w_span])
            weighted = (scores * decays[i - j]).astype(bf16)
            add_to(totals, i, nn(weighted, value[w_span]))
    return jnp.concatenate(totals, axis=0)


def local_kernel(layout, places, length_ref, parent_ref, rate_ref, query_ref, key_ref, value_ref, out_ref, masked_ref, scaled_ref, table_ref, facts_ref, distances):
    length = length_ref[lax.axis_index("seg")]
    weight_table(layout, length_ref, parent_ref, rate_ref, distances, table_ref)
    heads, size = layout.heads, layout.size
    for place in range(heads):
        facts_ref[place:place + 1, :] = jnp.full((1, size), rate_ref[layout.head(place)], f32)
    facts_ref[heads:, :] = jnp.full((1, size), length.astype(f32), f32)
    masked_ref[...] = masked_rows(query_ref[...], length)
    for place in range(heads):
        span = layout.span(place)
        scale = query_scale(layout.rows, size, rate_ref[layout.head(place)])
        scaled_ref[:, span] = (masked_ref[:, span].astype(f32) * scale).astype(bf16)
    for place in places:
        span = layout.span(place)
        rate = rate_ref[layout.head(place)]
        out_ref[:, layout.near(places, place)] = local_head(layout, rate, masked_ref[:, span], key_ref[:, span], value_ref[:, span])


def tile_pairs(count):
    return [(i, j) for j in range(count) for i in range(j, count)]


def weighted_kernel(layout, places, facts_ref, query_ref, key_ref, value_ref, out_ref, local_ref, key_end_ref, value_end_ref):
    tile = layout.tile
    length = facts_ref[layout.heads:, :]
    for place in range(layout.heads):
        span = layout.span(place)
        scale = key_scale(layout.rows, layout.size, length, facts_ref[place:place + 1, :])
        key_end_ref[:, span] = (key_ref[:, span].astype(f32) * scale).astype(bf16)
        value_end_ref[:, span] = (value_ref[:, span].astype(f32) * scale).astype(bf16)
        rate = facts_ref[place:place + 1, :1]
        query, key = query_ref[:, span], key_ref[:, span]
        decays = decay_tiles(tile, rate, layout.count, True)
        for at, (i, j) in enumerate(tile_pairs(layout.count)):
            scores = nt(key[j * tile:(j + 1) * tile], query[i * tile:(i + 1) * tile])
            out_ref[place, at] = (scores * decays[i - j]).astype(bf16)
        if place in places:
            local_ref[:, layout.near(places, place)] = local_head(layout, rate, query, key, value_ref[:, span])


def mix_kernel(layout, backward, targets, table_ref, *rest):
    chips, size, piece = layout.chips, layout.size, layout.piece
    mine, other, outs = rest[:chips], rest[chips:2 * chips], rest[len(rest) - len(targets):]
    part = min(piece, size)
    for at in range(piece // part):
        span = slice(at * part, (at + 1) * part)
        totals = [None] * len(targets)
        for offset in range(chips):
            for sibling, sources in ((0, mine), (1, other)):
                data = sources[offset][span, :]
                for index, target in enumerate(targets):
                    slot = ((backward * chips + target) * chips + offset) * 2 + sibling
                    add_to(totals, index, table_ref[slot, at:at + 1, :] * data)
        for out, total in zip(outs, totals):
            out[span, :] = total


def attend_kernel(layout, places, last, scaled_ref, upstream_ref, gain_ref, local_ref, *rest):
    pieces, rest = rest[:layout.chips], rest[layout.chips:]
    rows, size = layout.rows, layout.size
    if last is None:
        attended_ref, squares_ref, inners_ref = rest
        squares = jnp.zeros((rows, size), f32)
        inners = jnp.zeros((rows, size), f32)
    else:
        *before, attended_ref, sums_ref = rest
        squares, inners = (before[0][...], before[1][...]) if before else (jnp.zeros((rows, size), f32),) * 2
    for chosen in layout.pairs(places):
        carried = block_diagonal([layout.state(pieces, place).astype(bf16) for place in chosen])
        both = nn(side_by_side([scaled_ref[:, layout.span(place)] for place in chosen]), carried)
        for at, place in enumerate(chosen):
            span, near = layout.span(place), layout.near(places, place)
            attended = local_ref[:, near] + both[:, at * size:(at + 1) * size]
            attended_ref[:, near] = attended
            scaled = upstream_ref[:, span].astype(f32) * gain_ref[:, span]
            squares = squares + attended * attended
            inners = inners + scaled * attended
    if last is None:
        squares_ref[...] = squares
        inners_ref[...] = inners
        return
    groups = rows // size
    for at in range(groups):
        span = slice(at * size, (at + 1) * size)
        sums_ref[at:at + 1, :] = jnp.sum(squares[span].T, axis=0, keepdims=True)
        sums_ref[groups + at:groups + at + 1, :] = jnp.sum(inners[span].T, axis=0, keepdims=True)


def norm_columns(sum_refs, width, inverse_ref, factor_ref):
    total = sum_refs[0][...]
    for ref in sum_refs[1:]:
        total = total + ref[...]
    groups = total.shape[0] // 2
    size = total.shape[1]
    inverse = lax.rsqrt(total[:groups] / width + norm_eps)
    factor = inverse * inverse * inverse * total[groups:] / width
    for at in range(groups):
        span = slice(at * size, (at + 1) * size)
        inverse_ref[span, :] = column(inverse[at:at + 1])
        factor_ref[span, :] = column(factor[at:at + 1])


def pick(layout, groups, refs, place, rows=slice(None)):
    for places, ref in zip(groups, refs):
        if place in places:
            return ref[rows, layout.near(places, place)]
    raise ValueError(place)


def state_grad_kernel(layout, groups, offsets, sums, width, facts_ref, query_ref, upstream_ref, gain_ref, *rest):
    attended_refs, rest = rest[:len(groups)], rest[len(groups):]
    if sums:
        sum_refs, rest = rest[:sums], rest[sums:]
        outs, (inverse_ref, factor_ref, whole) = rest[:len(offsets)], rest[len(offsets):]
        norm_columns(sum_refs, width, inverse_ref, factor_ref)
    else:
        inverse_ref, factor_ref, *outs, whole = rest
    rows, size = layout.rows, layout.size
    inverse = inverse_ref[...]
    factor = factor_ref[...]

    def left(place):
        return query_ref[:, layout.span(place)]

    def right(place):
        span = layout.span(place)
        scaled = upstream_ref[:, span].astype(f32) * gain_ref[:, span]
        grad = inverse * scaled - factor * pick(layout, groups, attended_refs, place)
        return (grad * query_scale(rows, size, facts_ref[place:place + 1, :])).astype(bf16)

    write_states(layout, offsets, left, right, outs, whole)


def send(layout, places, place, sources, targets, sems, copies):
    for source, target in zip(sources, targets):
        near = source.at[:, layout.near(places, place)]
        copies.append(pltpu.make_async_copy(near, target.at[:, layout.span(place)], sems.at[len(copies)]))
        copies[-1].start()


def send_all(layout, kept, earlier, targets, sems, copies):
    for at, places in enumerate(kept):
        for place in places:
            send(layout, places, place, earlier[2 * at:2 * at + 2], targets, sems, copies)


def backward_kernel(layout, groups, places, kept, last, facts_ref, query_ref, key_ref, value_ref, upstream_ref, weighted_ref, gain_ref, inverse_ref, factor_ref, *rest):
    attended_refs, rest = rest[:len(groups)], rest[len(groups):]
    pieces, rest = rest[:layout.chips], rest[layout.chips:]
    earlier, rest = rest[:2 * len(kept)], rest[2 * len(kept):]
    rows, size, tile, count = layout.rows, layout.size, layout.tile, layout.count
    copies = []
    if last:
        out_any, query_grad_any, key_grad_ref, value_grad_ref, out_ref, query_grad_ref, sems = rest
        targets = (out_any, query_grad_any)
        send_all(layout, kept, earlier, targets, sems, copies)
    else:
        out_ref, query_grad_ref, key_grad_ref, value_grad_ref, token_ref = rest
        token_ref[...] = jnp.zeros_like(token_ref)
    used = row_index(rows, size).astype(f32) < facts_ref[layout.heads:, :]
    for place in places:
        span, near = layout.span(place), layout.near(places, place)
        rate = facts_ref[place:place + 1, :]
        query = query_ref[:, span]
        key = key_ref[:, span]
        value = value_ref[:, span]
        gain = gain_ref[:, span]
        inverse = inverse_ref[...]
        attended = pick(layout, groups, attended_refs, place)
        out_ref[:, near] = (attended * inverse * gain).astype(bf16)
        scaled = upstream_ref[:, span].astype(f32) * gain
        grad = (inverse * scaled - factor_ref[...] * attended).astype(bf16)
        carried = layout.state(pieces, place).astype(bf16)
        query_grad = nt(grad, carried) * query_scale(rows, size, rate)
        decays = decay_tiles(tile, rate[:, :1], count, True)
        query_totals, key_totals, value_totals = [None] * count, [None] * count, [None] * count
        for at, (i, j) in enumerate(tile_pairs(count)):
            u_span, w_span = slice(i * tile, (i + 1) * tile), slice(j * tile, (j + 1) * tile)
            score_grad = (nt(value[w_span], grad[u_span]) * decays[i - j]).astype(bf16)
            add_to(value_totals, j, nn(weighted_ref[place, at], grad[u_span]))
            add_to(key_totals, j, nn(score_grad, query[u_span]))
            add_to(query_totals, i, tn(score_grad, key[w_span]))
        key_grad_ref[:, near] = jnp.concatenate(key_totals, axis=0).astype(bf16)
        value_grad_ref[:, near] = jnp.concatenate(value_totals, axis=0).astype(bf16)
        query_grad = query_grad + jnp.concatenate(query_totals, axis=0)
        query_grad_ref[:, near] = jnp.where(used, query_grad, 0.0).astype(bf16)
        if last:
            send(layout, places, place, (out_ref, query_grad_ref), targets, sems, copies)
    for copy in copies:
        copy.wait()


def finish_kernel(layout, groups, places, first, last, key_end_ref, value_end_ref, *rest):
    key_locals, value_locals, rest = rest[:len(groups)], rest[len(groups):2 * len(groups)], rest[2 * len(groups):]
    pieces, rest = rest[:layout.chips], rest[layout.chips + (0 if first else 2):]
    key_full, value_full, *rest = rest
    half = layout.rows // 2 if last else layout.rows
    states = [layout.state(pieces, place).astype(bf16) for place in places]
    copies = []
    for begin in range(0, layout.rows, half):
        part = slice(begin, begin + half)
        for state_grad, place in zip(states, places):
            span = layout.span(place)
            key_part = nt(value_end_ref[part, span], state_grad)
            value_part = nn(key_end_ref[part, span], state_grad)
            key_full[part, span] = (pick(layout, groups, key_locals, place, part).astype(f32) + key_part).astype(bf16)
            value_full[part, span] = (pick(layout, groups, value_locals, place, part).astype(f32) + value_part).astype(bf16)
        if last:
            key_any, value_any, sems = rest
            for source, target in ((key_full, key_any), (value_full, value_any)):
                copies.append(pltpu.make_async_copy(source.at[part, :], target.at[part, :], sems.at[len(copies)]))
                copies[-1].start()
    for copy in copies:
        copy.wait()


def params(limit=VMEM_LIMIT):
    return pltpu.CompilerParams(vmem_limit_bytes=limit)


def shape(dims, dtype):
    return jax.ShapeDtypeStruct(dims, dtype)


def pass_on(piece_ref, before_ref, out_ref):
    pass


def after(piece, before):
    return pl.pallas_call(
        pass_on,
        out_shape=shape(piece.shape, piece.dtype),
        in_specs=[ANY_SPEC] * 2,
        out_specs=ANY_SPEC,
        input_output_aliases={0: 0},
        compiler_params=params(),
        name="after",
    )(piece, before)


def exchange(pieces, count):
    moved = [pieces[0]]
    for slot in range(1, len(pieces)):
        pairs = [(at, at ^ (2 * (core_offset(slot, at % 2) if False else slot))) for at in range(count)]
        moved.append(lax.ppermute(pieces[slot], "seg", pairs))
    return moved


def one_by_one(pieces, before, order):
    taken = list(pieces)
    for slot in order:
        taken[slot] = before = after(pieces[slot], before)
    return taken


def swap_cores(pieces, count):
    pairs = [(at, at ^ 1) for at in range(count)]
    return [lax.ppermute(piece, "seg", pairs) for piece in pieces]


def add_kernel(left_ref, right_ref, out_ref):
    out_ref[...] = left_ref[...] + right_ref[...]


def head_sums(sums, count):
    step = 1
    parts = [sums]
    while step < count:
        if len(parts) == 2:
            parts = [
                pl.pallas_call(
                    add_kernel,
                    out_shape=shape(sums.shape, sums.dtype),
                    in_specs=[VMEM_SPEC] * 2,
                    out_specs=VMEM_SPEC,
                    compiler_params=params(),
                    name="add_sums",
                )(*parts)
            ]
        parts.append(lax.ppermute(parts[0], "head", [(at, at ^ step) for at in range(count)]))
        step *= 2
    return parts


def local(seg_count, head_count, queries, key_tokens, values, upstream, norm_gain, decay_rate, block_length, parent):
    rows, wide = queries.shape
    heads = decay_rate.shape[0]
    size = wide // heads
    width = wide * head_count
    chips = seg_count // 2
    layout = Layout(rows, wide, size, chips)
    gain = norm_gain[None, :]
    piece_shape = shape((layout.piece, size), f32)
    whole = pltpu.VMEM((wide, size), f32)
    columns = shape((rows, size), f32)
    offsets = list(range(chips))
    sends = [[slot for slot in offsets if 0 < slot < 3], [slot for slot in offsets if slot == 0 or slot >= 3]]
    groups = [group for group in (layout.places(offsets[:2]), layout.places(offsets[2:])) if group]
    whole_sends = [sends[0] + sends[1]]
    early, late = groups if len(groups) == 2 else (groups[0], [])

    def near_shape(places, dtype):
        return shape((rows, len(places) * size), dtype)

    def near_scratch(places, dtype):
        return pltpu.VMEM((rows, len(places) * size), dtype)

    def in_order(parts):
        return [dict(zip(sends[0] + sends[1], parts))[offset] for offset in offsets]

    key_near, value_near, query_near = pl.pallas_call(
        near_kernel,
        out_shape=[shape((rows, wide), bf16)] * 3,
        in_specs=[ANY_SPEC] * 3,
        out_specs=[VMEM_SPEC] * 3,
        scratch_shapes=[pltpu.SemaphoreType.DMA((3,))],
        compiler_params=params(FIRST_LIMIT),
        name="bring_near",
    )(key_tokens, values, queries)

    states = []
    for chosen in whole_sends:
        states += pl.pallas_call(
            functools.partial(state_kernel, layout, chosen),
            out_shape=[piece_shape] * len(chosen),
            in_specs=[VMEM_SPEC] * 4,
            out_specs=[VMEM_SPEC] * len(chosen),
            scratch_shapes=[whole],
            compiler_params=params(),
            name="block_state",
        )(block_length[None, :], decay_rate[None, :], key_near, value_near)

    early_local, masked, scaled, table, facts = pl.pallas_call(
        functools.partial(local_kernel, layout, early),
        out_shape=[
            near_shape(early, f32),
            shape((rows, wide), bf16),
            shape((rows, wide), bf16),
            shape((4 * chips * chips, 8, size), f32),
            shape((heads + 1, size), f32),
        ],
        in_specs=[SMEM_SPEC] * 3 + [VMEM_SPEC] * 3,
        out_specs=[VMEM_SPEC] * 5,
        scratch_shapes=[pltpu.SMEM((seg_count * (seg_count + 1),), jnp.int32)],
        compiler_params=params(),
        cost_estimate=pl.CostEstimate(flops=2 * rows * rows * wide, bytes_accessed=10 * rows * wide, transcendentals=rows * rows * heads),
        name="local_attention",
    )(block_length, parent, decay_rate, query_near, key_near, value_near)

    pairs = len(tile_pairs(layout.count))
    weighted, late_local, key_end, value_end = pl.pallas_call(
        functools.partial(weighted_kernel, layout, late),
        out_shape=[shape((heads, pairs, layout.tile, layout.tile), bf16), near_shape(late or [0], f32)] + [shape((rows, wide), bf16)] * 2,
        in_specs=[VMEM_SPEC] * 4,
        out_specs=[VMEM_SPEC] * 4,
        compiler_params=params(),
        cost_estimate=pl.CostEstimate(flops=4 * rows * rows * wide, bytes_accessed=10 * rows * wide, transcendentals=rows * rows * heads),
        name="weighted_scores",
    )(facts, masked, key_near, value_near)

    def mix(pieces, backward, before):
        mine = exchange(pieces, seg_count)
        mine = mine[:1] + [after(piece, before) for piece in mine[1:]]
        other = swap_cores(mine, seg_count)
        mixed = []
        for chosen in whole_sends:
            mixed += pl.pallas_call(
                functools.partial(mix_kernel, layout, backward, chosen),
                out_shape=[piece_shape] * len(chosen),
                in_specs=[VMEM_SPEC] * (1 + 2 * chips) + [ANY_SPEC] * len(mixed[:1]),
                out_specs=[VMEM_SPEC] * len(chosen),
                compiler_params=params(),
                cost_estimate=pl.CostEstimate(flops=rows * rows * wide, bytes_accessed=10 * rows * wide, transcendentals=0),
                name="mix_backward" if backward else "mix_forward",
            )(table, *mine, *other, *mixed[:1])
        return exchange(in_order(mixed), seg_count)

    def shown(pieces, places):
        if not layout.each:
            return pieces
        return [piece if offset * layout.each in places else pieces[0] for offset, piece in enumerate(pieces)]

    carried = mix(in_order(states), 0, table)

    attended, before = [], []
    for index, (places, local_out) in enumerate(zip(groups, (early_local, late_local))):
        last = True if index == len(groups) - 1 else None
        out_shape = [near_shape(places, f32)] + ([shape((2 * rows // size, size), f32)] if last else [columns] * 2)
        part, *before = pl.pallas_call(
            functools.partial(attend_kernel, layout, places, last),
            out_shape=out_shape,
            in_specs=[VMEM_SPEC] * (4 + chips + len(before)),
            out_specs=[VMEM_SPEC] * len(out_shape),
            compiler_params=params(),
            cost_estimate=pl.CostEstimate(flops=rows * rows * wide, bytes_accessed=10 * rows * wide, transcendentals=rows * wide),
            name="attend",
        )(scaled, upstream, gain, local_out, *shown(carried, places), *before)
        attended.append(part)
    sum_parts = head_sums(before[0], head_count)

    state_grads, norms = [], []
    for chosen in whole_sends:
        first = not norms
        parts = pl.pallas_call(
            functools.partial(state_grad_kernel, layout, groups, chosen, len(sum_parts) if first else 0, width),
            out_shape=[piece_shape] * len(chosen) + ([columns] * 2 if first else []),
            in_specs=[VMEM_SPEC] * (4 + len(groups) + (len(sum_parts) if first else 2)),
            out_specs=[VMEM_SPEC] * (len(chosen) + (2 if first else 0)),
            scratch_shapes=[whole],
            compiler_params=params(),
            name="state_grad",
        )(facts, masked, upstream, gain, *attended, *(sum_parts if first else norms))
        state_grads += parts[:len(chosen)]
        norms = norms or parts[len(chosen):]

    def ending(places, kept, last):
        if not last:
            return [near_shape(places, bf16)] * 2, [VMEM_SPEC] * 2, []
        amount = len(places) + sum(len(group) for group in kept)
        scratch = [near_scratch(places, bf16)] * 2 + [pltpu.SemaphoreType.DMA((2 * amount,))]
        return [shape((rows, wide), bf16)] * 2, [ANY_SPEC] * 2, scratch

    def backward(places, kept, earlier, last):
        out_shape, out_specs, scratch = ending(places, kept, last)
        out_shape = out_shape + [near_shape(places, bf16)] * 2 + ([] if last else [shape((8, size), f32)])
        return pl.pallas_call(
            functools.partial(backward_kernel, layout, groups, places, kept, last),
            out_shape=out_shape,
            in_specs=[VMEM_SPEC] * (9 + len(groups) + chips + len(earlier)),
            out_specs=out_specs + [VMEM_SPEC] * (len(out_shape) - 2),
            scratch_shapes=scratch,
            compiler_params=params(),
            cost_estimate=pl.CostEstimate(
                flops=8 * rows * rows * size * len(places),
                bytes_accessed=16 * rows * size * len(places),
                transcendentals=rows * rows * len(places),
            ),
            name="local_backward",
        )(facts, masked, key_near, value_near, upstream, weighted, gain, *norms, *attended, *carried, *earlier)

    cut = heads * 4 // 8 if heads > 2 else heads // 2
    halves = [list(range(cut)), list(range(cut, heads))]
    out_part, query_part, key_first, value_first, token = backward(halves[0], [], [], False)
    state_sums = mix(in_order(state_grads), 1, token)
    attention_out, query_grad, key_last, value_last = backward(halves[1], halves[:1], [out_part, query_part], True)

    fulls = []
    for index, places in enumerate(groups):
        first, last = index == 0, index == len(groups) - 1
        inputs = 6 + chips
        fulls = pl.pallas_call(
            functools.partial(finish_kernel, layout, halves, places, first, last),
            out_shape=[shape((rows, wide), bf16)] * (4 if last else 2),
            in_specs=[VMEM_SPEC] * (inputs + len(fulls)),
            out_specs=[VMEM_SPEC] * 2 + [ANY_SPEC] * (2 if last else 0),
            scratch_shapes=[pltpu.SemaphoreType.DMA((4,))] if last else [],
            input_output_aliases={inputs + at: at for at in range(len(fulls))},
            compiler_params=params(),
            cost_estimate=pl.CostEstimate(flops=rows * rows * wide, bytes_accessed=10 * rows * wide, transcendentals=rows * wide),
            name="finish",
        )(key_end, value_end, key_first, key_last, value_first, value_last, *shown(state_sums, places), *fulls)
    return attention_out, query_grad, *fulls[2:]


def solution(mesh):
    sizes = dict(mesh.shape)
    tokens = P("seg", "head")
    return jax.shard_map(
        functools.partial(local, sizes["seg"], sizes["head"]),
        mesh=mesh,
        in_specs=(tokens, tokens, tokens, tokens, P("head"), P("head"), P(), P()),
        out_specs=(tokens, tokens, tokens, tokens),
        check_vma=False,
    )
```

```python
import functools

import jax
import jax.numpy as jnp
from jax import lax
from jax.experimental import pallas as pl
from jax.experimental.pallas import tpu as pltpu
from jax.sharding import PartitionSpec as P

norm_eps = 1e-05
f32 = jnp.float32
bf16 = jnp.bfloat16
VMEM_LIMIT = 40 * 1024 * 1024
FIRST_LIMIT = 514 * 1024 * 1024 // 10

SMEM_SPEC = pl.BlockSpec(memory_space=pltpu.SMEM)
VMEM_SPEC = pl.BlockSpec(memory_space=pltpu.VMEM)
ANY_SPEC = pl.BlockSpec(memory_space=pl.ANY)


def nn(a, b):
    return lax.dot_general(a, b, (((1,), (0,)), ((), ())), preferred_element_type=f32)


def nt(a, b):
    return lax.dot_general(a, b, (((1,), (1,)), ((), ())), preferred_element_type=f32)


def tn(a, b):
    return lax.dot_general(a, b, (((0,), (0,)), ((), ())), preferred_element_type=f32)


def side_by_side(parts):
    return jnp.concatenate(parts, axis=1)


def block_diagonal(blocks):
    zero = jnp.zeros_like(blocks[0])
    return jnp.concatenate([side_by_side([block if i == j else zero for j in range(len(blocks))]) for i, block in enumerate(blocks)], axis=0)


def row_index(rows, columns):
    return lax.broadcasted_iota(jnp.int32, (rows, columns), 0)


def key_scale(rows, size, length, rate):
    slot = row_index(rows, size).astype(f32)
    remaining = (length - 1) - slot
    return jnp.where(remaining >= 0, jnp.exp(-rate * remaining), 0.0)


def query_scale(rows, size, rate):
    return jnp.exp(-rate * (row_index(rows, size) + 1).astype(f32))


def masked_rows(array, length):
    return jnp.where(row_index(*array.shape) < length, array, jnp.zeros_like(array))


def column(row):
    count = row.shape[1]
    return jnp.broadcast_to(row, (count, count)).T


def add_to(totals, index, part):
    totals[index] = part if totals[index] is None else totals[index] + part


def core_offset(slot, core):
    crossed = (slot & ~3) | ((slot & 1) << 1) | ((slot & 2) >> 1)
    return slot + core * (crossed - slot)


class Layout:
    def __init__(self, rows, wide, size, chips):
        self.rows, self.wide, self.size, self.chips = rows, wide, size, chips
        self.heads = wide // size
        self.piece = wide // chips
        self.each = self.piece // size
        self.tile = min(256, rows)
        self.count = rows // self.tile

    def chip(self, slot, sibling=0):
        own = lax.axis_index("seg")
        crossing = False
        return (own // 2) ^ (core_offset(slot, (own % 2) ^ sibling) if crossing else slot)

    def head(self, place):
        if not self.each:
            return place
        return self.chip(place // self.each) * self.each + place % self.each

    def span(self, place):
        if not self.each:
            return pl.ds(place * self.size, self.size)
        return pl.ds(pl.multiple_of(self.head(place) * self.size, self.size), self.size)

    def near(self, places, place):
        at = list(places).index(place)
        return slice(at * self.size, (at + 1) * self.size)

    def places(self, offsets):
        if not self.each:
            return list(range(self.heads)) if 0 in offsets else []
        return [offset * self.each + at for offset in offsets for at in range(self.each)]

    def pairs(self, places):
        return [places[at:at + 2] for at in range(0, len(places), 2)]

    def state(self, pieces, place):
        if self.each:
            at = place % self.each
            return pieces[place // self.each][at * self.size:(at + 1) * self.size, :]
        first = place * self.size // self.piece
        parts = []
        for owner in range(first, first + self.size // self.piece):
            part = pieces[0][...]
            for offset in range(1, self.chips):
                part = jnp.where(self.chip(offset) == owner, pieces[offset][...], part)
            parts.append(part)
        return jnp.concatenate(parts, axis=0)


def near_kernel(key_any, value_any, query_any, key_ref, value_ref, sems):
    moves = ((key_any, key_ref), (value_any, value_ref))
    copies = [pltpu.make_async_copy(source, target, sems.at[at]) for at, (source, target) in enumerate(moves)]
    for copy in copies:
        copy.start()
    for copy in copies:
        copy.wait()


def write_states(layout, offsets, left, right, outs, whole):
    size = layout.size
    if layout.each:
        places = layout.places(offsets)
        targets = [(outs[place // size_of], place % size_of) for place, size_of in ((at, layout.each) for at in range(len(places)))]
    else:
        places = list(range(layout.heads))
        targets = [(whole, place) for place in places]
    group = min(2, len(places))
    for first in range(0, len(places), group):
        chosen = places[first:first + group]
        both = tn(
            jnp.concatenate([left(place) for place in chosen], axis=1),
            jnp.concatenate([right(place) for place in chosen], axis=1),
        )
        for at in range(len(chosen)):
            inner = slice(at * size, (at + 1) * size)
            target, row = targets[first + at]
            target[row * size:(row + 1) * size, :] = both[inner, inner]
    if not layout.each:
        for offset, out in zip(offsets, outs):
            begin = pl.multiple_of(layout.chip(offset) * layout.piece, layout.piece)
            out[...] = whole[pl.ds(begin, layout.piece), :]


def state_kernel(layout, offsets, length_ref, rate_ref, key_ref, value_ref, *rest):
    outs, whole = rest[:len(offsets)], rest[len(offsets)]
    rows, size = layout.rows, layout.size
    lengths = length_ref[...].astype(f32)
    mine = lax.broadcasted_iota(jnp.int32, lengths.shape, 1) == lax.axis_index("seg")
    length = jnp.sum(jnp.where(mine, lengths, 0.0), axis=1, keepdims=True)
    rates = rate_ref[...]
    lane = lax.broadcasted_iota(jnp.int32, rates.shape, 1)

    def left(place):
        return key_ref[:, layout.span(place)]

    def right(place):
        rate = jnp.sum(jnp.where(lane == layout.head(place), rates, 0.0), axis=1, keepdims=True)
        return (value_ref[:, layout.span(place)].astype(f32) * key_scale(rows, size, length, rate)).astype(bf16)

    write_states(layout, offsets, left, right, outs, whole)


def decay_tiles(tile, rate, count, transposed):
    u = lax.broadcasted_iota(jnp.int32, (tile, tile), 1 if transposed else 0)
    w = lax.broadcasted_iota(jnp.int32, (tile, tile), 0 if transposed else 1)
    base = jnp.exp((w - u).astype(f32) * rate)
    tiles = [jnp.where(u >= w, base, 0.0)]
    for gap in range(1, count):
        tiles.append(base * jnp.exp(jnp.full((1, tile), -(gap * tile), f32) * rate))
    return tiles


def tree_distances(length_ref, parent_ref, table, count):
    for at in range(count):
        table[at] = jnp.int32(-1)

    def one(block, carry):
        above = parent_ref[block]
        passed = length_ref[jnp.maximum(above, 0)]
        for at in range(count):
            distance = table[(above + 1) * count + at]
            distance = jnp.where(distance >= 0, distance + passed, distance)
            table[(block + 1) * count + at] = jnp.where(above == at, 0, distance)
        return carry

    lax.fori_loop(0, count, one, 0)


def weight_table(layout, length_ref, parent_ref, rate_ref, distances, table_ref):
    own = lax.axis_index("seg")
    chip, core = own // 2, own % 2
    chips, size, piece = layout.chips, layout.size, layout.piece
    count = 2 * chips
    tree_distances(length_ref, parent_ref, distances, count)
    row = row_index(8, size)
    rates = jnp.full((8, size), rate_ref[(chip * piece) // size], f32)
    for at in range(1, piece // size):
        rates = jnp.where(row == at, rate_ref[(chip * piece) // size + at], rates)
    for backward in range(2):
        for target in range(chips):
            wanted = layout.chip(target) * 2 + core
            for offset in range(chips):
                for sibling in range(2):
                    source = layout.chip(offset, sibling) * 2 + (core ^ sibling)
                    place = (source + 1) * count + wanted if backward else (wanted + 1) * count + source
                    distance = distances[place].astype(f32)
                    linked = (distance >= 0.0).astype(f32)
                    slot = ((backward * chips + target) * chips + offset) * 2 + sibling
                    table_ref[slot] = jnp.exp(rates * -distance) * linked


def local_head(layout, rate, query, key, value):
    tile, count = layout.tile, layout.count
    decays = decay_tiles(tile, rate, count, False)
    totals = [None] * count
    for i in range(count):
        for j in range(i + 1):
            w_span = slice(j * tile, (j + 1) * tile)
            scores = nt(query[i * tile:(i + 1) * tile], key[w_span])
            weighted = (scores * decays[i - j]).astype(bf16)
            add_to(totals, i, nn(weighted, value[w_span]))
    return jnp.concatenate(totals, axis=0)


def local_kernel(layout, places, length_ref, parent_ref, rate_ref, query_ref, key_ref, value_ref, out_ref, masked_ref, scaled_ref, table_ref, facts_ref, distances):
    length = length_ref[lax.axis_index("seg")]
    weight_table(layout, length_ref, parent_ref, rate_ref, distances, table_ref)
    heads, size = layout.heads, layout.size
    for place in range(heads):
        facts_ref[place:place + 1, :] = jnp.full((1, size), rate_ref[layout.head(place)], f32)
    facts_ref[heads:, :] = jnp.full((1, size), length.astype(f32), f32)
    masked_ref[...] = masked_rows(query_ref[...], length)
    for place in range(heads):
        span = layout.span(place)
        scale = query_scale(layout.rows, size, rate_ref[layout.head(place)])
        scaled_ref[:, span] = (masked_ref[:, span].astype(f32) * scale).astype(bf16)
    for place in places:
        span = layout.span(place)
        rate = rate_ref[layout.head(place)]
        out_ref[:, layout.near(places, place)] = local_head(layout, rate, masked_ref[:, span], key_ref[:, span], value_ref[:, span])


def tile_pairs(count):
    return [(i, j) for j in range(count) for i in range(j, count)]


def weighted_kernel(layout, places, facts_ref, query_ref, key_ref, value_ref, out_ref, local_ref, key_end_ref, value_end_ref):
    tile = layout.tile
    length = facts_ref[layout.heads:, :]
    for place in range(layout.heads):
        span = layout.span(place)
        scale = key_scale(layout.rows, layout.size, length, facts_ref[place:place + 1, :])
        key_end_ref[:, span] = (key_ref[:, span].astype(f32) * scale).astype(bf16)
        value_end_ref[:, span] = (value_ref[:, span].astype(f32) * scale).astype(bf16)
        rate = facts_ref[place:place + 1, :1]
        query, key = query_ref[:, span], key_ref[:, span]
        decays = decay_tiles(tile, rate, layout.count, True)
        for at, (i, j) in enumerate(tile_pairs(layout.count)):
            scores = nt(key[j * tile:(j + 1) * tile], query[i * tile:(i + 1) * tile])
            out_ref[place, at] = (scores * decays[i - j]).astype(bf16)
        if place in places:
            local_ref[:, layout.near(places, place)] = local_head(layout, rate, query, key, value_ref[:, span])


def mix_kernel(layout, backward, targets, table_ref, *rest):
    chips, size, piece = layout.chips, layout.size, layout.piece
    mine, other, outs = rest[:chips], rest[chips:2 * chips], rest[len(rest) - len(targets):]
    part = min(piece, size)
    for at in range(piece // part):
        span = slice(at * part, (at + 1) * part)
        totals = [None] * len(targets)
        for offset in range(chips):
            for sibling, sources in ((0, mine), (1, other)):
                data = sources[offset][span, :]
                for index, target in enumerate(targets):
                    slot = ((backward * chips + target) * chips + offset) * 2 + sibling
                    add_to(totals, index, table_ref[slot, at:at + 1, :] * data)
        for out, total in zip(outs, totals):
            out[span, :] = total


def attend_kernel(layout, places, last, scaled_ref, upstream_ref, gain_ref, local_ref, *rest):
    pieces, rest = rest[:layout.chips], rest[layout.chips:]
    rows, size = layout.rows, layout.size
    if last is None:
        attended_ref, squares_ref, inners_ref = rest
        squares = jnp.zeros((rows, size), f32)
        inners = jnp.zeros((rows, size), f32)
    else:
        *before, attended_ref, sums_ref = rest
        squares, inners = (before[0][...], before[1][...]) if before else (jnp.zeros((rows, size), f32),) * 2
    for chosen in layout.pairs(places):
        carried = block_diagonal([layout.state(pieces, place).astype(bf16) for place in chosen])
        both = nn(side_by_side([scaled_ref[:, layout.span(place)] for place in chosen]), carried)
        for at, place in enumerate(chosen):
            span, near = layout.span(place), layout.near(places, place)
            attended = local_ref[:, near] + both[:, at * size:(at + 1) * size]
            attended_ref[:, near] = attended
            scaled = upstream_ref[:, span].astype(f32) * gain_ref[:, span]
            squares = squares + attended * attended
            inners = inners + scaled * attended
    if last is None:
        squares_ref[...] = squares
        inners_ref[...] = inners
        return
    groups = rows // size
    for at in range(groups):
        span = slice(at * size, (at + 1) * size)
        sums_ref[at:at + 1, :] = jnp.sum(squares[span].T, axis=0, keepdims=True)
        sums_ref[groups + at:groups + at + 1, :] = jnp.sum(inners[span].T, axis=0, keepdims=True)


def norm_columns(sum_refs, width, inverse_ref, factor_ref):
    total = sum_refs[0][...]
    for ref in sum_refs[1:]:
        total = total + ref[...]
    groups = total.shape[0] // 2
    size = total.shape[1]
    inverse = lax.rsqrt(total[:groups] / width + norm_eps)
    factor = inverse * inverse * inverse * total[groups:] / width
    for at in range(groups):
        span = slice(at * size, (at + 1) * size)
        inverse_ref[span, :] = column(inverse[at:at + 1])
        factor_ref[span, :] = column(factor[at:at + 1])


def pick(layout, groups, refs, place, rows=slice(None)):
    for places, ref in zip(groups, refs):
        if place in places:
            return ref[rows, layout.near(places, place)]
    raise ValueError(place)


def state_grad_kernel(layout, groups, offsets, sums, width, scaled_ref, upstream_ref, gain_ref, *rest):
    attended_refs, rest = rest[:len(groups)], rest[len(groups):]
    if sums:
        sum_refs, rest = rest[:sums], rest[sums:]
        outs, (inverse_ref, factor_ref, whole) = rest[:len(offsets)], rest[len(offsets):]
        norm_columns(sum_refs, width, inverse_ref, factor_ref)
    else:
        inverse_ref, factor_ref, *outs, whole = rest
    inverse = inverse_ref[...]
    factor = factor_ref[...]

    def left(place):
        return scaled_ref[:, layout.span(place)]

    def right(place):
        span = layout.span(place)
        scaled = upstream_ref[:, span].astype(f32) * gain_ref[:, span]
        return (inverse * scaled - factor * pick(layout, groups, attended_refs, place)).astype(bf16)

    write_states(layout, offsets, left, right, outs, whole)


def send(layout, places, place, sources, targets, sems, copies):
    for source, target in zip(sources, targets):
        near = source.at[:, layout.near(places, place)]
        copies.append(pltpu.make_async_copy(near, target.at[:, layout.span(place)], sems.at[len(copies)]))
        copies[-1].start()


def send_all(layout, kept, earlier, targets, sems, copies):
    for at, places in enumerate(kept):
        for place in places:
            send(layout, places, place, earlier[2 * at:2 * at + 2], targets, sems, copies)


def backward_kernel(layout, groups, places, kept, last, facts_ref, query_ref, key_ref, value_ref, upstream_ref, weighted_ref, gain_ref, inverse_ref, factor_ref, *rest):
    attended_refs, rest = rest[:len(groups)], rest[len(groups):]
    pieces, rest = rest[:layout.chips], rest[layout.chips:]
    earlier, rest = rest[:2 * len(kept)], rest[2 * len(kept):]
    rows, size, tile, count = layout.rows, layout.size, layout.tile, layout.count
    copies = []
    if last:
        out_any, query_grad_any, key_grad_ref, value_grad_ref, out_ref, query_grad_ref, sems = rest
        targets = (out_any, query_grad_any)
        send_all(layout, kept, earlier, targets, sems, copies)
    else:
        out_ref, query_grad_ref, key_grad_ref, value_grad_ref, token_ref = rest
        token_ref[...] = jnp.zeros_like(token_ref)
    used = row_index(rows, size).astype(f32) < facts_ref[layout.heads:, :]
    for place in places:
        span, near = layout.span(place), layout.near(places, place)
        rate = facts_ref[place:place + 1, :]
        query = query_ref[:, span]
        key = key_ref[:, span]
        value = value_ref[:, span]
        gain = gain_ref[:, span]
        inverse = inverse_ref[...]
        attended = pick(layout, groups, attended_refs, place)
        out_ref[:, near] = (attended * inverse * gain).astype(bf16)
        scaled = upstream_ref[:, span].astype(f32) * gain
        grad = (inverse * scaled - factor_ref[...] * attended).astype(bf16)
        carried = layout.state(pieces, place).astype(bf16)
        query_grad = nt(grad, carried) * query_scale(rows, size, rate)
        decays = decay_tiles(tile, rate[:, :1], count, True)
        query_totals, key_totals, value_totals = [None] * count, [None] * count, [None] * count
        for at, (i, j) in enumerate(tile_pairs(count)):
            u_span, w_span = slice(i * tile, (i + 1) * tile), slice(j * tile, (j + 1) * tile)
            score_grad = (nt(value[w_span], grad[u_span]) * decays[i - j]).astype(bf16)
            add_to(value_totals, j, nn(weighted_ref[place, at], grad[u_span]))
            add_to(key_totals, j, nn(score_grad, query[u_span]))
            add_to(query_totals, i, tn(score_grad, key[w_span]))
        key_grad_ref[:, near] = jnp.concatenate(key_totals, axis=0).astype(bf16)
        value_grad_ref[:, near] = jnp.concatenate(value_totals, axis=0).astype(bf16)
        query_grad = query_grad + jnp.concatenate(query_totals, axis=0)
        query_grad_ref[:, near] = jnp.where(used, query_grad, 0.0).astype(bf16)
        if last:
            send(layout, places, place, (out_ref, query_grad_ref), targets, sems, copies)
    for copy in copies:
        copy.wait()


def finish_kernel(layout, groups, places, filled, key_end_ref, value_end_ref, *rest):
    key_locals, value_locals, rest = rest[:len(groups)], rest[len(groups):2 * len(groups)], rest[2 * len(groups):]
    pieces, rest = rest[:layout.chips], rest[layout.chips + filled:]
    key_any, value_any, key_grad_ref, value_grad_ref, sems = rest
    copies = []
    for place in places:
        span, near = layout.span(place), layout.near(places, place)
        state_grad = layout.state(pieces, place).astype(bf16)
        key_part = nt(value_end_ref[:, span], state_grad)
        value_part = nn(key_end_ref[:, span], state_grad)
        key_grad_ref[:, near] = (pick(layout, groups, key_locals, place).astype(f32) + key_part).astype(bf16)
        value_grad_ref[:, near] = (pick(layout, groups, value_locals, place).astype(f32) + value_part).astype(bf16)
        send(layout, places, place, (key_grad_ref, value_grad_ref), (key_any, value_any), sems, copies)
    for copy in copies:
        copy.wait()


def params(limit=VMEM_LIMIT):
    return pltpu.CompilerParams(vmem_limit_bytes=limit)


def shape(dims, dtype):
    return jax.ShapeDtypeStruct(dims, dtype)


def pass_on(piece_ref, before_ref, out_ref):
    pass


def after(piece, before):
    return pl.pallas_call(
        pass_on,
        out_shape=shape(piece.shape, piece.dtype),
        in_specs=[ANY_SPEC] * 2,
        out_specs=ANY_SPEC,
        input_output_aliases={0: 0},
        compiler_params=params(),
        name="after",
    )(piece, before)


def exchange(pieces, count):
    moved = [pieces[0]]
    for slot in range(1, len(pieces)):
        pairs = [(at, at ^ (2 * (core_offset(slot, at % 2) if False else slot))) for at in range(count)]
        moved.append(lax.ppermute(pieces[slot], "seg", pairs))
    return moved


def one_by_one(pieces, before, order):
    taken = list(pieces)
    for slot in order:
        taken[slot] = before = after(pieces[slot], before)
    return taken


def swap_cores(pieces, count):
    pairs = [(at, at ^ 1) for at in range(count)]
    return [lax.ppermute(piece, "seg", pairs) for piece in pieces]


def add_kernel(left_ref, right_ref, out_ref):
    out_ref[...] = left_ref[...] + right_ref[...]


def head_sums(sums, count):
    step = 1
    parts = [sums]
    while step < count:
        if len(parts) == 2:
            parts = [
                pl.pallas_call(
                    add_kernel,
                    out_shape=shape(sums.shape, sums.dtype),
                    in_specs=[VMEM_SPEC] * 2,
                    out_specs=VMEM_SPEC,
                    compiler_params=params(),
                    name="add_sums",
                )(*parts)
            ]
        parts.append(lax.ppermute(parts[0], "head", [(at, at ^ step) for at in range(count)]))
        step *= 2
    return parts


def local(seg_count, head_count, queries, key_tokens, values, upstream, norm_gain, decay_rate, block_length, parent):
    rows, wide = queries.shape
    heads = decay_rate.shape[0]
    size = wide // heads
    width = wide * head_count
    chips = seg_count // 2
    layout = Layout(rows, wide, size, chips)
    gain = norm_gain[None, :]
    piece_shape = shape((layout.piece, size), f32)
    whole = pltpu.VMEM((wide, size), f32)
    columns = shape((rows, size), f32)
    offsets = list(range(chips))
    sends = [[slot for slot in offsets if 0 < slot < 3], [slot for slot in offsets if slot == 0 or slot >= 3]]
    groups = [group for group in (layout.places(offsets[:2]), layout.places(offsets[2:])) if group]
    whole_sends = [sends[0] + sends[1]]
    early, late = groups if len(groups) == 2 else (groups[0], [])

    def near_shape(places, dtype):
        return shape((rows, len(places) * size), dtype)

    def near_scratch(places, dtype):
        return pltpu.VMEM((rows, len(places) * size), dtype)

    def in_order(parts):
        return [dict(zip(sends[0] + sends[1], parts))[offset] for offset in offsets]

    key_near, value_near = pl.pallas_call(
        near_kernel,
        out_shape=[shape((rows, wide), bf16)] * 2,
        in_specs=[ANY_SPEC] * 3,
        out_specs=[VMEM_SPEC] * 2,
        scratch_shapes=[pltpu.SemaphoreType.DMA((2,))],
        compiler_params=params(FIRST_LIMIT),
        name="bring_near",
    )(key_tokens, values, queries)

    states = []
    for chosen in whole_sends:
        states += pl.pallas_call(
            functools.partial(state_kernel, layout, chosen),
            out_shape=[piece_shape] * len(chosen),
            in_specs=[VMEM_SPEC] * 4,
            out_specs=[VMEM_SPEC] * len(chosen),
            scratch_shapes=[whole],
            compiler_params=params(),
            name="block_state",
        )(block_length[None, :], decay_rate[None, :], key_near, value_near)

    early_local, masked, scaled, table, facts = pl.pallas_call(
        functools.partial(local_kernel, layout, early),
        out_shape=[
            near_shape(early, f32),
            shape((rows, wide), bf16),
            shape((rows, wide), bf16),
            shape((4 * chips * chips, 8, size), f32),
            shape((heads + 1, size), f32),
        ],
        in_specs=[SMEM_SPEC] * 3 + [VMEM_SPEC] * 3,
        out_specs=[VMEM_SPEC] * 5,
        scratch_shapes=[pltpu.SMEM((seg_count * (seg_count + 1),), jnp.int32)],
        compiler_params=params(),
        cost_estimate=pl.CostEstimate(flops=2 * rows * rows * wide, bytes_accessed=10 * rows * wide, transcendentals=rows * rows * heads),
        name="local_attention",
    )(block_length, parent, decay_rate, queries, key_near, value_near)

    pairs = len(tile_pairs(layout.count))
    weighted, late_local, key_end, value_end = pl.pallas_call(
        functools.partial(weighted_kernel, layout, late),
        out_shape=[shape((heads, pairs, layout.tile, layout.tile), bf16), near_shape(late or [0], f32)] + [shape((rows, wide), bf16)] * 2,
        in_specs=[VMEM_SPEC] * 4,
        out_specs=[VMEM_SPEC] * 4,
        compiler_params=params(),
        cost_estimate=pl.CostEstimate(flops=4 * rows * rows * wide, bytes_accessed=10 * rows * wide, transcendentals=rows * rows * heads),
        name="weighted_scores",
    )(facts, masked, key_near, value_near)

    def mix(pieces, backward, before):
        mine = exchange(pieces, seg_count)
        mine = mine[:1] + [after(piece, before) for piece in mine[1:]]
        other = swap_cores(mine, seg_count)
        mixed = []
        for chosen in whole_sends:
            mixed += pl.pallas_call(
                functools.partial(mix_kernel, layout, backward, chosen),
                out_shape=[piece_shape] * len(chosen),
                in_specs=[VMEM_SPEC] * (1 + 2 * chips) + [ANY_SPEC] * len(mixed[:1]),
                out_specs=[VMEM_SPEC] * len(chosen),
                compiler_params=params(),
                cost_estimate=pl.CostEstimate(flops=rows * rows * wide, bytes_accessed=10 * rows * wide, transcendentals=0),
                name="mix_backward" if backward else "mix_forward",
            )(table, *mine, *other, *mixed[:1])
        return exchange(in_order(mixed), seg_count)

    def shown(pieces, places):
        if not layout.each:
            return pieces
        return [piece if offset * layout.each in places else pieces[0] for offset, piece in enumerate(pieces)]

    carried = mix(in_order(states), 0, table)

    attended, before = [], []
    for index, (places, local_out) in enumerate(zip(groups, (early_local, late_local))):
        last = True if index == len(groups) - 1 else None
        out_shape = [near_shape(places, f32)] + ([shape((2 * rows // size, size), f32)] if last else [columns] * 2)
        part, *before = pl.pallas_call(
            functools.partial(attend_kernel, layout, places, last),
            out_shape=out_shape,
            in_specs=[VMEM_SPEC] * (4 + chips + len(before)),
            out_specs=[VMEM_SPEC] * len(out_shape),
            compiler_params=params(),
            cost_estimate=pl.CostEstimate(flops=rows * rows * wide, bytes_accessed=10 * rows * wide, transcendentals=rows * wide),
            name="attend",
        )(scaled, upstream, gain, local_out, *shown(carried, places), *before)
        attended.append(part)
    sum_parts = head_sums(before[0], head_count)

    state_grads, norms = [], []
    for chosen in whole_sends:
        first = not norms
        parts = pl.pallas_call(
            functools.partial(state_grad_kernel, layout, groups, chosen, len(sum_parts) if first else 0, width),
            out_shape=[piece_shape] * len(chosen) + ([columns] * 2 if first else []),
            in_specs=[VMEM_SPEC] * (3 + len(groups) + (len(sum_parts) if first else 2)),
            out_specs=[VMEM_SPEC] * (len(chosen) + (2 if first else 0)),
            scratch_shapes=[whole],
            compiler_params=params(),
            name="state_grad",
        )(scaled, upstream, gain, *attended, *(sum_parts if first else norms))
        state_grads += parts[:len(chosen)]
        norms = norms or parts[len(chosen):]

    def ending(places, kept, last):
        if not last:
            return [near_shape(places, bf16)] * 2, [VMEM_SPEC] * 2, []
        amount = len(places) + sum(len(group) for group in kept)
        scratch = [near_scratch(places, bf16)] * 2 + [pltpu.SemaphoreType.DMA((2 * amount,))]
        return [shape((rows, wide), bf16)] * 2, [ANY_SPEC] * 2, scratch

    def backward(places, kept, earlier, last):
        out_shape, out_specs, scratch = ending(places, kept, last)
        out_shape = out_shape + [near_shape(places, bf16)] * 2 + ([] if last else [shape((8, size), f32)])
        return pl.pallas_call(
            functools.partial(backward_kernel, layout, groups, places, kept, last),
            out_shape=out_shape,
            in_specs=[VMEM_SPEC] * (9 + len(groups) + chips + len(earlier)),
            out_specs=out_specs + [VMEM_SPEC] * (len(out_shape) - 2),
            scratch_shapes=scratch,
            compiler_params=params(),
            cost_estimate=pl.CostEstimate(
                flops=8 * rows * rows * size * len(places),
                bytes_accessed=16 * rows * size * len(places),
                transcendentals=rows * rows * len(places),
            ),
            name="local_backward",
        )(facts, masked, key_near, value_near, upstream, weighted, gain, *norms, *attended, *carried, *earlier)

    cut = heads * 4 // 8 if heads > 2 else heads // 2
    halves = [list(range(cut)), list(range(cut, heads))]
    out_part, query_part, key_first, value_first, token = backward(halves[0], [], [], False)
    state_sums = mix(in_order(state_grads), 1, token)
    attention_out, query_grad, key_last, value_last = backward(halves[1], halves[:1], [out_part, query_part], True)

    grads = []
    for places in groups:
        inputs = 6 + chips
        grads = pl.pallas_call(
            functools.partial(finish_kernel, layout, halves, places, len(grads)),
            out_shape=[shape((rows, wide), bf16)] * 2,
            in_specs=[VMEM_SPEC] * inputs + [ANY_SPEC] * len(grads),
            out_specs=[ANY_SPEC] * 2,
            scratch_shapes=[near_scratch(places, bf16)] * 2 + [pltpu.SemaphoreType.DMA((2 * len(places),))],
            input_output_aliases={inputs + at: at for at in range(len(grads))},
            compiler_params=params(),
            cost_estimate=pl.CostEstimate(flops=rows * rows * wide, bytes_accessed=10 * rows * wide, transcendentals=rows * wide),
            name="finish",
        )(key_end, value_end, key_first, key_last, value_first, value_last, *shown(state_sums, places), *grads)
    return attention_out, query_grad, *grads


def solution(mesh):
    sizes = dict(mesh.shape)
    tokens = P("seg", "head")
    return jax.shard_map(
        functools.partial(local, sizes["seg"], sizes["head"]),
        mesh=mesh,
        in_specs=(tokens, tokens, tokens, tokens, P("head"), P("head"), P(), P()),
        out_specs=(tokens, tokens, tokens, tokens),
        check_vma=False,
    )
```

```python
import functools

import jax
import jax.numpy as jnp
from jax import lax
from jax.experimental import pallas as pl
from jax.experimental.pallas import tpu as pltpu
from jax.sharding import PartitionSpec as P

norm_eps = 1e-05
f32 = jnp.float32
bf16 = jnp.bfloat16
VMEM_LIMIT = 40 * 1024 * 1024
FIRST_LIMIT = 514 * 1024 * 1024 // 10

SMEM_SPEC = pl.BlockSpec(memory_space=pltpu.SMEM)
VMEM_SPEC = pl.BlockSpec(memory_space=pltpu.VMEM)
ANY_SPEC = pl.BlockSpec(memory_space=pl.ANY)


def nn(a, b):
    return lax.dot_general(a, b, (((1,), (0,)), ((), ())), preferred_element_type=f32)


def nt(a, b):
    return lax.dot_general(a, b, (((1,), (1,)), ((), ())), preferred_element_type=f32)


def tn(a, b):
    return lax.dot_general(a, b, (((0,), (0,)), ((), ())), preferred_element_type=f32)


def side_by_side(parts):
    return jnp.concatenate(parts, axis=1)


def block_diagonal(blocks):
    zero = jnp.zeros_like(blocks[0])
    return jnp.concatenate([side_by_side([block if i == j else zero for j in range(len(blocks))]) for i, block in enumerate(blocks)], axis=0)


def row_index(rows, columns):
    return lax.broadcasted_iota(jnp.int32, (rows, columns), 0)


def key_scale(rows, size, length, rate):
    slot = row_index(rows, size).astype(f32)
    remaining = (length - 1) - slot
    return jnp.where(remaining >= 0, jnp.exp(-rate * remaining), 0.0)


def query_scale(rows, size, rate):
    return jnp.exp(-rate * (row_index(rows, size) + 1).astype(f32))


def masked_rows(array, length):
    return jnp.where(row_index(*array.shape) < length, array, jnp.zeros_like(array))


def column(row):
    count = row.shape[1]
    return jnp.broadcast_to(row, (count, count)).T


def add_to(totals, index, part):
    totals[index] = part if totals[index] is None else totals[index] + part


def core_offset(slot, core, chips):
    crossed = slot ^ ((slot & 1) << 1) if chips >= 4 else slot
    return slot + core * (crossed - slot)


class Layout:
    def __init__(self, rows, wide, size, chips):
        self.rows, self.wide, self.size, self.chips = rows, wide, size, chips
        self.heads = wide // size
        self.piece = wide // chips
        self.each = self.piece // size
        self.tile = min(256, rows)
        self.count = rows // self.tile

    def chip(self, slot, sibling=0):
        own = lax.axis_index("seg")
        return (own // 2) ^ core_offset(slot, (own % 2) ^ sibling, self.chips)

    def head(self, place):
        if not self.each:
            return place
        return self.chip(place // self.each) * self.each + place % self.each

    def span(self, place):
        if not self.each:
            return pl.ds(place * self.size, self.size)
        return pl.ds(pl.multiple_of(self.head(place) * self.size, self.size), self.size)

    def near(self, places, place):
        at = list(places).index(place)
        return slice(at * self.size, (at + 1) * self.size)

    def places(self, offsets):
        if not self.each:
            return list(range(self.heads)) if 0 in offsets else []
        return [offset * self.each + at for offset in offsets for at in range(self.each)]

    def pairs(self, places):
        return [places[at:at + 2] for at in range(0, len(places), 2)]

    def state(self, pieces, place):
        if self.each:
            at = place % self.each
            return pieces[place // self.each][at * self.size:(at + 1) * self.size, :]
        first = place * self.size // self.piece
        parts = []
        for owner in range(first, first + self.size // self.piece):
            part = pieces[0][...]
            for offset in range(1, self.chips):
                part = jnp.where(self.chip(offset) == owner, pieces[offset][...], part)
            parts.append(part)
        return jnp.concatenate(parts, axis=0)


def near_kernel(key_any, value_any, query_any, key_ref, value_ref, sems):
    moves = ((key_any, key_ref), (value_any, value_ref))
    copies = [pltpu.make_async_copy(source, target, sems.at[at]) for at, (source, target) in enumerate(moves)]
    for copy in copies:
        copy.start()
    for copy in copies:
        copy.wait()


def write_states(layout, offsets, left, right, outs, whole):
    size = layout.size
    if layout.each:
        places = layout.places(offsets)
        targets = [(outs[place // size_of], place % size_of) for place, size_of in ((at, layout.each) for at in range(len(places)))]
    else:
        places = list(range(layout.heads))
        targets = [(whole, place) for place in places]
    group = min(2, len(places))
    for first in range(0, len(places), group):
        chosen = places[first:first + group]
        both = tn(
            jnp.concatenate([left(place) for place in chosen], axis=1),
            jnp.concatenate([right(place) for place in chosen], axis=1),
        )
        for at in range(len(chosen)):
            inner = slice(at * size, (at + 1) * size)
            target, row = targets[first + at]
            target[row * size:(row + 1) * size, :] = both[inner, inner]
    if not layout.each:
        for offset, out in zip(offsets, outs):
            begin = pl.multiple_of(layout.chip(offset) * layout.piece, layout.piece)
            out[...] = whole[pl.ds(begin, layout.piece), :]


def state_kernel(layout, offsets, length_ref, rate_ref, key_ref, value_ref, *rest):
    outs, whole = rest[:len(offsets)], rest[len(offsets)]
    rows, size = layout.rows, layout.size
    lengths = length_ref[...].astype(f32)
    mine = lax.broadcasted_iota(jnp.int32, lengths.shape, 1) == lax.axis_index("seg")
    length = jnp.sum(jnp.where(mine, lengths, 0.0), axis=1, keepdims=True)
    rates = rate_ref[...]
    lane = lax.broadcasted_iota(jnp.int32, rates.shape, 1)

    def left(place):
        return key_ref[:, layout.span(place)]

    def right(place):
        rate = jnp.sum(jnp.where(lane == layout.head(place), rates, 0.0), axis=1, keepdims=True)
        return (value_ref[:, layout.span(place)].astype(f32) * key_scale(rows, size, length, rate)).astype(bf16)

    write_states(layout, offsets, left, right, outs, whole)


def decay_tiles(tile, rate, count, transposed):
    u = lax.broadcasted_iota(jnp.int32, (tile, tile), 1 if transposed else 0)
    w = lax.broadcasted_iota(jnp.int32, (tile, tile), 0 if transposed else 1)
    base = jnp.exp((w - u).astype(f32) * rate)
    tiles = [jnp.where(u >= w, base, 0.0)]
    for gap in range(1, count):
        tiles.append(base * jnp.exp(jnp.full((1, tile), -(gap * tile), f32) * rate))
    return tiles


def tree_distances(length_ref, parent_ref, table, count):
    for at in range(count):
        table[at] = jnp.int32(-1)

    def one(block, carry):
        above = parent_ref[block]
        passed = length_ref[jnp.maximum(above, 0)]
        for at in range(count):
            distance = table[(above + 1) * count + at]
            distance = jnp.where(distance >= 0, distance + passed, distance)
            table[(block + 1) * count + at] = jnp.where(above == at, 0, distance)
        return carry

    lax.fori_loop(0, count, one, 0)


def weight_table(layout, length_ref, parent_ref, rate_ref, distances, table_ref):
    own = lax.axis_index("seg")
    chip, core = own // 2, own % 2
    chips, size, piece = layout.chips, layout.size, layout.piece
    count = 2 * chips
    tree_distances(length_ref, parent_ref, distances, count)
    row = row_index(8, size)
    rates = jnp.full((8, size), rate_ref[(chip * piece) // size], f32)
    for at in range(1, piece // size):
        rates = jnp.where(row == at, rate_ref[(chip * piece) // size + at], rates)
    for backward in range(2):
        for target in range(chips):
            wanted = layout.chip(target) * 2 + core
            for offset in range(chips):
                for sibling in range(2):
                    source = layout.chip(offset, sibling) * 2 + (core ^ sibling)
                    place = (source + 1) * count + wanted if backward else (wanted + 1) * count + source
                    distance = distances[place].astype(f32)
                    linked = (distance >= 0.0).astype(f32)
                    slot = ((backward * chips + target) * chips + offset) * 2 + sibling
                    table_ref[slot] = jnp.exp(rates * -distance) * linked


def local_head(layout, rate, query, key, value):
    tile, count = layout.tile, layout.count
    decays = decay_tiles(tile, rate, count, False)
    totals = [None] * count
    for i in range(count):
        for j in range(i + 1):
            w_span = slice(j * tile, (j + 1) * tile)
            scores = nt(query[i * tile:(i + 1) * tile], key[w_span])
            weighted = (scores * decays[i - j]).astype(bf16)
            add_to(totals, i, nn(weighted, value[w_span]))
    return jnp.concatenate(totals, axis=0)


def local_kernel(layout, places, length_ref, parent_ref, rate_ref, query_ref, key_ref, value_ref, out_ref, masked_ref, scaled_ref, table_ref, facts_ref, distances):
    length = length_ref[lax.axis_index("seg")]
    weight_table(layout, length_ref, parent_ref, rate_ref, distances, table_ref)
    heads, size = layout.heads, layout.size
    for place in range(heads):
        facts_ref[place:place + 1, :] = jnp.full((1, size), rate_ref[layout.head(place)], f32)
    facts_ref[heads:, :] = jnp.full((1, size), length.astype(f32), f32)
    masked_ref[...] = masked_rows(query_ref[...], length)
    for place in range(heads):
        span = layout.span(place)
        scale = query_scale(layout.rows, size, rate_ref[layout.head(place)])
        scaled_ref[:, span] = (masked_ref[:, span].astype(f32) * scale).astype(bf16)
    for place in places:
        span = layout.span(place)
        rate = rate_ref[layout.head(place)]
        out_ref[:, layout.near(places, place)] = local_head(layout, rate, masked_ref[:, span], key_ref[:, span], value_ref[:, span])


def tile_pairs(count):
    return [(i, j) for j in range(count) for i in range(j, count)]


def weighted_kernel(layout, places, facts_ref, query_ref, key_ref, value_ref, out_ref, local_ref, key_end_ref, value_end_ref):
    tile = layout.tile
    length = facts_ref[layout.heads:, :]
    for place in range(layout.heads):
        span = layout.span(place)
        scale = key_scale(layout.rows, layout.size, length, facts_ref[place:place + 1, :])
        key_end_ref[:, span] = (key_ref[:, span].astype(f32) * scale).astype(bf16)
        value_end_ref[:, span] = (value_ref[:, span].astype(f32) * scale).astype(bf16)
        rate = facts_ref[place:place + 1, :1]
        query, key = query_ref[:, span], key_ref[:, span]
        decays = decay_tiles(tile, rate, layout.count, True)
        for at, (i, j) in enumerate(tile_pairs(layout.count)):
            scores = nt(key[j * tile:(j + 1) * tile], query[i * tile:(i + 1) * tile])
            out_ref[place, at] = (scores * decays[i - j]).astype(bf16)
        if place in places:
            local_ref[:, layout.near(places, place)] = local_head(layout, rate, query, key, value_ref[:, span])


def mix_kernel(layout, backward, targets, table_ref, *rest):
    chips, size, piece = layout.chips, layout.size, layout.piece
    mine, other, outs = rest[:chips], rest[chips:2 * chips], rest[len(rest) - len(targets):]
    part = min(piece, size)
    for at in range(piece // part):
        span = slice(at * part, (at + 1) * part)
        totals = [None] * len(targets)
        for offset in range(chips):
            for sibling, sources in ((0, mine), (1, other)):
                data = sources[offset][span, :]
                for index, target in enumerate(targets):
                    slot = ((backward * chips + target) * chips + offset) * 2 + sibling
                    add_to(totals, index, table_ref[slot, at:at + 1, :] * data)
        for out, total in zip(outs, totals):
            out[span, :] = total


def attend_kernel(layout, places, last, scaled_ref, upstream_ref, gain_ref, local_ref, *rest):
    pieces, rest = rest[:layout.chips], rest[layout.chips:]
    rows, size = layout.rows, layout.size
    if last is None:
        attended_ref, squares_ref, inners_ref = rest
        squares = jnp.zeros((rows, size), f32)
        inners = jnp.zeros((rows, size), f32)
    else:
        *before, attended_ref, sums_ref = rest
        squares, inners = (before[0][...], before[1][...]) if before else (jnp.zeros((rows, size), f32),) * 2
    for chosen in layout.pairs(places):
        carried = block_diagonal([layout.state(pieces, place).astype(bf16) for place in chosen])
        both = nn(side_by_side([scaled_ref[:, layout.span(place)] for place in chosen]), carried)
        for at, place in enumerate(chosen):
            span, near = layout.span(place), layout.near(places, place)
            attended = local_ref[:, near] + both[:, at * size:(at + 1) * size]
            attended_ref[:, near] = attended
            scaled = upstream_ref[:, span].astype(f32) * gain_ref[:, span]
            squares = squares + attended * attended
            inners = inners + scaled * attended
    if last is None:
        squares_ref[...] = squares
        inners_ref[...] = inners
        return
    groups = rows // size
    for at in range(groups):
        span = slice(at * size, (at + 1) * size)
        sums_ref[at:at + 1, :] = jnp.sum(squares[span].T, axis=0, keepdims=True)
        sums_ref[groups + at:groups + at + 1, :] = jnp.sum(inners[span].T, axis=0, keepdims=True)


def norm_columns(sum_refs, width, inverse_ref, factor_ref):
    total = sum_refs[0][...]
    for ref in sum_refs[1:]:
        total = total + ref[...]
    groups = total.shape[0] // 2
    size = total.shape[1]
    inverse = lax.rsqrt(total[:groups] / width + norm_eps)
    factor = inverse * inverse * inverse * total[groups:] / width
    for at in range(groups):
        span = slice(at * size, (at + 1) * size)
        inverse_ref[span, :] = column(inverse[at:at + 1])
        factor_ref[span, :] = column(factor[at:at + 1])


def pick(layout, groups, refs, place, rows=slice(None)):
    for places, ref in zip(groups, refs):
        if place in places:
            return ref[rows, layout.near(places, place)]
    raise ValueError(place)


def state_grad_kernel(layout, groups, offsets, sums, width, scaled_ref, upstream_ref, gain_ref, *rest):
    attended_refs, rest = rest[:len(groups)], rest[len(groups):]
    if sums:
        sum_refs, rest = rest[:sums], rest[sums:]
        outs, (inverse_ref, factor_ref, whole) = rest[:len(offsets)], rest[len(offsets):]
        norm_columns(sum_refs, width, inverse_ref, factor_ref)
    else:
        inverse_ref, factor_ref, *outs, whole = rest
    inverse = inverse_ref[...]
    factor = factor_ref[...]

    def left(place):
        return scaled_ref[:, layout.span(place)]

    def right(place):
        span = layout.span(place)
        scaled = upstream_ref[:, span].astype(f32) * gain_ref[:, span]
        return (inverse * scaled - factor * pick(layout, groups, attended_refs, place)).astype(bf16)

    write_states(layout, offsets, left, right, outs, whole)


def send(layout, places, place, sources, targets, sems, copies):
    for source, target in zip(sources, targets):
        near = source.at[:, layout.near(places, place)]
        copies.append(pltpu.make_async_copy(near, target.at[:, layout.span(place)], sems.at[len(copies)]))
        copies[-1].start()


def send_all(layout, kept, earlier, targets, sems, copies):
    for at, places in enumerate(kept):
        for place in places:
            send(layout, places, place, earlier[2 * at:2 * at + 2], targets, sems, copies)


def backward_kernel(layout, groups, places, kept, last, facts_ref, query_ref, key_ref, value_ref, upstream_ref, weighted_ref, gain_ref, inverse_ref, factor_ref, *rest):
    attended_refs, rest = rest[:len(groups)], rest[len(groups):]
    pieces, rest = rest[:layout.chips], rest[layout.chips:]
    earlier, rest = rest[:2 * len(kept)], rest[2 * len(kept):]
    rows, size, tile, count = layout.rows, layout.size, layout.tile, layout.count
    copies = []
    if last:
        out_any, query_grad_any, key_grad_ref, value_grad_ref, out_ref, query_grad_ref, sems = rest
        targets = (out_any, query_grad_any)
        send_all(layout, kept, earlier, targets, sems, copies)
    else:
        out_ref, query_grad_ref, key_grad_ref, value_grad_ref, token_ref = rest
        token_ref[...] = jnp.zeros_like(token_ref)
    used = row_index(rows, size).astype(f32) < facts_ref[layout.heads:, :]
    for place in places:
        span, near = layout.span(place), layout.near(places, place)
        rate = facts_ref[place:place + 1, :]
        query = query_ref[:, span]
        key = key_ref[:, span]
        value = value_ref[:, span]
        gain = gain_ref[:, span]
        inverse = inverse_ref[...]
        attended = pick(layout, groups, attended_refs, place)
        out_ref[:, near] = (attended * inverse * gain).astype(bf16)
        scaled = upstream_ref[:, span].astype(f32) * gain
        grad = (inverse * scaled - factor_ref[...] * attended).astype(bf16)
        carried = layout.state(pieces, place).astype(bf16)
        query_grad = nt(grad, carried) * query_scale(rows, size, rate)
        decays = decay_tiles(tile, rate[:, :1], count, True)
        query_totals, key_totals, value_totals = [None] * count, [None] * count, [None] * count
        for at, (i, j) in enumerate(tile_pairs(count)):
            u_span, w_span = slice(i * tile, (i + 1) * tile), slice(j * tile, (j + 1) * tile)
            score_grad = (nt(value[w_span], grad[u_span]) * decays[i - j]).astype(bf16)
            add_to(value_totals, j, nn(weighted_ref[place, at], grad[u_span]))
            add_to(key_totals, j, nn(score_grad, query[u_span]))
            add_to(query_totals, i, tn(score_grad, key[w_span]))
        key_grad_ref[:, near] = jnp.concatenate(key_totals, axis=0).astype(bf16)
        value_grad_ref[:, near] = jnp.concatenate(value_totals, axis=0).astype(bf16)
        query_grad = query_grad + jnp.concatenate(query_totals, axis=0)
        query_grad_ref[:, near] = jnp.where(used, query_grad, 0.0).astype(bf16)
        if last:
            send(layout, places, place, (out_ref, query_grad_ref), targets, sems, copies)
    for copy in copies:
        copy.wait()


def finish_kernel(layout, groups, places, filled, key_end_ref, value_end_ref, *rest):
    key_locals, value_locals, rest = rest[:len(groups)], rest[len(groups):2 * len(groups)], rest[2 * len(groups):]
    pieces, rest = rest[:layout.chips], rest[layout.chips + filled:]
    key_any, value_any, key_grad_ref, value_grad_ref, sems = rest
    copies = []
    for place in places:
        span, near = layout.span(place), layout.near(places, place)
        state_grad = layout.state(pieces, place).astype(bf16)
        key_part = nt(value_end_ref[:, span], state_grad)
        value_part = nn(key_end_ref[:, span], state_grad)
        key_grad_ref[:, near] = (pick(layout, groups, key_locals, place).astype(f32) + key_part).astype(bf16)
        value_grad_ref[:, near] = (pick(layout, groups, value_locals, place).astype(f32) + value_part).astype(bf16)
        send(layout, places, place, (key_grad_ref, value_grad_ref), (key_any, value_any), sems, copies)
    for copy in copies:
        copy.wait()


def params(limit=VMEM_LIMIT):
    return pltpu.CompilerParams(vmem_limit_bytes=limit)


def shape(dims, dtype):
    return jax.ShapeDtypeStruct(dims, dtype)


def pass_on(piece_ref, before_ref, out_ref):
    pass


def after(piece, before):
    return pl.pallas_call(
        pass_on,
        out_shape=shape(piece.shape, piece.dtype),
        in_specs=[ANY_SPEC] * 2,
        out_specs=ANY_SPEC,
        input_output_aliases={0: 0},
        compiler_params=params(),
        name="after",
    )(piece, before)


def exchange(pieces, count):
    moved = [pieces[0]]
    for slot in range(1, len(pieces)):
        pairs = [(at, at ^ (2 * core_offset(slot, at % 2, len(pieces)))) for at in range(count)]
        moved.append(lax.ppermute(pieces[slot], "seg", pairs))
    return moved


def one_by_one(pieces, before, order):
    taken = list(pieces)
    for slot in order:
        taken[slot] = before = after(pieces[slot], before)
    return taken


def swap_cores(pieces, count):
    pairs = [(at, at ^ 1) for at in range(count)]
    return [lax.ppermute(piece, "seg", pairs) for piece in pieces]


def add_kernel(left_ref, right_ref, out_ref):
    out_ref[...] = left_ref[...] + right_ref[...]


def head_sums(sums, count):
    step = 1
    parts = [sums]
    while step < count:
        if len(parts) == 2:
            parts = [
                pl.pallas_call(
                    add_kernel,
                    out_shape=shape(sums.shape, sums.dtype),
                    in_specs=[VMEM_SPEC] * 2,
                    out_specs=VMEM_SPEC,
                    compiler_params=params(),
                    name="add_sums",
                )(*parts)
            ]
        parts.append(lax.ppermute(parts[0], "head", [(at, at ^ step) for at in range(count)]))
        step *= 2
    return parts


def local(seg_count, head_count, queries, key_tokens, values, upstream, norm_gain, decay_rate, block_length, parent):
    rows, wide = queries.shape
    heads = decay_rate.shape[0]
    size = wide // heads
    width = wide * head_count
    chips = seg_count // 2
    layout = Layout(rows, wide, size, chips)
    gain = norm_gain[None, :]
    piece_shape = shape((layout.piece, size), f32)
    whole = pltpu.VMEM((wide, size), f32)
    columns = shape((rows, size), f32)
    offsets = list(range(chips))
    order = [slot for slot in offsets if 0 < slot < 3] + [slot for slot in offsets if slot == 0 or slot >= 3]
    groups = [group for group in (layout.places(offsets[:2]), layout.places(offsets[2:])) if group]
    early, late = groups if len(groups) == 2 else (groups[0], [])

    def in_order(parts):
        return [dict(zip(order, parts))[slot] for slot in offsets]

    def near_shape(places, dtype):
        return shape((rows, len(places) * size), dtype)

    def near_scratch(places, dtype):
        return pltpu.VMEM((rows, len(places) * size), dtype)

    key_near, value_near = pl.pallas_call(
        near_kernel,
        out_shape=[shape((rows, wide), bf16)] * 2,
        in_specs=[ANY_SPEC] * 3,
        out_specs=[VMEM_SPEC] * 2,
        scratch_shapes=[pltpu.SemaphoreType.DMA((2,))],
        compiler_params=params(FIRST_LIMIT),
        name="bring_near",
    )(key_tokens, values, queries)

    states = []
    for chosen in [order]:
        states += pl.pallas_call(
            functools.partial(state_kernel, layout, chosen),
            out_shape=[piece_shape] * len(chosen),
            in_specs=[VMEM_SPEC] * 4,
            out_specs=[VMEM_SPEC] * len(chosen),
            scratch_shapes=[whole],
            compiler_params=params(),
            name="block_state",
        )(block_length[None, :], decay_rate[None, :], key_near, value_near)

    early_local, masked, scaled, table, facts = pl.pallas_call(
        functools.partial(local_kernel, layout, early),
        out_shape=[
            near_shape(early, f32),
            shape((rows, wide), bf16),
            shape((rows, wide), bf16),
            shape((4 * chips * chips, 8, size), f32),
            shape((heads + 1, size), f32),
        ],
        in_specs=[SMEM_SPEC] * 3 + [VMEM_SPEC] * 3,
        out_specs=[VMEM_SPEC] * 5,
        scratch_shapes=[pltpu.SMEM((seg_count * (seg_count + 1),), jnp.int32)],
        compiler_params=params(),
        cost_estimate=pl.CostEstimate(flops=2 * rows * rows * wide, bytes_accessed=10 * rows * wide, transcendentals=rows * rows * heads),
        name="local_attention",
    )(block_length, parent, decay_rate, queries, key_near, value_near)

    pairs = len(tile_pairs(layout.count))
    weighted, late_local, key_end, value_end = pl.pallas_call(
        functools.partial(weighted_kernel, layout, late),
        out_shape=[shape((heads, pairs, layout.tile, layout.tile), bf16), near_shape(late or [0], f32)] + [shape((rows, wide), bf16)] * 2,
        in_specs=[VMEM_SPEC] * 4,
        out_specs=[VMEM_SPEC] * 4,
        compiler_params=params(),
        cost_estimate=pl.CostEstimate(flops=4 * rows * rows * wide, bytes_accessed=10 * rows * wide, transcendentals=rows * rows * heads),
        name="weighted_scores",
    )(facts, masked, key_near, value_near)

    def mix(pieces, backward, before):
        mine = exchange(pieces, seg_count)
        mine = mine[:1] + [after(piece, before) for piece in mine[1:]]
        other = swap_cores(mine, seg_count)
        mixed = []
        for chosen in [order]:
            mixed += pl.pallas_call(
                functools.partial(mix_kernel, layout, backward, chosen),
                out_shape=[piece_shape] * len(chosen),
                in_specs=[VMEM_SPEC] * (1 + 2 * chips) + [ANY_SPEC] * len(mixed[:1]),
                out_specs=[VMEM_SPEC] * len(chosen),
                compiler_params=params(),
                cost_estimate=pl.CostEstimate(flops=rows * rows * wide, bytes_accessed=10 * rows * wide, transcendentals=0),
                name="mix_backward" if backward else "mix_forward",
            )(table, *mine, *other, *mixed[:1])
        return exchange(in_order(mixed), seg_count)

    def shown(pieces, places):
        if not layout.each:
            return pieces
        return [piece if offset * layout.each in places else pieces[0] for offset, piece in enumerate(pieces)]

    carried = mix(in_order(states), 0, table)

    attended, before = [], []
    for index, (places, local_out) in enumerate(zip(groups, (early_local, late_local))):
        last = True if index == len(groups) - 1 else None
        out_shape = [near_shape(places, f32)] + ([shape((2 * rows // size, size), f32)] if last else [columns] * 2)
        part, *before = pl.pallas_call(
            functools.partial(attend_kernel, layout, places, last),
            out_shape=out_shape,
            in_specs=[VMEM_SPEC] * (4 + chips + len(before)),
            out_specs=[VMEM_SPEC] * len(out_shape),
            compiler_params=params(),
            cost_estimate=pl.CostEstimate(flops=rows * rows * wide, bytes_accessed=10 * rows * wide, transcendentals=rows * wide),
            name="attend",
        )(scaled, upstream, gain, local_out, *shown(carried, places), *before)
        attended.append(part)
    sum_parts = head_sums(before[0], head_count)

    state_grads, norms = [], []
    for chosen in [order]:
        first = not norms
        parts = pl.pallas_call(
            functools.partial(state_grad_kernel, layout, groups, chosen, len(sum_parts) if first else 0, width),
            out_shape=[piece_shape] * len(chosen) + ([columns] * 2 if first else []),
            in_specs=[VMEM_SPEC] * (3 + len(groups) + (len(sum_parts) if first else 2)),
            out_specs=[VMEM_SPEC] * (len(chosen) + (2 if first else 0)),
            scratch_shapes=[whole],
            compiler_params=params(),
            name="state_grad",
        )(scaled, upstream, gain, *attended, *(sum_parts if first else norms))
        state_grads += parts[:len(chosen)]
        norms = norms or parts[len(chosen):]

    def ending(places, kept, last):
        if not last:
            return [near_shape(places, bf16)] * 2, [VMEM_SPEC] * 2, []
        amount = len(places) + sum(len(group) for group in kept)
        scratch = [near_scratch(places, bf16)] * 2 + [pltpu.SemaphoreType.DMA((2 * amount,))]
        return [shape((rows, wide), bf16)] * 2, [ANY_SPEC] * 2, scratch

    def backward(places, kept, earlier, last):
        out_shape, out_specs, scratch = ending(places, kept, last)
        out_shape = out_shape + [near_shape(places, bf16)] * 2 + ([] if last else [shape((8, size), f32)])
        return pl.pallas_call(
            functools.partial(backward_kernel, layout, groups, places, kept, last),
            out_shape=out_shape,
            in_specs=[VMEM_SPEC] * (9 + len(groups) + chips + len(earlier)),
            out_specs=out_specs + [VMEM_SPEC] * (len(out_shape) - 2),
            scratch_shapes=scratch,
            compiler_params=params(),
            cost_estimate=pl.CostEstimate(
                flops=8 * rows * rows * size * len(places),
                bytes_accessed=16 * rows * size * len(places),
                transcendentals=rows * rows * len(places),
            ),
            name="local_backward",
        )(facts, masked, key_near, value_near, upstream, weighted, gain, *norms, *attended, *carried, *earlier)

    cut = heads * 4 // 8 if heads > 2 else heads // 2
    halves = [list(range(cut)), list(range(cut, heads))]
    out_part, query_part, key_first, value_first, token = backward(halves[0], [], [], False)
    state_sums = mix(in_order(state_grads), 1, token)
    attention_out, query_grad, key_last, value_last = backward(halves[1], halves[:1], [out_part, query_part], True)

    grads = []
    for places in groups:
        inputs = 6 + chips
        grads = pl.pallas_call(
            functools.partial(finish_kernel, layout, halves, places, len(grads)),
            out_shape=[shape((rows, wide), bf16)] * 2,
            in_specs=[VMEM_SPEC] * inputs + [ANY_SPEC] * len(grads),
            out_specs=[ANY_SPEC] * 2,
            scratch_shapes=[near_scratch(places, bf16)] * 2 + [pltpu.SemaphoreType.DMA((2 * len(places),))],
            input_output_aliases={inputs + at: at for at in range(len(grads))},
            compiler_params=params(),
            cost_estimate=pl.CostEstimate(flops=rows * rows * wide, bytes_accessed=10 * rows * wide, transcendentals=rows * wide),
            name="finish",
        )(key_end, value_end, key_first, key_last, value_first, value_last, *shown(state_sums, places), *grads)
    return attention_out, query_grad, *grads


def solution(mesh):
    sizes = dict(mesh.shape)
    tokens = P("seg", "head")
    return jax.shard_map(
        functools.partial(local, sizes["seg"], sizes["head"]),
        mesh=mesh,
        in_specs=(tokens, tokens, tokens, tokens, P("head"), P("head"), P(), P()),
        out_specs=(tokens, tokens, tokens, tokens),
        check_vma=False,
    )
```

```python
import functools

import jax
import jax.numpy as jnp
from jax import lax
from jax.experimental import pallas as pl
from jax.experimental.pallas import tpu as pltpu
from jax.sharding import PartitionSpec as P

norm_eps = 1e-05
f32 = jnp.float32
bf16 = jnp.bfloat16
VMEM_LIMIT = 40 * 1024 * 1024
FIRST_LIMIT = 514 * 1024 * 1024 // 10

SMEM_SPEC = pl.BlockSpec(memory_space=pltpu.SMEM)
VMEM_SPEC = pl.BlockSpec(memory_space=pltpu.VMEM)
ANY_SPEC = pl.BlockSpec(memory_space=pl.ANY)


def nn(a, b):
    return lax.dot_general(a, b, (((1,), (0,)), ((), ())), preferred_element_type=f32)


def nt(a, b):
    return lax.dot_general(a, b, (((1,), (1,)), ((), ())), preferred_element_type=f32)


def tn(a, b):
    return lax.dot_general(a, b, (((0,), (0,)), ((), ())), preferred_element_type=f32)


def side_by_side(parts):
    return jnp.concatenate(parts, axis=1)


def block_diagonal(blocks):
    zero = jnp.zeros_like(blocks[0])
    return jnp.concatenate([side_by_side([block if i == j else zero for j in range(len(blocks))]) for i, block in enumerate(blocks)], axis=0)


def row_index(rows, columns):
    return lax.broadcasted_iota(jnp.int32, (rows, columns), 0)


def key_scale(rows, size, length, rate):
    slot = row_index(rows, size).astype(f32)
    remaining = (length - 1) - slot
    return jnp.where(remaining >= 0, jnp.exp(-rate * remaining), 0.0)


def query_scale(rows, size, rate):
    return jnp.exp(-rate * (row_index(rows, size) + 1).astype(f32))


def masked_rows(array, length):
    return jnp.where(row_index(*array.shape) < length, array, jnp.zeros_like(array))


def column(row):
    count = row.shape[1]
    return jnp.broadcast_to(row, (count, count)).T


def add_to(totals, index, part):
    totals[index] = part if totals[index] is None else totals[index] + part


def core_offset(slot, core):
    crossed = (slot & ~3) | ((slot & 1) << 1) | ((slot & 2) >> 1)
    return slot + core * (crossed - slot)


class Layout:
    def __init__(self, rows, wide, size, chips):
        self.rows, self.wide, self.size, self.chips = rows, wide, size, chips
        self.heads = wide // size
        self.piece = wide // chips
        self.each = self.piece // size
        self.tile = min(256, rows)
        self.count = rows // self.tile

    def chip(self, slot, sibling=0):
        own = lax.axis_index("seg")
        crossing = False
        return (own // 2) ^ (core_offset(slot, (own % 2) ^ sibling) if crossing else slot)

    def head(self, place):
        if not self.each:
            return place
        return self.chip(place // self.each) * self.each + place % self.each

    def span(self, place):
        if not self.each:
            return pl.ds(place * self.size, self.size)
        return pl.ds(pl.multiple_of(self.head(place) * self.size, self.size), self.size)

    def near(self, places, place):
        at = list(places).index(place)
        return slice(at * self.size, (at + 1) * self.size)

    def places(self, offsets):
        if not self.each:
            return list(range(self.heads)) if 0 in offsets else []
        return [offset * self.each + at for offset in offsets for at in range(self.each)]

    def pairs(self, places):
        return [places[at:at + 2] for at in range(0, len(places), 2)]

    def state(self, pieces, place):
        if self.each:
            at = place % self.each
            return pieces[place // self.each][at * self.size:(at + 1) * self.size, :]
        first = place * self.size // self.piece
        parts = []
        for owner in range(first, first + self.size // self.piece):
            part = pieces[0][...]
            for offset in range(1, self.chips):
                part = jnp.where(self.chip(offset) == owner, pieces[offset][...], part)
            parts.append(part)
        return jnp.concatenate(parts, axis=0)


def near_kernel(key_any, value_any, query_any, key_ref, value_ref, sems):
    moves = ((key_any, key_ref), (value_any, value_ref))
    copies = [pltpu.make_async_copy(source, target, sems.at[at]) for at, (source, target) in enumerate(moves)]
    for copy in copies:
        copy.start()
    for copy in copies:
        copy.wait()


def write_states(layout, offsets, left, right, outs, whole):
    size = layout.size
    if layout.each:
        places = layout.places(offsets)
        targets = [(outs[place // size_of], place % size_of) for place, size_of in ((at, layout.each) for at in range(len(places)))]
    else:
        places = list(range(layout.heads))
        targets = [(whole, place) for place in places]
    group = min(2, len(places))
    for first in range(0, len(places), group):
        chosen = places[first:first + group]
        both = tn(
            jnp.concatenate([left(place) for place in chosen], axis=1),
            jnp.concatenate([right(place) for place in chosen], axis=1),
        )
        for at in range(len(chosen)):
            inner = slice(at * size, (at + 1) * size)
            target, row = targets[first + at]
            target[row * size:(row + 1) * size, :] = both[inner, inner]
    if not layout.each:
        for offset, out in zip(offsets, outs):
            begin = pl.multiple_of(layout.chip(offset) * layout.piece, layout.piece)
            out[...] = whole[pl.ds(begin, layout.piece), :]


def state_kernel(layout, offsets, length_ref, rate_ref, key_ref, value_ref, *rest):
    outs, whole = rest[:len(offsets)], rest[len(offsets)]
    rows, size = layout.rows, layout.size
    lengths = length_ref[...].astype(f32)
    mine = lax.broadcasted_iota(jnp.int32, lengths.shape, 1) == lax.axis_index("seg")
    length = jnp.sum(jnp.where(mine, lengths, 0.0), axis=1, keepdims=True)
    rates = rate_ref[...]
    lane = lax.broadcasted_iota(jnp.int32, rates.shape, 1)

    def left(place):
        return key_ref[:, layout.span(place)]

    def right(place):
        rate = jnp.sum(jnp.where(lane == layout.head(place), rates, 0.0), axis=1, keepdims=True)
        return (value_ref[:, layout.span(place)].astype(f32) * key_scale(rows, size, length, rate)).astype(bf16)

    write_states(layout, offsets, left, right, outs, whole)


def decay_tiles(tile, rate, count, transposed):
    u = lax.broadcasted_iota(jnp.int32, (tile, tile), 1 if transposed else 0)
    w = lax.broadcasted_iota(jnp.int32, (tile, tile), 0 if transposed else 1)
    base = jnp.exp((w - u).astype(f32) * rate)
    tiles = [jnp.where(u >= w, base, 0.0)]
    for gap in range(1, count):
        tiles.append(base * jnp.exp(jnp.full((1, tile), -(gap * tile), f32) * rate))
    return tiles


def tree_distances(length_ref, parent_ref, table, count):
    for at in range(count):
        table[at] = jnp.int32(-1)

    def one(block, carry):
        above = parent_ref[block]
        passed = length_ref[jnp.maximum(above, 0)]
        for at in range(count):
            distance = table[(above + 1) * count + at]
            distance = jnp.where(distance >= 0, distance + passed, distance)
            table[(block + 1) * count + at] = jnp.where(above == at, 0, distance)
        return carry

    lax.fori_loop(0, count, one, 0)


def weight_table(layout, length_ref, parent_ref, rate_ref, distances, table_ref):
    own = lax.axis_index("seg")
    chip, core = own // 2, own % 2
    chips, size, piece = layout.chips, layout.size, layout.piece
    count = 2 * chips
    tree_distances(length_ref, parent_ref, distances, count)
    row = row_index(8, size)
    rates = jnp.full((8, size), rate_ref[(chip * piece) // size], f32)
    for at in range(1, piece // size):
        rates = jnp.where(row == at, rate_ref[(chip * piece) // size + at], rates)
    for backward in range(2):
        for target in range(chips):
            wanted = layout.chip(target) * 2 + core
            for offset in range(chips):
                for sibling in range(2):
                    source = layout.chip(offset, sibling) * 2 + (core ^ sibling)
                    place = (source + 1) * count + wanted if backward else (wanted + 1) * count + source
                    distance = distances[place].astype(f32)
                    linked = (distance >= 0.0).astype(f32)
                    slot = ((backward * chips + target) * chips + offset) * 2 + sibling
                    table_ref[slot] = jnp.exp(rates * -distance) * linked


def local_head(layout, rate, query, key, value):
    tile, count = layout.tile, layout.count
    decays = decay_tiles(tile, rate, count, False)
    totals = [None] * count
    for i in range(count):
        for j in range(i + 1):
            w_span = slice(j * tile, (j + 1) * tile)
            scores = nt(query[i * tile:(i + 1) * tile], key[w_span])
            weighted = (scores * decays[i - j]).astype(bf16)
            add_to(totals, i, nn(weighted, value[w_span]))
    return jnp.concatenate(totals, axis=0)


def local_kernel(layout, places, length_ref, parent_ref, rate_ref, query_ref, key_ref, value_ref, out_ref, masked_ref, scaled_ref, table_ref, facts_ref, distances):
    length = length_ref[lax.axis_index("seg")]
    weight_table(layout, length_ref, parent_ref, rate_ref, distances, table_ref)
    heads, size = layout.heads, layout.size
    for place in range(heads):
        facts_ref[place:place + 1, :] = jnp.full((1, size), rate_ref[layout.head(place)], f32)
    facts_ref[heads:, :] = jnp.full((1, size), length.astype(f32), f32)
    masked_ref[...] = masked_rows(query_ref[...], length)
    for place in range(heads):
        span = layout.span(place)
        scale = query_scale(layout.rows, size, rate_ref[layout.head(place)])
        scaled_ref[:, span] = (masked_ref[:, span].astype(f32) * scale).astype(bf16)
    for place in places:
        span = layout.span(place)
        rate = rate_ref[layout.head(place)]
        out_ref[:, layout.near(places, place)] = local_head(layout, rate, masked_ref[:, span], key_ref[:, span], value_ref[:, span])


def tile_pairs(count):
    return [(i, j) for j in range(count) for i in range(j, count)]


def weighted_kernel(layout, places, facts_ref, query_ref, key_ref, value_ref, out_ref, local_ref, key_end_ref, value_end_ref):
    tile = layout.tile
    length = facts_ref[layout.heads:, :]
    for place in range(layout.heads):
        span = layout.span(place)
        scale = key_scale(layout.rows, layout.size, length, facts_ref[place:place + 1, :])
        key_end_ref[:, span] = (key_ref[:, span].astype(f32) * scale).astype(bf16)
        value_end_ref[:, span] = (value_ref[:, span].astype(f32) * scale).astype(bf16)
        rate = facts_ref[place:place + 1, :1]
        query, key = query_ref[:, span], key_ref[:, span]
        decays = decay_tiles(tile, rate, layout.count, True)
        for at, (i, j) in enumerate(tile_pairs(layout.count)):
            scores = nt(key[j * tile:(j + 1) * tile], query[i * tile:(i + 1) * tile])
            out_ref[place, at] = (scores * decays[i - j]).astype(bf16)
        if place in places:
            local_ref[:, layout.near(places, place)] = local_head(layout, rate, query, key, value_ref[:, span])


def mix_kernel(layout, backward, targets, table_ref, *rest):
    chips, size, piece = layout.chips, layout.size, layout.piece
    mine, other, outs = rest[:chips], rest[chips:2 * chips], rest[len(rest) - len(targets):]
    part = min(piece, size)
    for at in range(piece // part):
        span = slice(at * part, (at + 1) * part)
        totals = [None] * len(targets)
        for offset in range(chips):
            for sibling, sources in ((0, mine), (1, other)):
                data = sources[offset][span, :]
                for index, target in enumerate(targets):
                    slot = ((backward * chips + target) * chips + offset) * 2 + sibling
                    add_to(totals, index, table_ref[slot, at:at + 1, :] * data)
        for out, total in zip(outs, totals):
            out[span, :] = total


def attend_kernel(layout, places, last, scaled_ref, upstream_ref, gain_ref, local_ref, *rest):
    pieces, rest = rest[:layout.chips], rest[layout.chips:]
    rows, size = layout.rows, layout.size
    if last is None:
        attended_ref, squares_ref, inners_ref = rest
        squares = jnp.zeros((rows, size), f32)
        inners = jnp.zeros((rows, size), f32)
    else:
        *before, attended_ref, sums_ref = rest
        squares, inners = (before[0][...], before[1][...]) if before else (jnp.zeros((rows, size), f32),) * 2
    for chosen in layout.pairs(places):
        carried = block_diagonal([layout.state(pieces, place).astype(bf16) for place in chosen])
        both = nn(side_by_side([scaled_ref[:, layout.span(place)] for place in chosen]), carried)
        for at, place in enumerate(chosen):
            span, near = layout.span(place), layout.near(places, place)
            attended = local_ref[:, near] + both[:, at * size:(at + 1) * size]
            attended_ref[:, near] = attended
            scaled = upstream_ref[:, span].astype(f32) * gain_ref[:, span]
            squares = squares + attended * attended
            inners = inners + scaled * attended
    if last is None:
        squares_ref[...] = squares
        inners_ref[...] = inners
        return
    groups = rows // size
    for at in range(groups):
        span = slice(at * size, (at + 1) * size)
        sums_ref[at:at + 1, :] = jnp.sum(squares[span].T, axis=0, keepdims=True)
        sums_ref[groups + at:groups + at + 1, :] = jnp.sum(inners[span].T, axis=0, keepdims=True)


def norm_columns(sum_refs, width, inverse_ref, factor_ref):
    total = sum_refs[0][...]
    for ref in sum_refs[1:]:
        total = total + ref[...]
    groups = total.shape[0] // 2
    size = total.shape[1]
    inverse = lax.rsqrt(total[:groups] / width + norm_eps)
    factor = inverse * inverse * inverse * total[groups:] / width
    for at in range(groups):
        span = slice(at * size, (at + 1) * size)
        inverse_ref[span, :] = column(inverse[at:at + 1])
        factor_ref[span, :] = column(factor[at:at + 1])


def pick(layout, groups, refs, place, rows=slice(None)):
    for places, ref in zip(groups, refs):
        if place in places:
            return ref[rows, layout.near(places, place)]
    raise ValueError(place)


def state_grad_kernel(layout, groups, offsets, sums, width, scaled_ref, upstream_ref, gain_ref, *rest):
    attended_refs, rest = rest[:len(groups)], rest[len(groups):]
    if sums:
        sum_refs, rest = rest[:sums], rest[sums:]
        outs, (inverse_ref, factor_ref, whole) = rest[:len(offsets)], rest[len(offsets):]
        norm_columns(sum_refs, width, inverse_ref, factor_ref)
    else:
        inverse_ref, factor_ref, *outs, whole = rest
    inverse = inverse_ref[...]
    factor = factor_ref[...]

    def left(place):
        return scaled_ref[:, layout.span(place)]

    def right(place):
        span = layout.span(place)
        scaled = upstream_ref[:, span].astype(f32) * gain_ref[:, span]
        return (inverse * scaled - factor * pick(layout, groups, attended_refs, place)).astype(bf16)

    write_states(layout, offsets, left, right, outs, whole)


def send(layout, places, place, sources, targets, sems, copies):
    for source, target in zip(sources, targets):
        near = source.at[:, layout.near(places, place)]
        copies.append(pltpu.make_async_copy(near, target.at[:, layout.span(place)], sems.at[len(copies)]))
        copies[-1].start()


def send_all(layout, kept, earlier, targets, sems, copies):
    for at, places in enumerate(kept):
        for place in places:
            send(layout, places, place, earlier[2 * at:2 * at + 2], targets, sems, copies)


def backward_kernel(layout, groups, places, kept, last, facts_ref, query_ref, key_ref, value_ref, upstream_ref, weighted_ref, gain_ref, inverse_ref, factor_ref, *rest):
    attended_refs, rest = rest[:len(groups)], rest[len(groups):]
    pieces, rest = rest[:layout.chips], rest[layout.chips:]
    earlier, rest = rest[:2 * len(kept)], rest[2 * len(kept):]
    rows, size, tile, count = layout.rows, layout.size, layout.tile, layout.count
    copies = []
    if last:
        out_any, query_grad_any, key_grad_ref, value_grad_ref, out_ref, query_grad_ref, sems = rest
        targets = (out_any, query_grad_any)
        send_all(layout, kept, earlier, targets, sems, copies)
    else:
        out_ref, query_grad_ref, key_grad_ref, value_grad_ref, token_ref = rest
        token_ref[...] = jnp.zeros_like(token_ref)
    used = row_index(rows, size).astype(f32) < facts_ref[layout.heads:, :]
    for place in places:
        span, near = layout.span(place), layout.near(places, place)
        rate = facts_ref[place:place + 1, :]
        query = query_ref[:, span]
        key = key_ref[:, span]
        value = value_ref[:, span]
        gain = gain_ref[:, span]
        inverse = inverse_ref[...]
        attended = pick(layout, groups, attended_refs, place)
        out_ref[:, near] = (attended * inverse * gain).astype(bf16)
        scaled = upstream_ref[:, span].astype(f32) * gain
        grad = (inverse * scaled - factor_ref[...] * attended).astype(bf16)
        carried = layout.state(pieces, place).astype(bf16)
        query_grad = nt(grad, carried) * query_scale(rows, size, rate)
        decays = decay_tiles(tile, rate[:, :1], count, True)
        query_totals, key_totals, value_totals = [None] * count, [None] * count, [None] * count
        for at, (i, j) in enumerate(tile_pairs(count)):
            u_span, w_span = slice(i * tile, (i + 1) * tile), slice(j * tile, (j + 1) * tile)
            score_grad = (nt(value[w_span], grad[u_span]) * decays[i - j]).astype(bf16)
            add_to(value_totals, j, nn(weighted_ref[place, at], grad[u_span]))
            add_to(key_totals, j, nn(score_grad, query[u_span]))
            add_to(query_totals, i, tn(score_grad, key[w_span]))
        key_grad_ref[:, near] = jnp.concatenate(key_totals, axis=0).astype(bf16)
        value_grad_ref[:, near] = jnp.concatenate(value_totals, axis=0).astype(bf16)
        query_grad = query_grad + jnp.concatenate(query_totals, axis=0)
        query_grad_ref[:, near] = jnp.where(used, query_grad, 0.0).astype(bf16)
        if last:
            send(layout, places, place, (out_ref, query_grad_ref), targets, sems, copies)
    for copy in copies:
        copy.wait()


def finish_kernel(layout, groups, places, filled, key_end_ref, value_end_ref, *rest):
    key_locals, value_locals, rest = rest[:len(groups)], rest[len(groups):2 * len(groups)], rest[2 * len(groups):]
    pieces, rest = rest[:layout.chips], rest[layout.chips + filled:]
    key_any, value_any, key_grad_ref, value_grad_ref, sems = rest
    copies = []
    for place in places:
        span, near = layout.span(place), layout.near(places, place)
        state_grad = layout.state(pieces, place).astype(bf16)
        key_part = nt(value_end_ref[:, span], state_grad)
        value_part = nn(key_end_ref[:, span], state_grad)
        key_grad_ref[:, near] = (pick(layout, groups, key_locals, place).astype(f32) + key_part).astype(bf16)
        value_grad_ref[:, near] = (pick(layout, groups, value_locals, place).astype(f32) + value_part).astype(bf16)
        send(layout, places, place, (key_grad_ref, value_grad_ref), (key_any, value_any), sems, copies)
    for copy in copies:
        copy.wait()


def params(limit=VMEM_LIMIT):
    return pltpu.CompilerParams(vmem_limit_bytes=limit)


def shape(dims, dtype):
    return jax.ShapeDtypeStruct(dims, dtype)


def pass_on(piece_ref, before_ref, out_ref):
    pass


def after(piece, before):
    return pl.pallas_call(
        pass_on,
        out_shape=shape(piece.shape, piece.dtype),
        in_specs=[ANY_SPEC] * 2,
        out_specs=ANY_SPEC,
        input_output_aliases={0: 0},
        compiler_params=params(),
        name="after",
    )(piece, before)


def exchange(pieces, count):
    moved = [pieces[0]]
    for slot in range(1, len(pieces)):
        pairs = [(at, at ^ (2 * (core_offset(slot, at % 2) if False else slot))) for at in range(count)]
        moved.append(lax.ppermute(pieces[slot], "seg", pairs))
    return moved


def one_by_one(pieces, before, order):
    taken = list(pieces)
    for slot in order:
        taken[slot] = before = after(pieces[slot], before)
    return taken


def swap_cores(pieces, count):
    pairs = [(at, at ^ 1) for at in range(count)]
    return [lax.ppermute(piece, "seg", pairs) for piece in pieces]


def add_kernel(left_ref, right_ref, out_ref):
    out_ref[...] = left_ref[...] + right_ref[...]


def head_sums(sums, count):
    step = count // 2
    parts = [sums]
    while step:
        if len(parts) == 2:
            parts = [
                pl.pallas_call(
                    add_kernel,
                    out_shape=shape(sums.shape, sums.dtype),
                    in_specs=[VMEM_SPEC] * 2,
                    out_specs=VMEM_SPEC,
                    compiler_params=params(),
                    name="add_sums",
                )(*parts)
            ]
        parts.append(lax.ppermute(parts[0], "head", [(at, at ^ step) for at in range(count)]))
        step //= 2
    return parts


def local(seg_count, head_count, queries, key_tokens, values, upstream, norm_gain, decay_rate, block_length, parent):
    rows, wide = queries.shape
    heads = decay_rate.shape[0]
    size = wide // heads
    width = wide * head_count
    chips = seg_count // 2
    layout = Layout(rows, wide, size, chips)
    gain = norm_gain[None, :]
    piece_shape = shape((layout.piece, size), f32)
    whole = pltpu.VMEM((wide, size), f32)
    columns = shape((rows, size), f32)
    offsets = list(range(chips))
    sends = [[slot for slot in offsets if 0 < slot < 3], [slot for slot in offsets if slot == 0 or slot >= 3]]
    groups = [group for group in (layout.places(offsets[:2]), layout.places(offsets[2:])) if group]
    whole_sends = [sends[0] + sends[1]]
    early, late = groups if len(groups) == 2 else (groups[0], [])

    def near_shape(places, dtype):
        return shape((rows, len(places) * size), dtype)

    def near_scratch(places, dtype):
        return pltpu.VMEM((rows, len(places) * size), dtype)

    def in_order(parts):
        return [dict(zip(sends[0] + sends[1], parts))[offset] for offset in offsets]

    key_near, value_near = pl.pallas_call(
        near_kernel,
        out_shape=[shape((rows, wide), bf16)] * 2,
        in_specs=[ANY_SPEC] * 3,
        out_specs=[VMEM_SPEC] * 2,
        scratch_shapes=[pltpu.SemaphoreType.DMA((2,))],
        compiler_params=params(FIRST_LIMIT),
        name="bring_near",
    )(key_tokens, values, queries)

    states = []
    for chosen in whole_sends:
        states += pl.pallas_call(
            functools.partial(state_kernel, layout, chosen),
            out_shape=[piece_shape] * len(chosen),
            in_specs=[VMEM_SPEC] * 4,
            out_specs=[VMEM_SPEC] * len(chosen),
            scratch_shapes=[whole],
            compiler_params=params(),
            name="block_state",
        )(block_length[None, :], decay_rate[None, :], key_near, value_near)

    early_local, masked, scaled, table, facts = pl.pallas_call(
        functools.partial(local_kernel, layout, early),
        out_shape=[
            near_shape(early, f32),
            shape((rows, wide), bf16),
            shape((rows, wide), bf16),
            shape((4 * chips * chips, 8, size), f32),
            shape((heads + 1, size), f32),
        ],
        in_specs=[SMEM_SPEC] * 3 + [VMEM_SPEC] * 3,
        out_specs=[VMEM_SPEC] * 5,
        scratch_shapes=[pltpu.SMEM((seg_count * (seg_count + 1),), jnp.int32)],
        compiler_params=params(),
        cost_estimate=pl.CostEstimate(flops=2 * rows * rows * wide, bytes_accessed=10 * rows * wide, transcendentals=rows * rows * heads),
        name="local_attention",
    )(block_length, parent, decay_rate, queries, key_near, value_near)

    pairs = len(tile_pairs(layout.count))
    weighted, late_local, key_end, value_end = pl.pallas_call(
        functools.partial(weighted_kernel, layout, late),
        out_shape=[shape((heads, pairs, layout.tile, layout.tile), bf16), near_shape(late or [0], f32)] + [shape((rows, wide), bf16)] * 2,
        in_specs=[VMEM_SPEC] * 4,
        out_specs=[VMEM_SPEC] * 4,
        compiler_params=params(),
        cost_estimate=pl.CostEstimate(flops=4 * rows * rows * wide, bytes_accessed=10 * rows * wide, transcendentals=rows * rows * heads),
        name="weighted_scores",
    )(facts, masked, key_near, value_near)

    def mix(pieces, backward, before):
        mine = exchange(pieces, seg_count)
        mine = mine[:1] + [after(piece, before) for piece in mine[1:]]
        other = swap_cores(mine, seg_count)
        mixed = []
        for chosen in whole_sends:
            mixed += pl.pallas_call(
                functools.partial(mix_kernel, layout, backward, chosen),
                out_shape=[piece_shape] * len(chosen),
                in_specs=[VMEM_SPEC] * (1 + 2 * chips) + [ANY_SPEC] * len(mixed[:1]),
                out_specs=[VMEM_SPEC] * len(chosen),
                compiler_params=params(),
                cost_estimate=pl.CostEstimate(flops=rows * rows * wide, bytes_accessed=10 * rows * wide, transcendentals=0),
                name="mix_backward" if backward else "mix_forward",
            )(table, *mine, *other, *mixed[:1])
        return exchange(in_order(mixed), seg_count)

    def shown(pieces, places):
        if not layout.each:
            return pieces
        return [piece if offset * layout.each in places else pieces[0] for offset, piece in enumerate(pieces)]

    carried = mix(in_order(states), 0, table)

    attended, before = [], []
    for index, (places, local_out) in enumerate(zip(groups, (early_local, late_local))):
        last = True if index == len(groups) - 1 else None
        out_shape = [near_shape(places, f32)] + ([shape((2 * rows // size, size), f32)] if last else [columns] * 2)
        part, *before = pl.pallas_call(
            functools.partial(attend_kernel, layout, places, last),
            out_shape=out_shape,
            in_specs=[VMEM_SPEC] * (4 + chips + len(before)),
            out_specs=[VMEM_SPEC] * len(out_shape),
            compiler_params=params(),
            cost_estimate=pl.CostEstimate(flops=rows * rows * wide, bytes_accessed=10 * rows * wide, transcendentals=rows * wide),
            name="attend",
        )(scaled, upstream, gain, local_out, *shown(carried, places), *before)
        attended.append(part)
    sum_parts = head_sums(before[0], head_count)

    state_grads, norms = [], []
    for chosen in whole_sends:
        first = not norms
        parts = pl.pallas_call(
            functools.partial(state_grad_kernel, layout, groups, chosen, len(sum_parts) if first else 0, width),
            out_shape=[piece_shape] * len(chosen) + ([columns] * 2 if first else []),
            in_specs=[VMEM_SPEC] * (3 + len(groups) + (len(sum_parts) if first else 2)),
            out_specs=[VMEM_SPEC] * (len(chosen) + (2 if first else 0)),
            scratch_shapes=[whole],
            compiler_params=params(),
            name="state_grad",
        )(scaled, upstream, gain, *attended, *(sum_parts if first else norms))
        state_grads += parts[:len(chosen)]
        norms = norms or parts[len(chosen):]

    def ending(places, kept, last):
        if not last:
            return [near_shape(places, bf16)] * 2, [VMEM_SPEC] * 2, []
        amount = len(places) + sum(len(group) for group in kept)
        scratch = [near_scratch(places, bf16)] * 2 + [pltpu.SemaphoreType.DMA((2 * amount,))]
        return [shape((rows, wide), bf16)] * 2, [ANY_SPEC] * 2, scratch

    def backward(places, kept, earlier, last):
        out_shape, out_specs, scratch = ending(places, kept, last)
        out_shape = out_shape + [near_shape(places, bf16)] * 2 + ([] if last else [shape((8, size), f32)])
        return pl.pallas_call(
            functools.partial(backward_kernel, layout, groups, places, kept, last),
            out_shape=out_shape,
            in_specs=[VMEM_SPEC] * (9 + len(groups) + chips + len(earlier)),
            out_specs=out_specs + [VMEM_SPEC] * (len(out_shape) - 2),
            scratch_shapes=scratch,
            compiler_params=params(),
            cost_estimate=pl.CostEstimate(
                flops=8 * rows * rows * size * len(places),
                bytes_accessed=16 * rows * size * len(places),
                transcendentals=rows * rows * len(places),
            ),
            name="local_backward",
        )(facts, masked, key_near, value_near, upstream, weighted, gain, *norms, *attended, *carried, *earlier)

    cut = heads * 4 // 8 if heads > 2 else heads // 2
    halves = [list(range(cut)), list(range(cut, heads))]
    out_part, query_part, key_first, value_first, token = backward(halves[0], [], [], False)
    state_sums = mix(in_order(state_grads), 1, token)
    attention_out, query_grad, key_last, value_last = backward(halves[1], halves[:1], [out_part, query_part], True)

    grads = []
    for places in groups:
        inputs = 6 + chips
        grads = pl.pallas_call(
            functools.partial(finish_kernel, layout, halves, places, len(grads)),
            out_shape=[shape((rows, wide), bf16)] * 2,
            in_specs=[VMEM_SPEC] * inputs + [ANY_SPEC] * len(grads),
            out_specs=[ANY_SPEC] * 2,
            scratch_shapes=[near_scratch(places, bf16)] * 2 + [pltpu.SemaphoreType.DMA((2 * len(places),))],
            input_output_aliases={inputs + at: at for at in range(len(grads))},
            compiler_params=params(),
            cost_estimate=pl.CostEstimate(flops=rows * rows * wide, bytes_accessed=10 * rows * wide, transcendentals=rows * wide),
            name="finish",
        )(key_end, value_end, key_first, key_last, value_first, value_last, *shown(state_sums, places), *grads)
    return attention_out, query_grad, *grads


def solution(mesh):
    sizes = dict(mesh.shape)
    tokens = P("seg", "head")
    return jax.shard_map(
        functools.partial(local, sizes["seg"], sizes["head"]),
        mesh=mesh,
        in_specs=(tokens, tokens, tokens, tokens, P("head"), P("head"), P(), P()),
        out_specs=(tokens, tokens, tokens, tokens),
        check_vma=False,
    )
```

```python
import functools

import jax
import jax.numpy as jnp
from jax import lax
from jax.experimental import pallas as pl
from jax.experimental.pallas import tpu as pltpu
from jax.sharding import PartitionSpec as P

norm_eps = 1e-05
f32 = jnp.float32
bf16 = jnp.bfloat16
VMEM_LIMIT = 40 * 1024 * 1024
FIRST_LIMIT = 514 * 1024 * 1024 // 10

SMEM_SPEC = pl.BlockSpec(memory_space=pltpu.SMEM)
VMEM_SPEC = pl.BlockSpec(memory_space=pltpu.VMEM)
ANY_SPEC = pl.BlockSpec(memory_space=pl.ANY)


def nn(a, b):
    return lax.dot_general(a, b, (((1,), (0,)), ((), ())), preferred_element_type=f32)


def nt(a, b):
    return lax.dot_general(a, b, (((1,), (1,)), ((), ())), preferred_element_type=f32)


def tn(a, b):
    return lax.dot_general(a, b, (((0,), (0,)), ((), ())), preferred_element_type=f32)


def side_by_side(parts):
    return jnp.concatenate(parts, axis=1)


def block_diagonal(blocks):
    zero = jnp.zeros_like(blocks[0])
    return jnp.concatenate([side_by_side([block if i == j else zero for j in range(len(blocks))]) for i, block in enumerate(blocks)], axis=0)


def row_index(rows, columns):
    return lax.broadcasted_iota(jnp.int32, (rows, columns), 0)


def key_scale(rows, size, length, rate):
    slot = row_index(rows, size).astype(f32)
    remaining = (length - 1) - slot
    return jnp.where(remaining >= 0, jnp.exp(-rate * remaining), 0.0)


def query_scale(rows, size, rate):
    return jnp.exp(-rate * (row_index(rows, size) + 1).astype(f32))


def masked_rows(array, length):
    return jnp.where(row_index(*array.shape) < length, array, jnp.zeros_like(array))


def column(row):
    count = row.shape[1]
    return jnp.broadcast_to(row, (count, count)).T


def add_to(totals, index, part):
    totals[index] = part if totals[index] is None else totals[index] + part


def core_offset(slot, core, chips):
    crossed = slot ^ ((slot & 1) << 1) if chips >= 4 else slot
    return slot + core * (crossed - slot)


class Layout:
    def __init__(self, rows, wide, size, chips):
        self.rows, self.wide, self.size, self.chips = rows, wide, size, chips
        self.heads = wide // size
        self.piece = wide // chips
        self.each = self.piece // size
        self.tile = min(256, rows)
        self.count = rows // self.tile

    def chip(self, slot, sibling=0):
        own = lax.axis_index("seg")
        return (own // 2) ^ core_offset(slot, (own % 2) ^ sibling, self.chips)

    def head(self, place):
        if not self.each:
            return place
        return self.chip(place // self.each) * self.each + place % self.each

    def span(self, place):
        if not self.each:
            return pl.ds(place * self.size, self.size)
        return pl.ds(pl.multiple_of(self.head(place) * self.size, self.size), self.size)

    def near(self, places, place):
        at = list(places).index(place)
        return slice(at * self.size, (at + 1) * self.size)

    def places(self, offsets):
        if not self.each:
            return list(range(self.heads)) if 0 in offsets else []
        return [offset * self.each + at for offset in offsets for at in range(self.each)]

    def pairs(self, places):
        return [places[at:at + 2] for at in range(0, len(places), 2)]

    def state(self, pieces, place):
        if self.each:
            at = place % self.each
            return pieces[place // self.each][at * self.size:(at + 1) * self.size, :]
        first = place * self.size // self.piece
        parts = []
        for owner in range(first, first + self.size // self.piece):
            part = pieces[0][...]
            for offset in range(1, self.chips):
                part = jnp.where(self.chip(offset) == owner, pieces[offset][...], part)
            parts.append(part)
        return jnp.concatenate(parts, axis=0)


def near_kernel(key_any, value_any, query_any, key_ref, value_ref, sems):
    moves = ((key_any, key_ref), (value_any, value_ref))
    copies = [pltpu.make_async_copy(source, target, sems.at[at]) for at, (source, target) in enumerate(moves)]
    for copy in copies:
        copy.start()
    for copy in copies:
        copy.wait()


def write_states(layout, offsets, left, right, outs, whole):
    size = layout.size
    if layout.each:
        places = layout.places(offsets)
        targets = [(outs[place // size_of], place % size_of) for place, size_of in ((at, layout.each) for at in range(len(places)))]
    else:
        places = list(range(layout.heads))
        targets = [(whole, place) for place in places]
    group = min(2, len(places))
    for first in range(0, len(places), group):
        chosen = places[first:first + group]
        both = tn(
            jnp.concatenate([left(place) for place in chosen], axis=1),
            jnp.concatenate([right(place) for place in chosen], axis=1),
        )
        for at in range(len(chosen)):
            inner = slice(at * size, (at + 1) * size)
            target, row = targets[first + at]
            target[row * size:(row + 1) * size, :] = both[inner, inner]
    if not layout.each:
        for offset, out in zip(offsets, outs):
            begin = pl.multiple_of(layout.chip(offset) * layout.piece, layout.piece)
            out[...] = whole[pl.ds(begin, layout.piece), :]


def state_kernel(layout, offsets, length_ref, rate_ref, key_ref, value_ref, *rest):
    outs, whole = rest[:len(offsets)], rest[len(offsets)]
    rows, size = layout.rows, layout.size
    lengths = length_ref[...].astype(f32)
    mine = lax.broadcasted_iota(jnp.int32, lengths.shape, 1) == lax.axis_index("seg")
    length = jnp.sum(jnp.where(mine, lengths, 0.0), axis=1, keepdims=True)
    rates = rate_ref[...]
    lane = lax.broadcasted_iota(jnp.int32, rates.shape, 1)

    def left(place):
        return key_ref[:, layout.span(place)]

    def right(place):
        rate = jnp.sum(jnp.where(lane == layout.head(place), rates, 0.0), axis=1, keepdims=True)
        return (value_ref[:, layout.span(place)].astype(f32) * key_scale(rows, size, length, rate)).astype(bf16)

    write_states(layout, offsets, left, right, outs, whole)


def decay_tiles(tile, rate, count, transposed):
    u = lax.broadcasted_iota(jnp.int32, (tile, tile), 1 if transposed else 0)
    w = lax.broadcasted_iota(jnp.int32, (tile, tile), 0 if transposed else 1)
    base = jnp.exp((w - u).astype(f32) * rate)
    tiles = [jnp.where(u >= w, base, 0.0)]
    for gap in range(1, count):
        tiles.append(base * jnp.exp(jnp.full((1, tile), -(gap * tile), f32) * rate))
    return tiles


def tree_distances(length_ref, parent_ref, table, count):
    for at in range(count):
        table[at] = jnp.int32(-1)

    def one(block, carry):
        above = parent_ref[block]
        passed = length_ref[jnp.maximum(above, 0)]
        for at in range(count):
            distance = table[(above + 1) * count + at]
            distance = jnp.where(distance >= 0, distance + passed, distance)
            table[(block + 1) * count + at] = jnp.where(above == at, 0, distance)
        return carry

    lax.fori_loop(0, count, one, 0)


def weight_table(layout, length_ref, parent_ref, rate_ref, distances, table_ref):
    own = lax.axis_index("seg")
    chip, core = own // 2, own % 2
    chips, size, piece = layout.chips, layout.size, layout.piece
    count = 2 * chips
    tree_distances(length_ref, parent_ref, distances, count)
    row = row_index(8, size)
    rates = jnp.full((8, size), rate_ref[(chip * piece) // size], f32)
    for at in range(1, piece // size):
        rates = jnp.where(row == at, rate_ref[(chip * piece) // size + at], rates)
    for backward in range(2):
        for target in range(chips):
            wanted = layout.chip(target) * 2 + core
            for offset in range(chips):
                for sibling in range(2):
                    source = layout.chip(offset, sibling) * 2 + (core ^ sibling)
                    place = (source + 1) * count + wanted if backward else (wanted + 1) * count + source
                    distance = distances[place].astype(f32)
                    linked = (distance >= 0.0).astype(f32)
                    slot = ((backward * chips + target) * chips + offset) * 2 + sibling
                    table_ref[slot] = jnp.exp(rates * -distance) * linked


def local_head(layout, rate, query, key, value):
    tile, count = layout.tile, layout.count
    decays = decay_tiles(tile, rate, count, False)
    totals = [None] * count
    for i in range(count):
        for j in range(i + 1):
            w_span = slice(j * tile, (j + 1) * tile)
            scores = nt(query[i * tile:(i + 1) * tile], key[w_span])
            weighted = (scores * decays[i - j]).astype(bf16)
            add_to(totals, i, nn(weighted, value[w_span]))
    return jnp.concatenate(totals, axis=0)


def local_kernel(layout, places, length_ref, parent_ref, rate_ref, query_ref, key_ref, value_ref, out_ref, masked_ref, scaled_ref, table_ref, facts_ref, distances):
    length = length_ref[lax.axis_index("seg")]
    weight_table(layout, length_ref, parent_ref, rate_ref, distances, table_ref)
    heads, size = layout.heads, layout.size
    for place in range(heads):
        facts_ref[place:place + 1, :] = jnp.full((1, size), rate_ref[layout.head(place)], f32)
    facts_ref[heads:, :] = jnp.full((1, size), length.astype(f32), f32)
    masked_ref[...] = masked_rows(query_ref[...], length)
    for place in range(heads):
        span = layout.span(place)
        scale = query_scale(layout.rows, size, rate_ref[layout.head(place)])
        scaled_ref[:, span] = (masked_ref[:, span].astype(f32) * scale).astype(bf16)
    for place in places:
        span = layout.span(place)
        rate = rate_ref[layout.head(place)]
        out_ref[:, layout.near(places, place)] = local_head(layout, rate, masked_ref[:, span], key_ref[:, span], value_ref[:, span])


def tile_pairs(count):
    return [(i, j) for j in range(count) for i in range(j, count)]


def weighted_kernel(layout, places, facts_ref, query_ref, key_ref, value_ref, out_ref, local_ref, key_end_ref, value_end_ref):
    tile = layout.tile
    length = facts_ref[layout.heads:, :]
    for place in range(layout.heads):
        span = layout.span(place)
        scale = key_scale(layout.rows, layout.size, length, facts_ref[place:place + 1, :])
        key_end_ref[:, span] = (key_ref[:, span].astype(f32) * scale).astype(bf16)
        value_end_ref[:, span] = (value_ref[:, span].astype(f32) * scale).astype(bf16)
        rate = facts_ref[place:place + 1, :1]
        query, key = query_ref[:, span], key_ref[:, span]
        decays = decay_tiles(tile, rate, layout.count, True)
        for at, (i, j) in enumerate(tile_pairs(layout.count)):
            scores = nt(key[j * tile:(j + 1) * tile], query[i * tile:(i + 1) * tile])
            out_ref[place, at] = (scores * decays[i - j]).astype(bf16)
        if place in places:
            local_ref[:, layout.near(places, place)] = local_head(layout, rate, query, key, value_ref[:, span])


def mix_kernel(layout, backward, targets, table_ref, *rest):
    chips, size, piece = layout.chips, layout.size, layout.piece
    mine, other, outs = rest[:chips], rest[chips:2 * chips], rest[len(rest) - len(targets):]
    part = min(piece, size)
    for at in range(piece // part):
        span = slice(at * part, (at + 1) * part)
        totals = [None] * len(targets)
        for offset in range(chips):
            for sibling, sources in ((0, mine), (1, other)):
                data = sources[offset][span, :]
                for index, target in enumerate(targets):
                    slot = ((backward * chips + target) * chips + offset) * 2 + sibling
                    add_to(totals, index, table_ref[slot, at:at + 1, :] * data)
        for out, total in zip(outs, totals):
            out[span, :] = total


def attend_kernel(layout, places, last, scaled_ref, upstream_ref, gain_ref, local_ref, *rest):
    pieces, rest = rest[:layout.chips], rest[layout.chips:]
    rows, size = layout.rows, layout.size
    if last is None:
        attended_ref, squares_ref, inners_ref = rest
        squares = jnp.zeros((rows, size), f32)
        inners = jnp.zeros((rows, size), f32)
    else:
        *before, attended_ref, sums_ref = rest
        squares, inners = (before[0][...], before[1][...]) if before else (jnp.zeros((rows, size), f32),) * 2
    for chosen in layout.pairs(places):
        carried = block_diagonal([layout.state(pieces, place).astype(bf16) for place in chosen])
        both = nn(side_by_side([scaled_ref[:, layout.span(place)] for place in chosen]), carried)
        for at, place in enumerate(chosen):
            span, near = layout.span(place), layout.near(places, place)
            attended = local_ref[:, near] + both[:, at * size:(at + 1) * size]
            attended_ref[:, near] = attended
            scaled = upstream_ref[:, span].astype(f32) * gain_ref[:, span]
            squares = squares + attended * attended
            inners = inners + scaled * attended
    if last is None:
        squares_ref[...] = squares
        inners_ref[...] = inners
        return
    groups = rows // size
    for at in range(groups):
        span = slice(at * size, (at + 1) * size)
        sums_ref[at:at + 1, :] = jnp.sum(squares[span].T, axis=0, keepdims=True)
        sums_ref[groups + at:groups + at + 1, :] = jnp.sum(inners[span].T, axis=0, keepdims=True)


def norm_columns(sum_refs, width, inverse_ref, factor_ref):
    total = sum_refs[0][...]
    for ref in sum_refs[1:]:
        total = total + ref[...]
    groups = total.shape[0] // 2
    size = total.shape[1]
    inverse = lax.rsqrt(total[:groups] / width + norm_eps)
    factor = inverse * inverse * inverse * total[groups:] / width
    for at in range(groups):
        span = slice(at * size, (at + 1) * size)
        inverse_ref[span, :] = column(inverse[at:at + 1])
        factor_ref[span, :] = column(factor[at:at + 1])


def pick(layout, groups, refs, place, rows=slice(None)):
    for places, ref in zip(groups, refs):
        if place in places:
            return ref[rows, layout.near(places, place)]
    raise ValueError(place)


def state_grad_kernel(layout, groups, offsets, sums, width, scaled_ref, upstream_ref, gain_ref, *rest):
    attended_refs, rest = rest[:len(groups)], rest[len(groups):]
    if sums:
        sum_refs, rest = rest[:sums], rest[sums:]
        outs, (inverse_ref, factor_ref, whole) = rest[:len(offsets)], rest[len(offsets):]
        norm_columns(sum_refs, width, inverse_ref, factor_ref)
    else:
        inverse_ref, factor_ref, *outs, whole = rest
    inverse = inverse_ref[...]
    factor = factor_ref[...]

    def left(place):
        return scaled_ref[:, layout.span(place)]

    def right(place):
        span = layout.span(place)
        scaled = upstream_ref[:, span].astype(f32) * gain_ref[:, span]
        return (inverse * scaled - factor * pick(layout, groups, attended_refs, place)).astype(bf16)

    write_states(layout, offsets, left, right, outs, whole)


def send(layout, places, place, sources, targets, sems, copies):
    for source, target in zip(sources, targets):
        near = source.at[:, layout.near(places, place)]
        copies.append(pltpu.make_async_copy(near, target.at[:, layout.span(place)], sems.at[len(copies)]))
        copies[-1].start()


def send_all(layout, kept, earlier, targets, sems, copies):
    for at, places in enumerate(kept):
        for place in places:
            send(layout, places, place, earlier[2 * at:2 * at + 2], targets, sems, copies)


def backward_kernel(layout, groups, places, kept, last, facts_ref, query_ref, key_ref, value_ref, upstream_ref, weighted_ref, gain_ref, inverse_ref, factor_ref, *rest):
    attended_refs, rest = rest[:len(groups)], rest[len(groups):]
    pieces, rest = rest[:layout.chips], rest[layout.chips:]
    earlier, rest = rest[:2 * len(kept)], rest[2 * len(kept):]
    rows, size, tile, count = layout.rows, layout.size, layout.tile, layout.count
    copies = []
    if last:
        out_any, query_grad_any, key_grad_ref, value_grad_ref, out_ref, query_grad_ref, sems = rest
        targets = (out_any, query_grad_any)
        send_all(layout, kept, earlier, targets, sems, copies)
    else:
        out_ref, query_grad_ref, key_grad_ref, value_grad_ref, token_ref = rest
        token_ref[...] = jnp.zeros_like(token_ref)
    used = row_index(rows, size).astype(f32) < facts_ref[layout.heads:, :]
    for place in places:
        span, near = layout.span(place), layout.near(places, place)
        rate = facts_ref[place:place + 1, :]
        query = query_ref[:, span]
        key = key_ref[:, span]
        value = value_ref[:, span]
        gain = gain_ref[:, span]
        inverse = inverse_ref[...]
        attended = pick(layout, groups, attended_refs, place)
        out_ref[:, near] = (attended * inverse * gain).astype(bf16)
        scaled = upstream_ref[:, span].astype(f32) * gain
        grad = (inverse * scaled - factor_ref[...] * attended).astype(bf16)
        carried = layout.state(pieces, place).astype(bf16)
        query_grad = nt(grad, carried) * query_scale(rows, size, rate)
        decays = decay_tiles(tile, rate[:, :1], count, True)
        query_totals, key_totals, value_totals = [None] * count, [None] * count, [None] * count
        for at, (i, j) in enumerate(tile_pairs(count)):
            u_span, w_span = slice(i * tile, (i + 1) * tile), slice(j * tile, (j + 1) * tile)
            score_grad = (nt(value[w_span], grad[u_span]) * decays[i - j]).astype(bf16)
            add_to(value_totals, j, nn(weighted_ref[place, at], grad[u_span]))
            add_to(key_totals, j, nn(score_grad, query[u_span]))
            add_to(query_totals, i, tn(score_grad, key[w_span]))
        key_grad_ref[:, near] = jnp.concatenate(key_totals, axis=0).astype(bf16)
        value_grad_ref[:, near] = jnp.concatenate(value_totals, axis=0).astype(bf16)
        query_grad = query_grad + jnp.concatenate(query_totals, axis=0)
        query_grad_ref[:, near] = jnp.where(used, query_grad, 0.0).astype(bf16)
        if last:
            send(layout, places, place, (out_ref, query_grad_ref), targets, sems, copies)
    for copy in copies:
        copy.wait()


def finish_kernel(layout, groups, places, filled, key_end_ref, value_end_ref, *rest):
    key_locals, value_locals, rest = rest[:len(groups)], rest[len(groups):2 * len(groups)], rest[2 * len(groups):]
    pieces, rest = rest[:layout.chips], rest[layout.chips + filled:]
    key_any, value_any, key_grad_ref, value_grad_ref, sems = rest
    copies = []
    for place in places:
        span, near = layout.span(place), layout.near(places, place)
        state_grad = layout.state(pieces, place).astype(bf16)
        key_part = nt(value_end_ref[:, span], state_grad)
        value_part = nn(key_end_ref[:, span], state_grad)
        key_grad_ref[:, near] = (pick(layout, groups, key_locals, place).astype(f32) + key_part).astype(bf16)
        value_grad_ref[:, near] = (pick(layout, groups, value_locals, place).astype(f32) + value_part).astype(bf16)
        send(layout, places, place, (key_grad_ref, value_grad_ref), (key_any, value_any), sems, copies)
    for copy in copies:
        copy.wait()


def params(limit=VMEM_LIMIT):
    return pltpu.CompilerParams(vmem_limit_bytes=limit)


def shape(dims, dtype):
    return jax.ShapeDtypeStruct(dims, dtype)


def pass_on(piece_ref, before_ref, out_ref):
    pass


def after(piece, before):
    return pl.pallas_call(
        pass_on,
        out_shape=shape(piece.shape, piece.dtype),
        in_specs=[ANY_SPEC] * 2,
        out_specs=ANY_SPEC,
        input_output_aliases={0: 0},
        compiler_params=params(),
        name="after",
    )(piece, before)


def exchange(pieces, count):
    moved = [pieces[0]]
    for slot in range(1, len(pieces)):
        pairs = [(at, at ^ (2 * core_offset(slot, at % 2, len(pieces)))) for at in range(count)]
        moved.append(lax.ppermute(pieces[slot], "seg", pairs))
    return moved


def one_by_one(pieces, before, order):
    taken = list(pieces)
    for slot in order:
        taken[slot] = before = after(pieces[slot], before)
    return taken


def swap_cores(pieces, count):
    pairs = [(at, at ^ 1) for at in range(count)]
    return [lax.ppermute(piece, "seg", pairs) for piece in pieces]


def add_kernel(left_ref, right_ref, out_ref):
    out_ref[...] = left_ref[...] + right_ref[...]


def head_sums(sums, count):
    step = count // 2
    parts = [sums]
    while step:
        if len(parts) == 2:
            parts = [
                pl.pallas_call(
                    add_kernel,
                    out_shape=shape(sums.shape, sums.dtype),
                    in_specs=[VMEM_SPEC] * 2,
                    out_specs=VMEM_SPEC,
                    compiler_params=params(),
                    name="add_sums",
                )(*parts)
            ]
        parts.append(lax.ppermute(parts[0], "head", [(at, at ^ step) for at in range(count)]))
        step //= 2
    return parts


def local(seg_count, head_count, queries, key_tokens, values, upstream, norm_gain, decay_rate, block_length, parent):
    rows, wide = queries.shape
    heads = decay_rate.shape[0]
    size = wide // heads
    width = wide * head_count
    chips = seg_count // 2
    layout = Layout(rows, wide, size, chips)
    gain = norm_gain[None, :]
    piece_shape = shape((layout.piece, size), f32)
    whole = pltpu.VMEM((wide, size), f32)
    columns = shape((rows, size), f32)
    offsets = list(range(chips))
    order = [slot for slot in offsets if 0 < slot < 3] + [slot for slot in offsets if slot == 0 or slot >= 3]
    groups = [group for group in (layout.places(offsets[:2]), layout.places(offsets[2:])) if group]
    early, late = groups if len(groups) == 2 else (groups[0], [])

    def in_order(parts):
        return [dict(zip(order, parts))[slot] for slot in offsets]

    def near_shape(places, dtype):
        return shape((rows, len(places) * size), dtype)

    def near_scratch(places, dtype):
        return pltpu.VMEM((rows, len(places) * size), dtype)

    key_near, value_near = pl.pallas_call(
        near_kernel,
        out_shape=[shape((rows, wide), bf16)] * 2,
        in_specs=[ANY_SPEC] * 3,
        out_specs=[VMEM_SPEC] * 2,
        scratch_shapes=[pltpu.SemaphoreType.DMA((2,))],
        compiler_params=params(FIRST_LIMIT),
        name="bring_near",
    )(key_tokens, values, queries)

    states = []
    for chosen in [order]:
        states += pl.pallas_call(
            functools.partial(state_kernel, layout, chosen),
            out_shape=[piece_shape] * len(chosen),
            in_specs=[VMEM_SPEC] * 4,
            out_specs=[VMEM_SPEC] * len(chosen),
            scratch_shapes=[whole],
            compiler_params=params(),
            name="block_state",
        )(block_length[None, :], decay_rate[None, :], key_near, value_near)

    early_local, masked, scaled, table, facts = pl.pallas_call(
        functools.partial(local_kernel, layout, early),
        out_shape=[
            near_shape(early, f32),
            shape((rows, wide), bf16),
            shape((rows, wide), bf16),
            shape((4 * chips * chips, 8, size), f32),
            shape((heads + 1, size), f32),
        ],
        in_specs=[SMEM_SPEC] * 3 + [VMEM_SPEC] * 3,
        out_specs=[VMEM_SPEC] * 5,
        scratch_shapes=[pltpu.SMEM((seg_count * (seg_count + 1),), jnp.int32)],
        compiler_params=params(),
        cost_estimate=pl.CostEstimate(flops=2 * rows * rows * wide, bytes_accessed=10 * rows * wide, transcendentals=rows * rows * heads),
        name="local_attention",
    )(block_length, parent, decay_rate, queries, key_near, value_near)

    pairs = len(tile_pairs(layout.count))
    weighted, late_local, key_end, value_end = pl.pallas_call(
        functools.partial(weighted_kernel, layout, late),
        out_shape=[shape((heads, pairs, layout.tile, layout.tile), bf16), near_shape(late or [0], f32)] + [shape((rows, wide), bf16)] * 2,
        in_specs=[VMEM_SPEC] * 4,
        out_specs=[VMEM_SPEC] * 4,
        compiler_params=params(),
        cost_estimate=pl.CostEstimate(flops=4 * rows * rows * wide, bytes_accessed=10 * rows * wide, transcendentals=rows * rows * heads),
        name="weighted_scores",
    )(facts, masked, key_near, value_near)

    def mix(pieces, backward, before):
        mine = exchange(pieces, seg_count)
        mine = mine[:1] + [after(piece, before) for piece in mine[1:]]
        other = swap_cores(mine, seg_count)
        mixed = []
        for chosen in [order]:
            mixed += pl.pallas_call(
                functools.partial(mix_kernel, layout, backward, chosen),
                out_shape=[piece_shape] * len(chosen),
                in_specs=[VMEM_SPEC] * (1 + 2 * chips) + [ANY_SPEC] * len(mixed[:1]),
                out_specs=[VMEM_SPEC] * len(chosen),
                compiler_params=params(),
                cost_estimate=pl.CostEstimate(flops=rows * rows * wide, bytes_accessed=10 * rows * wide, transcendentals=0),
                name="mix_backward" if backward else "mix_forward",
            )(table, *mine, *other, *mixed[:1])
        return exchange(in_order(mixed), seg_count)

    def shown(pieces, places):
        if not layout.each:
            return pieces
        return [piece if offset * layout.each in places else pieces[0] for offset, piece in enumerate(pieces)]

    carried = mix(in_order(states), 0, table)

    attended, before = [], []
    for index, (places, local_out) in enumerate(zip(groups, (early_local, late_local))):
        last = True if index == len(groups) - 1 else None
        out_shape = [near_shape(places, f32)] + ([shape((2 * rows // size, size), f32)] if last else [columns] * 2)
        part, *before = pl.pallas_call(
            functools.partial(attend_kernel, layout, places, last),
            out_shape=out_shape,
            in_specs=[VMEM_SPEC] * (4 + chips + len(before)),
            out_specs=[VMEM_SPEC] * len(out_shape),
            compiler_params=params(),
            cost_estimate=pl.CostEstimate(flops=rows * rows * wide, bytes_accessed=10 * rows * wide, transcendentals=rows * wide),
            name="attend",
        )(scaled, upstream, gain, local_out, *shown(carried, places), *before)
        attended.append(part)
    sum_parts = head_sums(before[0], head_count)

    state_grads, norms = [], []
    for chosen in [order]:
        first = not norms
        parts = pl.pallas_call(
            functools.partial(state_grad_kernel, layout, groups, chosen, len(sum_parts) if first else 0, width),
            out_shape=[piece_shape] * len(chosen) + ([columns] * 2 if first else []),
            in_specs=[VMEM_SPEC] * (3 + len(groups) + (len(sum_parts) if first else 2)),
            out_specs=[VMEM_SPEC] * (len(chosen) + (2 if first else 0)),
            scratch_shapes=[whole],
            compiler_params=params(),
            name="state_grad",
        )(scaled, upstream, gain, *attended, *(sum_parts if first else norms))
        state_grads += parts[:len(chosen)]
        norms = norms or parts[len(chosen):]

    def ending(places, kept, last):
        if not last:
            return [near_shape(places, bf16)] * 2, [VMEM_SPEC] * 2, []
        amount = len(places) + sum(len(group) for group in kept)
        scratch = [near_scratch(places, bf16)] * 2 + [pltpu.SemaphoreType.DMA((2 * amount,))]
        return [shape((rows, wide), bf16)] * 2, [ANY_SPEC] * 2, scratch

    def backward(places, kept, earlier, last):
        out_shape, out_specs, scratch = ending(places, kept, last)
        out_shape = out_shape + [near_shape(places, bf16)] * 2 + ([] if last else [shape((8, size), f32)])
        return pl.pallas_call(
            functools.partial(backward_kernel, layout, groups, places, kept, last),
            out_shape=out_shape,
            in_specs=[VMEM_SPEC] * (9 + len(groups) + chips + len(earlier)),
            out_specs=out_specs + [VMEM_SPEC] * (len(out_shape) - 2),
            scratch_shapes=scratch,
            compiler_params=params(),
            cost_estimate=pl.CostEstimate(
                flops=8 * rows * rows * size * len(places),
                bytes_accessed=16 * rows * size * len(places),
                transcendentals=rows * rows * len(places),
            ),
            name="local_backward",
        )(facts, masked, key_near, value_near, upstream, weighted, gain, *norms, *attended, *carried, *earlier)

    cut = heads * 4 // 8 if heads > 2 else heads // 2
    halves = [list(range(cut)), list(range(cut, heads))]
    out_part, query_part, key_first, value_first, token = backward(halves[0], [], [], False)
    state_sums = mix(in_order(state_grads), 1, token)
    attention_out, query_grad, key_last, value_last = backward(halves[1], halves[:1], [out_part, query_part], True)

    grads = []
    for places in groups:
        inputs = 6 + chips
        grads = pl.pallas_call(
            functools.partial(finish_kernel, layout, halves, places, len(grads)),
            out_shape=[shape((rows, wide), bf16)] * 2,
            in_specs=[VMEM_SPEC] * inputs + [ANY_SPEC] * len(grads),
            out_specs=[ANY_SPEC] * 2,
            scratch_shapes=[near_scratch(places, bf16)] * 2 + [pltpu.SemaphoreType.DMA((2 * len(places),))],
            input_output_aliases={inputs + at: at for at in range(len(grads))},
            compiler_params=params(),
            cost_estimate=pl.CostEstimate(flops=rows * rows * wide, bytes_accessed=10 * rows * wide, transcendentals=rows * wide),
            name="finish",
        )(key_end, value_end, key_first, key_last, value_first, value_last, *shown(state_sums, places), *grads)
    return attention_out, query_grad, *grads


def solution(mesh):
    sizes = dict(mesh.shape)
    tokens = P("seg", "head")
    return jax.shard_map(
        functools.partial(local, sizes["seg"], sizes["head"]),
        mesh=mesh,
        in_specs=(tokens, tokens, tokens, tokens, P("head"), P("head"), P(), P()),
        out_specs=(tokens, tokens, tokens, tokens),
        check_vma=False,
    )
```
